32 devices in a mesh: dp: 4 (over y, x), seq: 8 (over z, core).
Axes of the slice: x: 2, y: 2, z: 4, core: 2. Of those that a mesh axis runs over, the one named last changes fastest.
Arguments:
- tokens: bfloat16 [8, 1024, 1024], P('dp', 'seq'), may hold values from -7 to 7
- cotangent: bfloat16 [8, 1024, 1024], P('dp', 'seq'), may hold values from -6 to 6
- starts: int32 [8, 4], P('dp'), may hold values from 0 to 768, as said below
- mixer_gain: bfloat16 [1, 1024], P(None, ('dp', 'seq')), may hold values from 0.5 to 1.5
- mix_weight: bfloat16 [1, 1024, 4096], P(None, ('dp', 'seq')), may hold values from -0.1875 to 0.1875
- conv_weight: bfloat16 [1, 4, 3072], P(None, None, ('dp', 'seq')), may hold values from -3 to 3
- beta_weight: bfloat16 [1, 1024, 8], P(None, ('dp', 'seq')), may hold values from -0.5 to 0.5
- head_gain: bfloat16 [1, 128], replicated, may hold values from 0.5 to 1.5
- out_weight: bfloat16 [1, 1024, 1024], P(None, ('dp', 'seq')), may hold values from -0.1875 to 0.1875
- mlp_gain: bfloat16 [1, 1024], P(None, ('dp', 'seq')), may hold values from 0.5 to 1.5
- upgate_weight: bfloat16 [1, 1024, 5632], P(None, ('dp', 'seq')), may hold values from -0.1875 to 0.1875
- down_weight: bfloat16 [1, 2816, 1024], P(None, ('dp', 'seq')), may hold values from -0.109375 to 0.109375
Outputs:
- output: bfloat16 [8, 1024, 1024], P('dp', 'seq')
- input_grad: float32 [8, 1024, 1024], P('dp', 'seq')
- mixer_gain_grad: float32 [1, 1024], P(None, ('dp', 'seq'))
- mix_weight_grad: float32 [1, 1024, 4096], P(None, ('dp', 'seq'))
- conv_weight_grad: float32 [1, 4, 3072], P(None, None, ('dp', 'seq'))
- beta_weight_grad: float32 [1, 1024, 8], P(None, ('dp', 'seq'))
- head_gain_grad: float32 [1, 128], replicated
- out_weight_grad: float32 [1, 1024, 1024], P(None, ('dp', 'seq'))
- mlp_gain_grad: float32 [1, 1024], P(None, ('dp', 'seq'))
- upgate_weight_grad: float32 [1, 1024, 5632], P(None, ('dp', 'seq'))
- down_weight_grad: float32 [1, 2816, 1024], P(None, ('dp', 'seq'))
The draws below stay inside these ranges and needn't reach their ends.
Inputs may be any that keep to these rules, and one draw needn't show every extreme that they name: `starts`: entries are multiples of 64, and each row's first entry is 0. Rows come in groups of 2 consecutive rows; in two groups one row packs 4 sequences whose increasing start positions are its entries, the last at 768; every other row holds one sequence and has all entries 0.
All inputs are finite; a program needn't handle non-finite values.
Results may differ from the reference program's by a relative error of at most 0.015.
Values may be sent and summed in bfloat16 or wider, within the bound.
A program may use at most 256 MiB of HBM per device.

```python
import jax
import jax.numpy as jnp
from jax import lax

MODEL_WIDTH = 1024
HEADS = 8
HEAD_SIZE = 128
FF = 2816
KW = 4
BLOCK_TOKENS = 64
LAYERS = 1
ROWS_DP = 2
ROW_LENGTH = 1024
ROW_COUNT = 8


offset_scale = 1.0


def draw_starts(key, part):
    key = jax.random.fold_in(key, 11)
    group_key, slot_key, shift_key = jax.random.split(key, 3)
    groups = jax.random.permutation(group_key, ROW_COUNT // ROWS_DP)[:2]
    slots = jax.random.randint(slot_key, (2,), 0, ROWS_DP)
    packed_rows = groups * ROWS_DP + slots
    convolution_reach = ROW_LENGTH // (16 * BLOCK_TOKENS)
    jitter = jax.random.randint(shift_key, (ROW_COUNT, 2), -convolution_reach, convolution_reach + 1)
    quarter_width = ROW_LENGTH // 4
    first = quarter_width + jitter[:, 0] * BLOCK_TOKENS
    second = 2 * quarter_width + jitter[:, 1] * BLOCK_TOKENS
    third = jnp.full((ROW_COUNT,), 3 * quarter_width, jnp.int32)
    packed = jnp.stack([jnp.zeros((ROW_COUNT,), jnp.int32), first, second, third], axis=1)
    chosen = jnp.any(jnp.arange(ROW_COUNT)[:, None] == packed_rows[None, :], axis=1)
    return jnp.where(chosen[:, None], packed, 0).astype(jnp.int32)


def shared_direction(key):
    return jnp.clip(jax.random.normal(jax.random.fold_in(key, 101), (MODEL_WIDTH,), jnp.float32), -3.0, 3.0)


def draw_tokens(key, part):
    direction = shared_direction(key)
    key = jax.random.fold_in(key, 12)
    noise_portion = jnp.clip(jax.random.normal(key, (ROW_COUNT, ROW_LENGTH, MODEL_WIDTH), jnp.float32), -4.0, 4.0)
    return (noise_portion + direction[None, None, :]).astype(jnp.bfloat16)


def draw_beta_weight(key, part):
    direction = shared_direction(key)
    key = jax.random.fold_in(key, 13)
    noise_key, order_key, spread_key = jax.random.split(key, 3)
    noise_portion = jnp.clip(jax.random.normal(noise_key, (LAYERS, MODEL_WIDTH, HEADS), jnp.float32), -4.0, 4.0) * MODEL_WIDTH ** (-0.5)
    fast_count = HEADS // 2
    head_order = jnp.stack([jax.random.permutation(jax.random.fold_in(order_key, layer_index), HEADS) for layer_index in range(LAYERS)])
    fast_heads = head_order < fast_count
    spread_factor = jax.random.uniform(spread_key, (LAYERS, HEADS), jnp.float32)
    slower_rate = jnp.minimum(0.3, HEAD_SIZE / ROW_LENGTH * (0.5 + spread_factor))
    fast_rate = 0.3 + 0.4 * spread_factor
    rate_value = jnp.where(fast_heads, fast_rate, slower_rate)
    centre = jnp.log(rate_value / (1.0 - rate_value))
    layer_depth = jnp.arange(LAYERS, dtype=jnp.float32)
    lift_factor = jnp.sqrt(1.0 + offset_scale ** 2 + 0.7 * layer_depth)
    offsets = centre * lift_factor[:, None]
    weight = noise_portion + offsets[:, None, :] * direction[None, :, None] / MODEL_WIDTH
    return weight.astype(jnp.bfloat16)


def steps_of(own_key, dims, cuts, least, high):
    factor_of, own = 1.0, jax.random.fold_in(own_key, 6)
    for position, shards_of in cuts:
        draws = jnp.exp(jax.random.uniform(jax.random.fold_in(own, position), (shards_of,), jnp.float32, least / len(cuts), high / len(cuts)))
        factor_of = factor_of * jnp.repeat(draws, dims[position] // shards_of).reshape([-1 if axis == position else 1 for axis in range(len(dims))])
    return factor_of


def normal_values(own_key, dims, deviation, reach, pieces=(), kind=jnp.bfloat16):
    drawn = jax.random.normal(own_key, dims, jnp.float32) * deviation
    if len(pieces) > 0:
        drawn = steps_of(own_key, dims, pieces, -0.22, 0.18) * drawn
    return jnp.clip(drawn, min=-reach, max=reach).astype(kind)


def setup_inputs(seed: int = 0) -> dict:
    streams_of = jax.random.split(jax.random.key(seed), 13)
    tokens = draw_tokens(jax.random.fold_in(streams_of[12], 71), 0)
    cotangent = normal_values(streams_of[1], (ROW_COUNT, ROW_LENGTH, MODEL_WIDTH), 1.0, 6.0, ((0, 4), (1, 8)))
    starts = draw_starts(jax.random.fold_in(streams_of[12], 71), 0)
    mixer_gain = jnp.clip(1.0 + 0.1 * jax.random.normal(streams_of[3], (LAYERS, MODEL_WIDTH), jnp.float32), 0.5, 1.5).astype(jnp.bfloat16)
    mix_weight = normal_values(streams_of[4], (LAYERS, MODEL_WIDTH, 4 * MODEL_WIDTH), MODEL_WIDTH ** -0.5, 0.1875, ((1, 32),))
    conv_weight = normal_values(streams_of[5], (LAYERS, KW, 3 * MODEL_WIDTH), 0.5, 3.0, ((2, 32),))
    beta_weight = draw_beta_weight(jax.random.fold_in(streams_of[12], 71), 0)
    head_gain = jnp.clip(1.0 + 0.1 * jax.random.normal(streams_of[7], (LAYERS, HEAD_SIZE), jnp.float32), 0.5, 1.5).astype(jnp.bfloat16)
    out_weight = normal_values(streams_of[8], (LAYERS, MODEL_WIDTH, MODEL_WIDTH), MODEL_WIDTH ** -0.5, 0.1875, ((1, 32),))
    mlp_gain = jnp.clip(1.0 + 0.1 * jax.random.normal(streams_of[9], (LAYERS, MODEL_WIDTH), jnp.float32), 0.5, 1.5).astype(jnp.bfloat16)
    upgate_weight = normal_values(streams_of[10], (LAYERS, MODEL_WIDTH, 2 * FF), MODEL_WIDTH ** -0.5, 0.1875, ((1, 32),))
    down_weight = normal_values(streams_of[11], (LAYERS, FF, MODEL_WIDTH), FF ** -0.5, 0.109375, ((1, 32),))
    return {"tokens": tokens, "cotangent": cotangent, "starts": starts, "mixer_gain": mixer_gain, "mix_weight": mix_weight, "conv_weight": conv_weight, "beta_weight": beta_weight, "head_gain": head_gain, "out_weight": out_weight, "mlp_gain": mlp_gain, "upgate_weight": upgate_weight, "down_weight": down_weight}


small_block = 1e-06
small_head = 1e-05
exact = lax.Precision.HIGHEST

@jax.custom_vjp
def low(v):
    return lax.optimization_barrier(v.astype(jnp.bfloat16)).astype(jnp.float32)

@jax.custom_vjp
def low_back(v):
    return v

def low_keep(v):
    return (low(v), None)

def low_pass(kept, grad):
    return (grad,)

def back_keep(v):
    return (v, None)

def back_low(kept, grad):
    return (low(grad),)
low.defvjp(low_keep, low_pass)
low_back.defvjp(back_keep, back_low)

def matmul(left, right):
    return jnp.einsum('...k,kn->...n', left, right, precision=exact)

def segment_of(starts, token_places):
    live = starts > 0
    hits = live[:, None, :] & (starts[:, None, :] <= token_places[None, :, None])
    return lax.optimization_barrier(jnp.sum(hits.astype(jnp.int32), axis=-1))

def make_taps(starts, token_places):
    current = segment_of(starts, token_places)
    listed = []
    for shift_by in range(KW):
        source = token_places - shift_by
        valid = (source[None, :] >= 0) & (segment_of(starts, source) == current)
        listed.append(valid.astype(jnp.float32))
    return jnp.stack(listed)

def build_kept_masks(starts, begins):
    hit = jnp.any((starts[:, None, :] == begins[None, :, None]) & (starts[:, None, :] > 0), axis=-1)
    return 1.0 - hit.astype(jnp.float32)

def convolve(padded, weight, taps, length):
    total = jnp.zeros((padded.shape[0], length, padded.shape[2]), jnp.float32)
    for shift_by in range(KW):
        begin = KW - 1 - shift_by
        total = total + weight[shift_by] * padded[:, begin:begin + length] * taps[shift_by][..., None]
    return total

def head_inputs(active, betas, rows, count):

    def arrange(part):
        return part.reshape(rows, count, BLOCK_TOKENS, HEADS, HEAD_SIZE).transpose(1, 0, 3, 2, 4)

    def unit(part):
        split = part.reshape(part.shape[0], part.shape[1], HEADS, HEAD_SIZE)
        scaled = split * lax.rsqrt(lax.optimization_barrier(jnp.sum(split * split, axis=-1, keepdims=True)) + 1e-06)
        return scaled.reshape(part.shape)
    queries = arrange(unit(active[..., :MODEL_WIDTH]) * HEAD_SIZE ** (-0.5))
    keys_in = arrange(unit(active[..., MODEL_WIDTH:2 * MODEL_WIDTH]))
    values = arrange(active[..., 2 * MODEL_WIDTH:])
    betas_h = betas.reshape(rows, count, BLOCK_TOKENS, HEADS).transpose(1, 0, 3, 2)
    return (queries, keys_in, values, betas_h)

def block_parts(queries, keys_in, values, betas_h):
    size = keys_in.shape[-2]
    lower = jnp.tril(jnp.ones((size, size), jnp.float32), -1)
    within = jnp.tril(jnp.ones((size, size), jnp.float32))
    weighted = betas_h[..., None]
    gram = jnp.einsum('...ik,...jk->...ij', keys_in, keys_in, precision=exact)
    system = jnp.eye(size, dtype=jnp.float32) + lower * weighted * gram
    solved_w = jax.scipy.linalg.solve_triangular(system, weighted * keys_in, lower=True, unit_diagonal=True)
    solved_u = jax.scipy.linalg.solve_triangular(system, weighted * values, lower=True, unit_diagonal=True)
    attend = within * jnp.einsum('...ik,...jk->...ij', queries, keys_in, precision=exact)
    return (solved_w, solved_u, attend)

def block_step(state, inputs):
    queries, keys_in, solved_w, solved_u, attend, keep = inputs
    state = keep[:, None, None, None] * state
    fresh = solved_u - jnp.einsum('rhck,rhkv->rhcv', solved_w, state, precision=exact)
    output = jnp.einsum('rhck,rhkv->rhcv', queries, state, precision=exact)
    output = output + jnp.einsum('rhij,rhjv->rhiv', attend, fresh, precision=exact)
    state = state + jnp.einsum('rhck,rhcv->rhkv', keys_in, fresh, precision=exact)
    return (state, output)

def whole_step(state, inputs):
    queries, keys_in, values, betas_h, keep = inputs
    solved_w, solved_u, attend = block_parts(queries, keys_in, values, betas_h)
    return block_step(state, (queries, keys_in, solved_w, solved_u, attend, keep))

def delta_rows(active, betas, kept_masks):
    rows, length = (active.shape[0], active.shape[1])
    count = length // BLOCK_TOKENS
    queries, keys_in, values, betas_h = head_inputs(active, betas, rows, count)
    initial = jnp.zeros((rows, HEADS, HEAD_SIZE, HEAD_SIZE), jnp.float32)
    final, outputs = lax.scan(jax.checkpoint(whole_step), initial, (queries, keys_in, values, betas_h, kept_masks.T))
    return outputs.transpose(1, 0, 3, 2, 4).reshape(rows, length, MODEL_WIDTH)

def rms(values, gain):
    return values * lax.rsqrt(lax.optimization_barrier(jnp.mean(values * values, axis=-1, keepdims=True)) + small_block) * gain

def layer(hidden, params, taps, kept_masks):
    mixer_g, mix_w, conv_w, beta_w, head_g, out_w, mlp_g, upgate_w, down_w = params
    rows, length = (hidden.shape[0], hidden.shape[1])
    normed = low(rms(hidden, mixer_g))
    project = low_back(matmul(normed, mix_w))
    betas = jax.nn.sigmoid(low_back(matmul(normed, beta_w)))
    before = project[..., :3 * MODEL_WIDTH]
    gates = project[..., 3 * MODEL_WIDTH:]
    padded = jnp.pad(before, ((0, 0), (KW - 1, 0), (0, 0)))
    active = jax.nn.silu(convolve(padded, conv_w, taps, length))
    outputs = delta_rows(active, betas, kept_masks)
    heads = outputs.reshape(rows, length, HEADS, HEAD_SIZE)
    gaussian_sample = heads * lax.rsqrt(lax.optimization_barrier(jnp.mean(heads * heads, axis=-1, keepdims=True)) + small_head) * head_g
    gated = low(gaussian_sample.reshape(rows, length, MODEL_WIDTH) * jax.nn.silu(gates))
    hidden = hidden + low_back(matmul(gated, out_w))
    normed_mid = low(rms(hidden, mlp_g))
    upgate = low_back(matmul(normed_mid, upgate_w))
    acted = low(jax.nn.silu(upgate[..., :FF]) * upgate[..., FF:])
    return hidden + low_back(matmul(acted, down_w))

def reference(tokens, cotangent, starts, mixer_gain, mix_weight, conv_weight, beta_weight, head_gain, out_weight, mlp_gain, upgate_weight, down_weight):
    token_places = jnp.arange(ROW_LENGTH, dtype=jnp.int32)
    taps = make_taps(starts, token_places)
    kept_masks = build_kept_masks(starts, jnp.arange(ROW_LENGTH // BLOCK_TOKENS, dtype=jnp.int32) * BLOCK_TOKENS)
    weights = tuple((weight.astype(jnp.float32) for weight in (mixer_gain, mix_weight, conv_weight, beta_weight, head_gain, out_weight, mlp_gain, upgate_weight, down_weight)))

    def model(hidden, params):
        for layer_index in range(LAYERS):
            hidden = layer(hidden, tuple((param[layer_index] for param in params)), taps, kept_masks)
        return hidden
    result, pullback = jax.vjp(model, tokens.astype(jnp.float32), weights)
    grad_tokens, grads = pullback(cotangent.astype(jnp.float32))
    return (result.astype(jnp.bfloat16), grad_tokens, grads[0], grads[1], grads[2], grads[3], grads[4], grads[5], grads[6], grads[7], grads[8])
```

```python
import functools

import jax
import jax.numpy as jnp
from jax import lax
from jax.experimental import pallas as pl
from jax.experimental.pallas import tpu as pltpu
from jax.sharding import PartitionSpec as P

MODEL_WIDTH = 1024
HEADS = 8
HEAD_SIZE = 128
FF = 2816
KW = 4
PACKED = 4

MESH = pl.DeviceIdType.MESH
F32 = jnp.float32
BF16 = jnp.bfloat16
TOKENS = 128
ROWS = 2
ALL = ROWS * TOKENS
HALO = 8
NEAR_ZERO = 1e-06
HEAD_ZERO = 1e-05
MIX = 4 * MODEL_WIDTH
QKV = 3 * MODEL_WIDTH
SMALL = 256
BETA_AT = 2
CONV_AT = 10
AT_SMALL = MIX
AT_OUT = AT_SMALL + SMALL
AT_UP = AT_OUT + MODEL_WIDTH
AT_DOWN = AT_UP + 2 * FF
PACK = AT_DOWN + FF
CHUNK = PACK // 12


def nn(a, b):
    return lax.dot_general(a, b, (((1,), (0,)), ((), ())), preferred_element_type=F32)


def nt(a, b):
    return lax.dot_general(a, b, (((1,), (1,)), ((), ())), preferred_element_type=F32)


def tn(a, b):
    return lax.dot_general(a, b, (((0,), (0,)), ((), ())), preferred_element_type=F32)


def low(value):
    return value.astype(BF16)


def when(condition, action):
    if condition is None:
        action()
    else:
        pl.when(condition)(action)


def segment(starts, row, places):
    total = jnp.zeros_like(places)
    for k in range(PACKED):
        begin = starts[row, k]
        total = total + jnp.where((begin > 0) & (places >= begin), 1, 0)
    return total


def row_scalars(starts, row, first):
    before = jnp.int32(0)
    last = jnp.int32(0)
    for k in range(PACKED):
        begin = starts[row, k]
        before = before + jnp.where((begin > 0) & (begin <= first - 1), 1, 0)
        last = last + jnp.where((begin > 0) & (begin <= first + TOKENS - 1), 1, 0)
    return before, last


def fill_masks(starts, first, carry_in, carry_out, taps, within, below):
    places = first + lax.broadcasted_iota(jnp.int32, (TOKENS, HEAD_SIZE), 0)
    side = lax.broadcasted_iota(jnp.int32, (TOKENS, TOKENS), 0)
    across = lax.broadcasted_iota(jnp.int32, (TOKENS, TOKENS), 1)
    within[...] = jnp.zeros_like(within)
    below[...] = jnp.zeros_like(below)
    for row in range(ROWS):
        span = pl.ds(row * TOKENS, TOKENS)
        mine = segment(starts, row, places)
        before, last = row_scalars(starts, row, first)
        carry_in[span, :] = (mine == before).astype(F32)
        carry_out[span, :] = (mine == last).astype(F32)
        for shift in range(1, KW):
            there = places - shift
            same = (segment(starts, row, there) == mine) & (there >= 0)
            taps[shift - 1, span, :] = same.astype(F32)
        same = segment(starts, row, first + side) == segment(starts, row, first + across)
        within[span, span] = (same & (side >= across)).astype(F32)
        below[span, span] = (same & (side > across)).astype(F32)


def padded(main, halo):
    return jnp.concatenate([halo, main], axis=0)


def unit_scale(values):
    return lax.rsqrt(jnp.sum(values * values, axis=-1, keepdims=True) + NEAR_ZERO)


def lane_of(values, lane):
    lanes = lax.broadcasted_iota(jnp.int32, values.shape, 1)
    return jnp.sum(jnp.where(lanes == lane, values, 0.0), axis=-1, keepdims=True)


def head_columns(part, head):
    return pl.ds(pl.multiple_of(part * MODEL_WIDTH + head * HEAD_SIZE, HEAD_SIZE), HEAD_SIZE)


def halves(value):
    high = low(value)
    return high, low(value - high.astype(F32))


def gram_of(keys):
    high, rest = halves(keys)
    return nt(high, high) + nt(high, rest) + nt(rest, high)


def per_row(function, *arrays):
    return jnp.concatenate(
        [
            function(row, *[array[row * TOKENS : (row + 1) * TOKENS] for array in arrays])
            for row in range(ROWS)
        ],
        axis=0,
    )


def invert(system, apart):
    eye = jnp.where(apart == 0, 1.0, 0.0)
    solved = eye - jnp.where(apart == 1, system, 0.0)
    size = 2
    while size < TOKENS:
        cross = low(jnp.where((apart >= size) & (apart < 2 * size), system, 0.0))
        rough = low(solved)
        solved = solved - nn(low(nn(rough, cross)), rough)
        size *= 2
    return solved


def kappa_eye(kept):
    side = lax.broadcasted_iota(jnp.int32, (HEAD_SIZE, HEAD_SIZE), 0)
    across = lax.broadcasted_iota(jnp.int32, (HEAD_SIZE, HEAD_SIZE), 1)
    return jnp.where(side == across, 1.0, 0.0) * kept


def mixer_forward_kernel(
    starts, tokens, halo, mixer_gain, mix, small, conv, head_gain,
    normed, pre, raw, beta, solved, solved_w, fresh, state, power, outputs, gated,
    every, carry_in, carry_out, taps, within, below, apart,
    offset, solved_u, attend, queries, arriving, leaving, send, receive,
):
    count = lax.axis_size("seq")
    index = lax.axis_index("seq")
    first = index * TOKENS
    barrier = pltpu.get_barrier_semaphore()

    @pl.when(index > 0)
    def _():
        pl.semaphore_signal(barrier, inc=1, device_id={"seq": index - 1}, device_id_type=MESH)

    @pl.when(index == 0)
    def _():
        arriving[...] = jnp.zeros_like(arriving)

    fill_masks(starts, first, carry_in, carry_out, taps, within, below)
    side = lax.broadcasted_iota(jnp.int32, (ALL, ALL), 0)
    across = lax.broadcasted_iota(jnp.int32, (ALL, ALL), 1)
    apart[...] = jnp.bitwise_xor(side, across)

    def norm(source, target, rows):
        values = source[...].astype(F32)
        scale = lax.rsqrt(jnp.mean(values * values, axis=-1, keepdims=True) + NEAR_ZERO)
        target[rows, :] = low(values * scale * mixer_gain[...])

    norm(tokens, every, pl.ds(0, ALL))
    norm(halo, every, pl.ds(ALL, ROWS * HALO))
    normed[...] = every[pl.ds(0, ALL), :]
    beta[...] = jax.nn.sigmoid(nn(every[pl.ds(0, ALL), :], small[...]))

    def project(step, _):
        columns = pl.ds(pl.multiple_of(step * 512, 512), 512)
        pre[:, columns] = nn(every[...], mix[:, columns])
        return 0

    lax.fori_loop(0, MIX // 512, project, 0)

    def convolve(columns):
        weight = conv[:, columns]
        rows = []
        for row in range(ROWS):
            main = pre[pl.ds(row * TOKENS, TOKENS), columns]
            before = pre[pl.ds(ALL + row * HALO, HALO), columns]
            longer = padded(main, before)
            total = weight[0:1] * main
            for shift in range(1, KW):
                tap = taps[shift - 1, pl.ds(row * TOKENS, TOKENS), :]
                total = total + weight[shift : shift + 1] * longer[HALO - shift : HALO - shift + TOKENS] * tap
            rows.append(total)
        total = jnp.concatenate(rows, axis=0)
        raw[:, columns] = total
        return total * jax.nn.sigmoid(total)

    def local(head):
        active_q = convolve(head_columns(0, head))
        active_k = convolve(head_columns(1, head))
        values = convolve(head_columns(2, head))
        query = active_q * (unit_scale(active_q) * HEAD_SIZE**-0.5)
        key = active_k * unit_scale(active_k)
        strength = lane_of(beta[...], BETA_AT + head)
        columns = head_columns(0, head)
        system = below[...] * (strength * gram_of(key))
        inverse = low(invert(system, apart[...]))
        solved[head] = inverse
        enter = carry_in[...]
        w = low(nn(inverse, low(strength * enter * key)))
        u = nn(inverse, low(strength * values))
        solved_w[:, columns] = w
        solved_u[:, columns] = u
        leave = low(carry_out[...] * key)
        u_low = low(u)
        for row in range(ROWS):
            span = slice(row * TOKENS, (row + 1) * TOKENS)
            before, last = row_scalars(starts, row, first)
            kept = jnp.where(before == last, 1.0, 0.0)
            power[head, row] = low(kappa_eye(kept) - tn(leave[span], w[span]))
            offset[head, row] = tn(leave[span], u_low[span])
        attend[head] = low(within[...] * nt(low(query), low(key)))
        queries[:, columns] = low(enter * query)

    def pair(step, _):
        for part in range(GROUP):
            local(step * GROUP + part)
        return 0

    lax.fori_loop(0, HEADS // GROUP, pair, 0)

    @pl.when(index + 1 < count)
    def _():
        pl.semaphore_wait(barrier, 1)

    def copy(head):
        return pltpu.make_async_remote_copy(
            src_ref=leaving.at[head], dst_ref=arriving.at[head], send_sem=send.at[head], recv_sem=receive.at[head],
            device_id={"seq": index + 1}, device_id_type=MESH,
        )

    def chain(head, _):
        @pl.when(index > 0)
        def _():
            copy(head).wait_recv()

        @pl.when(index + 1 < count)
        def _():
            for row in range(ROWS):
                leaving[head, row] = low(nn(power[head, row], arriving[head, row]) + offset[head, row])
            copy(head).start()

        columns = head_columns(0, head)
        w, u, query = solved_w[:, columns], solved_u[:, columns], queries[:, columns]
        x = low(u - per_row(lambda row, part: nn(part, arriving[head, row]), w))
        fresh[:, columns] = x
        output = per_row(lambda row, part: nn(part, arriving[head, row]), query) + nn(attend[head], x)
        outputs[:, columns] = output
        scale = lax.rsqrt(jnp.mean(output * output, axis=-1, keepdims=True) + HEAD_ZERO)
        gate = pre[pl.ds(0, ALL), head_columns(3, head)]
        gated[:, columns] = low(output * scale * head_gain[...] * (gate * jax.nn.sigmoid(gate)))
        return 0

    lax.fori_loop(0, HEADS, chain, 0)
    state[...] = arriving[...]

    @pl.when(index + 1 < count)
    def _():
        def drain(head, _):
            copy(head).wait_send()
            return 0

        lax.fori_loop(0, HEADS, drain, 0)


GROUP = 2


def mixer_forward(starts, tokens, halo, mixer_gain, mix, small, conv, head_gain):
    vmem = pl.BlockSpec(memory_space=pltpu.VMEM)
    shape = jax.ShapeDtypeStruct
    states = (HEADS, ROWS, HEAD_SIZE, HEAD_SIZE)
    return pl.pallas_call(
        mixer_forward_kernel,
        out_shape=[
            shape((ALL, MODEL_WIDTH), BF16),
            shape((ALL + ROWS * HALO, MIX), F32),
            shape((ALL, QKV), F32),
            shape((ALL, SMALL), F32),
            shape((HEADS, ALL, ALL), BF16),
            shape((ALL, MODEL_WIDTH), BF16),
            shape((ALL, MODEL_WIDTH), BF16),
            shape(states, BF16),
            shape(states, BF16),
            shape((ALL, MODEL_WIDTH), F32),
            shape((ALL, MODEL_WIDTH), BF16),
        ],
        in_specs=[pl.BlockSpec(memory_space=pltpu.SMEM)] + [vmem] * 7,
        out_specs=[vmem] * 11,
        scratch_shapes=[
            pltpu.VMEM((ALL + ROWS * HALO, MODEL_WIDTH), BF16),
            pltpu.VMEM((ALL, HEAD_SIZE), F32),
            pltpu.VMEM((ALL, HEAD_SIZE), F32),
            pltpu.VMEM((KW - 1, ALL, HEAD_SIZE), F32),
            pltpu.VMEM((ALL, ALL), F32),
            pltpu.VMEM((ALL, ALL), F32),
            pltpu.VMEM((ALL, ALL), jnp.int32),
            pltpu.VMEM(states, F32),
            pltpu.VMEM((ALL, MODEL_WIDTH), F32),
            pltpu.VMEM((HEADS, ALL, ALL), BF16),
            pltpu.VMEM((ALL, MODEL_WIDTH), BF16),
            pltpu.VMEM(states, BF16),
            pltpu.VMEM(states, BF16),
            pltpu.SemaphoreType.DMA((HEADS,)),
            pltpu.SemaphoreType.DMA((HEADS,)),
        ],
        compiler_params=pltpu.CompilerParams(
            collective_id=3, has_side_effects=True, vmem_limit_bytes=56 * 2**20
        ),
        name="mixer_forward",
    )(starts, tokens, halo, mixer_gain, mix, small, conv, head_gain)


def mixer_backward_kernel(
    starts, grad_gated, grad_mid, tokens, mixer_gain, mix, small, conv, head_gain,
    pre, raw, beta, solved, solved_w, fresh, state, power, outputs,
    grad_hidden, grad_project, grad_logits, grad_conv, grad_head, grad_gain,
    carry_in, carry_out, taps, within, below,
    grad_out, fresh_part, offset, grad_raw, grad_beta, arriving, leaving, halo_out, halo_in,
    send, receive, halo_send, halo_receive,
):
    count = lax.axis_size("seq")
    index = lax.axis_index("seq")
    first = index * TOKENS
    barrier = pltpu.get_barrier_semaphore()

    @pl.when(index + 1 < count)
    def _():
        pl.semaphore_signal(barrier, inc=1, device_id={"seq": index + 1}, device_id_type=MESH)

    @pl.when(index + 1 == count)
    def _():
        arriving[...] = jnp.zeros_like(arriving)
        halo_in[...] = jnp.zeros_like(halo_in)

    fill_masks(starts, first, carry_in, carry_out, taps, within, below)
    grad_head[...] = jnp.zeros_like(grad_head)
    grad_beta[...] = jnp.zeros_like(grad_beta)

    def active_of(part, head):
        values = raw[:, head_columns(part, head)]
        return values * jax.nn.sigmoid(values)

    def prepare(head):
        columns = head_columns(0, head)
        gate_columns = head_columns(3, head)
        gate = pre[pl.ds(0, ALL), gate_columns]
        sigma = jax.nn.sigmoid(gate)
        output = outputs[:, columns]
        scale = lax.rsqrt(jnp.mean(output * output, axis=-1, keepdims=True) + HEAD_ZERO)
        sample = output * scale
        incoming = grad_gated[:, columns]
        gain = head_gain[...]
        grad_project[:, gate_columns] = low(incoming * sample * gain * (sigma * (1.0 + gate * (1.0 - sigma))))
        grad_sample = incoming * (gate * sigma)
        grad_head[0:1, :] += jnp.sum(grad_sample * sample, axis=0, keepdims=True)
        scaled = grad_sample * gain
        mean = jnp.mean(scaled * output, axis=-1, keepdims=True)
        here = low(scale * scaled - output * (scale * scale * scale * mean))
        grad_out[:, columns] = here
        active_q, active_k = active_of(0, head), active_of(1, head)
        query = active_q * (unit_scale(active_q) * HEAD_SIZE**-0.5)
        key = active_k * unit_scale(active_k)
        attend = low(within[...] * nt(low(query), low(key)))
        part = tn(attend, here)
        fresh_part[:, columns] = part
        entering = low(carry_in[...] * query)
        part_low = low(part)
        w = solved_w[:, columns]
        for row in range(ROWS):
            span = slice(row * TOKENS, (row + 1) * TOKENS)
            offset[head, row] = tn(entering[span], here[span]) - tn(w[span], part_low[span])

    def prepare_some(step, _):
        for part in range(GROUP):
            prepare(step * GROUP + part)
        return 0

    lax.fori_loop(0, HEADS // GROUP, prepare_some, 0)

    @pl.when(index > 0)
    def _():
        pl.semaphore_wait(barrier, 1)

    def copy(head):
        return pltpu.make_async_remote_copy(
            src_ref=leaving.at[head], dst_ref=arriving.at[head], send_sem=send.at[head], recv_sem=receive.at[head],
            device_id={"seq": index - 1}, device_id_type=MESH,
        )

    def chain(head, _):
        @pl.when(index + 1 < count)
        def _():
            copy(head).wait_recv()

        @pl.when(index > 0)
        def _():
            for row in range(ROWS):
                leaving[head, row] = low(tn(power[head, row], arriving[head, row]) + offset[head, row])
            copy(head).start()

        return 0

    lax.fori_loop(0, HEADS, chain, 0)

    def finish(head):
        columns = head_columns(0, head)
        raw_q, raw_k = raw[:, columns], raw[:, head_columns(1, head)]
        raw_v = raw[:, head_columns(2, head)]
        sigma_q, sigma_k, sigma_v = jax.nn.sigmoid(raw_q), jax.nn.sigmoid(raw_k), jax.nn.sigmoid(raw_v)
        active_q, active_k, values = raw_q * sigma_q, raw_k * sigma_k, raw_v * sigma_v
        scale_q, scale_k = unit_scale(active_q), unit_scale(active_k)
        query = low(active_q * (scale_q * HEAD_SIZE**-0.5))
        key_full = active_k * scale_k
        key = low(key_full)
        enter, leave = carry_in[...], carry_out[...]
        strength = lane_of(beta[...], BETA_AT + head)
        here = grad_out[:, columns]
        x = fresh[:, columns]
        leaving_keys = low(leave * key_full)
        grad_x = fresh_part[:, columns] + per_row(lambda row, part: nn(part, arriving[head, row]), leaving_keys)
        y = tn(solved[head], low(grad_x))
        y_low = low(y)
        grad_attend = low(within[...] * nt(here, x))
        gram = nt(key, key)
        grad_system = -below[...] * nt(y_low, x)
        grad_gram = low(strength * grad_system)
        grad_q = nn(grad_attend, key) + enter * per_row(lambda row, part: nt(part, state[head, row]), here)
        grad_k = (
            tn(grad_attend, query)
            + leave * per_row(lambda row, part: nt(part, arriving[head, row]), x)
            + nn(grad_gram, key)
            + tn(grad_gram, key)
            - strength * enter * per_row(lambda row, part: nt(part, state[head, row]), y_low)
        )
        z = values - enter * per_row(lambda row, part: nn(part, state[head, row]), key)
        grad_v = strength * y
        grad_strength = jnp.sum(y * z, axis=-1, keepdims=True) + jnp.sum(grad_system * gram, axis=-1, keepdims=True)
        lanes = lax.broadcasted_iota(jnp.int32, grad_beta.shape, 1)
        grad_beta[...] = jnp.where(lanes == BETA_AT + head, grad_strength, grad_beta[...])

        def through(grad, active, scale, part, sigma, extra):
            grad = grad * extra
            mean = jnp.sum(active * grad, axis=-1, keepdims=True)
            grad = scale * grad - active * (scale * scale * scale * mean)
            return grad * (sigma * (1.0 + part * (1.0 - sigma)))

        grad_raw[:, columns] = through(grad_q, active_q, scale_q, raw_q, sigma_q, HEAD_SIZE**-0.5)
        grad_raw[:, head_columns(1, head)] = through(grad_k, active_k, scale_k, raw_k, sigma_k, 1.0)
        grad_raw[:, head_columns(2, head)] = grad_v * (sigma_v * (1.0 + raw_v * (1.0 - sigma_v)))

    def finish_some(step, _):
        for part in range(GROUP):
            finish(step * GROUP + part)
        return 0

    lax.fori_loop(0, HEADS // GROUP, finish_some, 0)

    def convolve_back(step, _):
        columns = pl.ds(pl.multiple_of(step * HEAD_SIZE, HEAD_SIZE), HEAD_SIZE)
        weight = conv[:, columns]
        nothing = jnp.zeros((HALO, HEAD_SIZE), F32)
        sums = [jnp.zeros((1, HEAD_SIZE), F32) for _ in range(KW)]
        early = []
        for row in range(ROWS):
            span = pl.ds(row * TOKENS, TOKENS)
            grad = grad_raw[span, columns]
            main = pre[span, columns]
            longer = padded(main, pre[pl.ds(ALL + row * HALO, HALO), columns])
            total = weight[0:1] * jnp.concatenate([nothing, grad], axis=0)
            sums[0] = sums[0] + jnp.sum(grad * main, axis=0, keepdims=True)
            for shift in range(1, KW):
                masked = grad * taps[shift - 1, span, :]
                wide = jnp.concatenate([nothing, masked, nothing], axis=0)
                total = total + weight[shift : shift + 1] * wide[shift : shift + HALO + TOKENS]
                before = longer[HALO - shift : HALO - shift + TOKENS]
                sums[shift] = sums[shift] + jnp.sum(masked * before, axis=0, keepdims=True)
            early.append(total[:HALO])
            grad_raw[span, columns] = total[HALO:]
        halo_out[:, columns] = low(jnp.concatenate(early, axis=0))
        grad_conv[:, columns] = jnp.concatenate(sums, axis=0)
        return 0

    lax.fori_loop(0, QKV // HEAD_SIZE, convolve_back, 0)
    back = pltpu.make_async_remote_copy(
        src_ref=halo_out, dst_ref=halo_in, send_sem=halo_send, recv_sem=halo_receive,
        device_id={"seq": index - 1}, device_id_type=MESH,
    )

    @pl.when(index > 0)
    def _():
        back.start()

    strengths = beta[...]
    grad_logits[...] = low(grad_beta[...] * strengths * (1.0 - strengths))

    @pl.when(index + 1 < count)
    def _():
        back.wait_recv()

    for row in range(ROWS):
        end = pl.ds((row + 1) * TOKENS - HALO, HALO)
        grad_raw[end, :] += halo_in[...].astype(F32)[row * HALO : (row + 1) * HALO]
    grad_project[:, pl.ds(0, QKV)] = low(grad_raw[...])

    def normed_back(step, _):
        rows = pl.ds(pl.multiple_of(step * 256, 256), 256)
        grad_hidden[:, rows] = nt(grad_project[...], mix[rows, :]) + nt(grad_logits[...], small[rows, :])
        return 0

    lax.fori_loop(0, MODEL_WIDTH // 256, normed_back, 0)
    hidden = tokens[...].astype(F32)
    scale = lax.rsqrt(jnp.mean(hidden * hidden, axis=-1, keepdims=True) + NEAR_ZERO)
    grad = grad_hidden[...]
    grad_gain[...] = jnp.sum(grad * hidden * scale, axis=0, keepdims=True)
    scaled = grad * mixer_gain[...]
    mean = jnp.mean(scaled * hidden, axis=-1, keepdims=True)
    grad_hidden[...] = grad_mid[...] + scale * scaled - hidden * (scale * scale * scale * mean)

    @pl.when(index > 0)
    def _():
        back.wait_send()

        def drain(head, _):
            copy(head).wait_send()
            return 0

        lax.fori_loop(0, HEADS, drain, 0)


def mixer_backward(*operands):
    vmem = pl.BlockSpec(memory_space=pltpu.VMEM)
    shape = jax.ShapeDtypeStruct
    states = (HEADS, ROWS, HEAD_SIZE, HEAD_SIZE)
    return pl.pallas_call(
        mixer_backward_kernel,
        out_shape=[
            shape((ALL, MODEL_WIDTH), F32),
            shape((ALL, MIX), BF16),
            shape((ALL, SMALL), BF16),
            shape((KW, QKV), F32),
            shape((8, HEAD_SIZE), F32),
            shape((1, MODEL_WIDTH), F32),
        ],
        in_specs=[pl.BlockSpec(memory_space=pltpu.SMEM)] + [vmem] * 17,
        out_specs=[vmem] * 6,
        scratch_shapes=[
            pltpu.VMEM((ALL, HEAD_SIZE), F32),
            pltpu.VMEM((ALL, HEAD_SIZE), F32),
            pltpu.VMEM((KW - 1, ALL, HEAD_SIZE), F32),
            pltpu.VMEM((ALL, ALL), F32),
            pltpu.VMEM((ALL, ALL), F32),
            pltpu.VMEM((ALL, MODEL_WIDTH), BF16),
            pltpu.VMEM((ALL, MODEL_WIDTH), F32),
            pltpu.VMEM(states, F32),
            pltpu.VMEM((ALL, QKV), F32),
            pltpu.VMEM((ALL, SMALL), F32),
            pltpu.VMEM(states, BF16),
            pltpu.VMEM(states, BF16),
            pltpu.VMEM((ROWS * HALO, QKV), BF16),
            pltpu.VMEM((ROWS * HALO, QKV), BF16),
            pltpu.SemaphoreType.DMA((HEADS,)),
            pltpu.SemaphoreType.DMA((HEADS,)),
            pltpu.SemaphoreType.DMA,
            pltpu.SemaphoreType.DMA,
        ],
        compiler_params=pltpu.CompilerParams(
            collective_id=4, has_side_effects=True, vmem_limit_bytes=56 * 2**20
        ),
        name="mixer_backward",
    )(*operands)


def place():
    row, spot = lax.axis_index("dp"), lax.axis_index("seq")
    level, core = spot // 2, lax.rem(spot, 2)
    near = row + 1 - 2 * lax.rem(row, 2)
    far = row + 2 - 4 * (row // 2)
    first = near * (1 - core) + far * core
    second = far * (1 - core) + near * core
    return row, spot, level, core, first, second, 3 - row


def greet(levels, row, spot, level, core, first, second):
    barrier = pltpu.get_barrier_semaphore()
    above, below = level + 1 < levels, level >= 1
    sibling = spot + 1 - 2 * core

    def signal(device):
        pl.semaphore_signal(barrier, inc=1, device_id=device, device_id_type=MESH)

    signal({"dp": first, "seq": spot})
    signal({"dp": second, "seq": spot})
    signal({"dp": row, "seq": sibling})
    pl.when(above)(lambda: signal({"dp": row, "seq": spot + 2}))
    pl.when(below)(lambda: signal({"dp": row, "seq": spot - 2}))
    peers = 3 + (level + levels - 1) // levels + (2 * levels - 2 - level) // levels
    pl.semaphore_wait(barrier, peers)
    return above, below, sibling


class Sender:
    def __init__(self, semaphores):
        self.semaphores, self.used, self.pending = semaphores, 0, []

    def start(self, condition, source, target, device, arrival):
        copy = pltpu.make_async_remote_copy(
            src_ref=source, dst_ref=target, send_sem=self.semaphores.at[self.used], recv_sem=arrival,
            device_id=device, device_id_type=MESH,
        )
        self.used += 1
        when(condition, copy.start)
        self.pending.append((condition, copy))

    def arrived(self, condition, target, device, arrival):
        copy = pltpu.make_async_remote_copy(
            src_ref=target, dst_ref=target, send_sem=self.semaphores.at[0], recv_sem=arrival,
            device_id=device, device_id_type=MESH,
        )
        when(condition, copy.wait_recv)

    def drain(self):
        for condition, copy in self.pending:
            when(condition, copy.wait_send)


def gather_kernel(levels, share, full, by_level, by_first, by_second, by_core, sends, local):
    row, spot, level, core, first, second, both = place()
    above, below, sibling = greet(levels, row, spot, level, core, first, second)
    sender = Sender(sends)
    here = {"dp": first, "seq": spot}

    def piece(half, owner, owner_level):
        return full.at[owner, owner_level * 2 + core, half]

    def send(condition, half, owner, owner_level, device, arrival, own):
        target = piece(half, owner, owner_level)
        sender.start(condition, share.at[half] if own else target, target, device, arrival)

    def along(condition, up, half, side, owner, owner_level, own=False):
        device = {"dp": row, "seq": spot + 2 if up else spot - 2}
        send(condition, half, owner, owner_level, device, by_level.at[half, side, owner_level], own)

    def to_first(condition, half, owner_level, own=False):
        send(condition, half, row, owner_level, here, by_first.at[half, owner_level], own)

    def to_second(condition, half, side, owner, owner_level, own=False):
        device = {"dp": second, "seq": spot}
        send(condition, half, owner, owner_level, device, by_second.at[half, side, owner_level], own)

    def to_core(condition, half, owner, owner_level, own=False):
        device = {"dp": row, "seq": sibling}
        send(condition, half, owner, owner_level, device, by_core.at[half, owner, owner_level], own)

    def arrived(condition, half, owner, owner_level, arrival):
        sender.arrived(condition, piece(half, owner, owner_level), here, arrival)

    kept = [pltpu.make_async_copy(share.at[half], full.at[row, spot, half], local.at[half]) for half in range(2)]
    for copy in kept:
        copy.start()
    to_first(None, 1, level, True)
    along(above, True, 0, 0, row, level, True)
    along(below, False, 0, 0, row, level, True)
    to_second(None, 0, 0, row, level, True)
    to_first(None, 0, level, True)
    to_second(None, 1, 0, row, level, True)
    along(above, True, 1, 0, row, level, True)
    along(below, False, 1, 0, row, level, True)
    to_core(None, 0, row, level, True)
    to_core(None, 1, row, level, True)
    arrived(None, 1, first, level, by_first.at[1, level])
    along(above, True, 1, 1, first, level)
    along(below, False, 1, 1, first, level)
    to_second(None, 1, 1, first, level)
    to_core(None, 1, first, level)
    arrived(None, 0, first, level, by_first.at[0, level])
    to_second(None, 0, 1, first, level)
    to_core(None, 0, first, level)

    def from_second(condition, owner_level):
        for half in range(2):
            for side, owner in ((0, second), (1, both)):
                arrived(condition, half, owner, owner_level, by_second.at[half, side, owner_level])
                to_core(condition, half, owner, owner_level)

    waiting = [(None, level)]
    for step in range(1, levels):
        ways = ((level - step >= 0, level - step, True), (level + step < levels, level + step, False))

        def onward(up):
            if up:
                return (level - step >= 0) & above
            return (level + step < levels) & below

        for condition, source, up in ways:
            arrived(condition, 0, row, source, by_level.at[0, 0, source])
            if step < levels - 1:
                along(onward(up), up, 0, 0, row, source)
            to_first(condition, 0, source)
            to_second(condition, 0, 0, row, source)
            to_core(condition, 0, row, source)
        for side, owner in ((0, row), (1, first)):
            for condition, source, up in ways:
                arrived(condition, 1, owner, source, by_level.at[1, side, source])
                if step < levels - 1:
                    along(onward(up), up, 1, side, owner, source)
                to_second(condition, 1, side, owner, source)
                to_core(condition, 1, owner, source)
        for condition, source, up in ways:
            arrived(condition, 0, first, source, by_first.at[0, source])
            to_second(condition, 0, 1, first, source)
            to_core(condition, 0, first, source)
        for condition, source in waiting:
            from_second(condition, source)
        waiting = [(condition, source) for condition, source, _ in ways]
    for condition, source in waiting:
        from_second(condition, source)
    for half in range(2):
        for owner in range(4):
            for source in range(levels):
                target = full.at[owner, source * 2 + 1 - core, half]
                sender.arrived(None, target, here, by_core.at[half, owner, source])
    for copy in kept:
        copy.wait()
    sender.drain()


def gather(levels, share):
    dma = pltpu.SemaphoreType.DMA
    return pl.pallas_call(
        functools.partial(gather_kernel, levels),
        out_shape=jax.ShapeDtypeStruct((4, 2 * levels) + share.shape, share.dtype),
        in_specs=[pl.BlockSpec(memory_space=pl.ANY)],
        out_specs=pl.BlockSpec(memory_space=pl.ANY),
        scratch_shapes=[
            dma((2, 2, levels)),
            dma((2, levels)),
            dma((2, 2, levels)),
            dma((2, 4, levels)),
            dma((8 + 34 * levels,)),
            dma((2,)),
        ],
        compiler_params=pltpu.CompilerParams(collective_id=1, has_side_effects=True),
        name="gather_weights",
    )(share)


def scatter_kernel(
    levels, slots, grads, result, total, by_second, by_first, by_level, staged,
    core_sem, second_sem, first_sem, level_sem, load_sem, sends,
):
    row, spot, level, core, first, second, both = place()
    above, below, sibling = greet(levels, row, spot, level, core, first, second)
    sender = Sender(sends)
    here = {"dp": first, "seq": spot}
    width = grads.shape[-1]
    order = []
    for step in range((levels + 1) // 2):
        order += [levels - 1 - step] + ([step] if step < levels - 1 - step else [])

    def add(target, *others):
        def body(step, _):
            columns = pl.ds(pl.multiple_of(step * CHUNK, CHUNK), CHUNK)
            value = target[:, columns]
            for other in others:
                value = value + other[:, columns]
            target[:, columns] = value
            return 0

        lax.fori_loop(0, width // CHUNK, body, 0)

    def arrived(target, arrival):
        sender.arrived(None, target, here, arrival)

    away = [(end, half, side, owner) for end in order for half in (1, 0) for side, owner in ((0, second), (1, both))]
    stay = [(end, half, side, owner) for end in order for half in (1, 0) for side, owner in ((0, row), (1, first))]
    listed = away + stay
    for end, half, _, owner in listed:
        device = {"dp": row, "seq": sibling}
        source = grads.at[owner, end * 2 + 1 - core, half]
        sender.start(None, source, total.at[half, owner, end], device, core_sem.at[half, owner, end])

    def load(place_in_list):
        end, half, _, owner = listed[place_in_list]
        slot = place_in_list % slots
        return pltpu.make_async_copy(grads.at[owner, end * 2 + core, half], staged.at[slot], load_sem.at[slot])

    for slot in range(slots):
        load(slot).start()
    for number, (end, half, side, owner) in enumerate(listed):
        load(number).wait()
        sums = total.at[half, owner, end]
        arrived(sums, core_sem.at[half, owner, end])
        add(sums, staged.at[number % slots])
        if number + slots < len(listed):
            load(number + slots).start()
        if number < len(away):
            device = {"dp": second, "seq": spot}
            sender.start(None, sums, by_second.at[half, side, end], device, second_sem.at[half, side, end])

    def along(half, side, owner, end):
        sums = total.at[half, owner, end]

        def take(way):
            arrived(by_level.at[half, side, way, end], level_sem.at[half, side, way, end])
            add(sums, by_level.at[half, side, way, end])

        def pass_on(way, condition, has_more):
            pl.when(condition & has_more)(lambda: take(way))
            device = {"dp": row, "seq": spot + 2 if way == 0 else spot - 2}
            target = by_level.at[half, side, way, end]
            sender.start(condition, sums, target, device, level_sem.at[half, side, way, end])

        if end > 0:
            pass_on(0, level < end, below)
        if end < levels - 1:
            pass_on(1, level > end, above)

    def finish_first(end):
        sums = total.at[0, row, end]
        arrived(by_first.at[0, end], first_sem.at[0, end])
        add(sums, by_first.at[0, end])
        along(0, 0, row, end)

    previous = None
    for end in order:
        for side, owner in ((0, row), (1, first)):
            arrived(by_second.at[1, side, end], second_sem.at[1, side, end])
            add(total.at[1, owner, end], by_second.at[1, side, end])
            along(1, side, owner, end)
        for side, owner in ((1, first), (0, row)):
            sums = total.at[0, owner, end]
            arrived(by_second.at[0, side, end], second_sem.at[0, side, end])
            add(sums, by_second.at[0, side, end])
            if side == 1:
                sender.start(None, sums, by_first.at[0, end], here, first_sem.at[0, end])
        if previous is not None:
            finish_first(previous)
        previous = end
    finish_first(previous)

    def collect(half, side, owner):
        sums = total.at[half, owner, level]

        def take(way):
            arrived(by_level.at[half, side, way, level], level_sem.at[half, side, way, level])
            add(sums, by_level.at[half, side, way, level])

        pl.when(below)(lambda: take(0))
        pl.when(above)(lambda: take(1))

    def write(half, *parts):
        def body(step, _):
            columns = pl.ds(pl.multiple_of(step * CHUNK, CHUNK), CHUNK)
            value = parts[0][:, columns].astype(F32)
            for part in parts[1:]:
                value = value + part[:, columns].astype(F32)
            result[half, :, columns] = value
            return 0

        lax.fori_loop(0, width // CHUNK, body, 0)

    collect(1, 1, first)
    sender.start(None, total.at[1, first, level], by_first.at[1, 0], here, first_sem.at[1, 0])
    collect(1, 0, row)
    collect(0, 0, row)
    write(0, total.at[0, row, level])
    arrived(by_first.at[1, 0], first_sem.at[1, 0])
    write(1, total.at[1, row, level], by_first.at[1, 0])
    sender.drain()


def scatter(levels, grads):
    dma = pltpu.SemaphoreType.DMA
    piece = grads.shape[-2:]
    slots = 4
    return pl.pallas_call(
        functools.partial(scatter_kernel, levels, slots),
        out_shape=jax.ShapeDtypeStruct((2,) + piece, F32),
        in_specs=[pl.BlockSpec(memory_space=pl.ANY)],
        out_specs=pl.BlockSpec(memory_space=pltpu.VMEM),
        scratch_shapes=[
            pltpu.VMEM((2, 4, levels) + piece, BF16),
            pltpu.VMEM((2, 2, levels) + piece, BF16),
            pltpu.VMEM((2, levels) + piece, BF16),
            pltpu.VMEM((2, 2, 2, levels) + piece, BF16),
            pltpu.VMEM((slots,) + piece, BF16),
            dma((2, 4, levels)),
            dma((2, 2, levels)),
            dma((2, levels)),
            dma((2, 2, 2, levels)),
            dma((slots,)),
            dma((8 + 24 * levels,)),
        ],
        compiler_params=pltpu.CompilerParams(
            collective_id=2, has_side_effects=True, vmem_limit_bytes=58 * 2**20
        ),
        name="scatter_grads",
    )(grads)


def fits(rows):
    return lax.axis_size("dp") == 4 and lax.axis_size("seq") <= 16 and lax.axis_size("seq") % 2 == 0 and rows == 32


def gather_all(share):
    rows, width = share.shape
    if fits(rows):
        full = gather(lax.axis_size("seq") // 2, share.reshape(2, rows // 2, width))
        return full.reshape(-1, width)
    return lax.all_gather(share, ("dp", "seq"), axis=0, tiled=True)


def scatter_sum(grads):
    width = grads.shape[1]
    rows = grads.shape[0] // lax.axis_size(("dp", "seq"))
    if fits(rows):
        shaped = grads.reshape(lax.axis_size("dp"), lax.axis_size("seq"), 2, rows // 2, width)
        return scatter(lax.axis_size("seq") // 2, shaped).reshape(rows, width)
    return lax.psum_scatter(grads, ("dp", "seq"), scatter_dimension=0, tiled=True).astype(F32)


def pack_down(part):
    lead, tall = part.shape[:-2], part.shape[-2] // 11
    tiles = part.reshape(lead + (11, tall, 4, 2, 128))
    n = len(lead)
    moved = tiles.transpose(tuple(range(n)) + (n + 2, n + 1, n + 3, n, n + 4))
    return moved.reshape(lead + (4 * tall, FF))


def unpack_down(part):
    lead, tall = part.shape[:-2], part.shape[-2] // 4
    tiles = part.reshape(lead + (4, tall, 2, 11, 128))
    n = len(lead)
    moved = tiles.transpose(tuple(range(n)) + (n + 3, n + 1, n, n + 2, n + 4))
    return moved.reshape(lead + (11 * tall, MODEL_WIDTH))


def pack_small(mixer, mlp, beta, conv):
    rows = mixer.shape[0]
    taps = conv.reshape(KW, 3, rows).transpose(2, 0, 1).reshape(rows, 3 * KW)
    parts = jnp.concatenate([mixer[:, None], mlp[:, None], beta, taps], axis=1)
    return jnp.pad(parts, ((0, 0), (0, SMALL - parts.shape[1])))


def unpack_conv(small, rows):
    taps = small[:, CONV_AT : CONV_AT + 3 * KW].reshape(-1, rows, KW, 3)
    return taps.transpose(2, 0, 3, 1).reshape(KW, QKV)


def silu_slope(values):
    sigma = jax.nn.sigmoid(values)
    return sigma * (1.0 + values * (1.0 - sigma))


def norm_back(grad_in, values, inverse, gain):
    scaled = grad_in * gain
    return inverse * scaled - values * inverse**3 * jnp.mean(scaled * values, axis=-1, keepdims=True)


def dot(left, right, axes):
    return lax.dot_general(left, right, ((axes[:1], axes[1:]), ((), ())), preferred_element_type=F32)


def shards(
    tokens, cotangent, starts, mixer_gain, mix_weight, conv_weight, beta_weight, head_gain, out_weight, mlp_gain,
    upgate_weight, down_weight,
):
    rows, block, width = tokens.shape
    share_rows = mix_weight.shape[1]
    count = lax.axis_size("seq")
    halo = lax.ppermute(tokens[:, block - HALO :, :], "seq", [(k, k + 1) for k in range(count - 1)])
    halo = halo.reshape(rows * HALO, width)
    share = jnp.concatenate(
        [
            mix_weight[0],
            pack_small(mixer_gain[0], mlp_gain[0], beta_weight[0], conv_weight[0]),
            out_weight[0],
            upgate_weight[0],
            pack_down(down_weight[0]),
        ],
        axis=1,
    )
    full = gather_all(share)
    mix = full[:, :MIX]
    small = full[:, AT_SMALL:AT_OUT]
    out_w = full[:, AT_OUT:AT_UP]
    upgate_w = full[:, AT_UP:AT_DOWN]
    down_w = unpack_down(full[:, AT_DOWN:].reshape(-1, share_rows, FF)).reshape(FF, width)
    conv = unpack_conv(small, share_rows).astype(F32)
    mixer_g = small[:, 0].astype(F32)[None]
    mlp_g = small[:, 1].astype(F32)[None]
    head_f = head_gain.astype(F32)

    flat = tokens.reshape(rows * block, width)
    normed, pre, raw, beta, solved, solved_w, fresh, state, power, outputs, gated = mixer_forward(
        starts, flat, halo, mixer_g, mix, small, conv, head_f
    )
    hidden_mid = flat.astype(F32) + dot(gated, out_w, (1, 0))
    inverse_mid = lax.rsqrt(jnp.mean(hidden_mid * hidden_mid, axis=-1, keepdims=True) + NEAR_ZERO)
    normed_mid = (hidden_mid * inverse_mid * mlp_g).astype(BF16)
    upgate = dot(normed_mid, upgate_w, (1, 0))
    gate_part, up_part = upgate[:, :FF], upgate[:, FF:]
    acted = (jax.nn.silu(gate_part) * up_part).astype(BF16)
    output = (hidden_mid + dot(acted, down_w, (1, 0))).astype(BF16)

    down_grad = cotangent.reshape(rows * block, width)
    grad = down_grad.astype(F32)
    grad_down_w = dot(acted, down_grad, (0, 0)).astype(BF16)
    grad_acted = dot(down_grad, down_w, (1, 1))
    grad_upgate = jnp.concatenate(
        [grad_acted * up_part * silu_slope(gate_part), grad_acted * jax.nn.silu(gate_part)], axis=-1
    ).astype(BF16)
    grad_upgate_w = dot(normed_mid, grad_upgate, (0, 0)).astype(BF16)
    grad_normed_mid = dot(grad_upgate, upgate_w, (1, 1))
    grad_mlp_g = jnp.sum(grad_normed_mid * hidden_mid * inverse_mid, axis=0)
    grad_mid = grad + norm_back(grad_normed_mid, hidden_mid, inverse_mid, mlp_g)
    attn_grad = grad_mid.astype(BF16)
    grad_out_w = dot(gated, attn_grad, (0, 0)).astype(BF16)
    grad_gated = dot(attn_grad, out_w, (1, 1))

    grad_hidden, grad_project, grad_logits, grad_conv, grad_head, grad_mixer_g = mixer_backward(
        starts, grad_gated, grad_mid, flat, mixer_g, mix, small, conv, head_f,
        pre, raw, beta, solved, solved_w, fresh, state, power, outputs,
    )
    head_sum = lax.psum(jnp.sum(grad_head, axis=0, keepdims=True), ("dp", "seq"))
    grad_mix_w = dot(normed, grad_project, (0, 0)).astype(BF16)
    grad_beta_w = dot(normed, grad_logits, (0, 0))[:, BETA_AT:CONV_AT]
    taps = grad_conv.reshape(KW, -1, 3, share_rows).transpose(1, 3, 0, 2).reshape(width, 3 * KW)
    grad_small = jnp.concatenate([grad_mixer_g.T, grad_mlp_g[:, None], grad_beta_w, taps], axis=1)
    grad_small = jnp.pad(grad_small, ((0, 0), (0, SMALL - grad_small.shape[1]))).astype(BF16)
    packed = jnp.concatenate(
        [
            grad_mix_w,
            grad_small,
            grad_out_w,
            grad_upgate_w,
            pack_down(grad_down_w.reshape(-1, share_rows * FF // width, width)).reshape(width, FF),
        ],
        axis=1,
    )
    mine = scatter_sum(packed)
    conv_mine = mine[:, AT_SMALL + CONV_AT : AT_SMALL + CONV_AT + 3 * KW]
    conv_mine = conv_mine.reshape(share_rows, KW, 3).transpose(1, 2, 0).reshape(1, KW, 3 * share_rows)
    return (
        output.reshape(rows, block, width),
        grad_hidden.reshape(rows, block, width),
        mine[:, AT_SMALL][None],
        mine[:, :MIX][None],
        conv_mine,
        mine[:, AT_SMALL + BETA_AT : AT_SMALL + CONV_AT][None],
        head_sum,
        mine[:, AT_OUT:AT_UP][None],
        mine[:, AT_SMALL + 1][None],
        mine[:, AT_UP:AT_DOWN][None],
        unpack_down(mine[:, AT_DOWN:])[None],
    )


def solution(mesh):
    both = ("dp", "seq")
    in_specs = (
        P("dp", "seq", None),
        P("dp", "seq", None),
        P("dp", None),
        P(None, both),
        P(None, both, None),
        P(None, None, both),
        P(None, both, None),
        P(),
        P(None, both, None),
        P(None, both),
        P(None, both, None),
        P(None, both, None),
    )
    out_specs = (
        P("dp", "seq", None),
        P("dp", "seq", None),
        P(None, both),
        P(None, both, None),
        P(None, None, both),
        P(None, both, None),
        P(),
        P(None, both, None),
        P(None, both),
        P(None, both, None),
        P(None, both, None),
    )
    return jax.shard_map(shards, mesh=mesh, in_specs=in_specs, out_specs=out_specs, check_vma=False)
```

```python
import functools

import jax
import jax.numpy as jnp
from jax import lax
from jax.experimental import pallas as pl
from jax.experimental.pallas import tpu as pltpu
from jax.sharding import PartitionSpec as P

MODEL_WIDTH = 1024
HEADS = 8
HEAD_SIZE = 128
FF = 2816
KW = 4
PACKED = 4

MESH = pl.DeviceIdType.MESH
F32 = jnp.float32
BF16 = jnp.bfloat16
TOKENS = 128
ROWS = 2
ALL = ROWS * TOKENS
HALO = 8
NEAR_ZERO = 1e-06
HEAD_ZERO = 1e-05
MIX = 4 * MODEL_WIDTH
QKV = 3 * MODEL_WIDTH
SMALL = 256
BETA_AT = 2
CONV_AT = 10
AT_SMALL = MIX
AT_OUT = AT_SMALL + SMALL
AT_UP = AT_OUT + MODEL_WIDTH
AT_DOWN = AT_UP + 2 * FF
PACK = AT_DOWN + FF
CHUNK_REST = (PACK - AT_OUT) // 2
CHUNK_MIX = AT_OUT // 2
PIECE = 16
SLOTS = 4
EDGE = 16
WIDE = 512
GROUP = 2


def nn(a, b):
    return lax.dot_general(a, b, (((1,), (0,)), ((), ())), preferred_element_type=F32)


def nt(a, b):
    return lax.dot_general(a, b, (((1,), (1,)), ((), ())), preferred_element_type=F32)


def tn(a, b):
    return lax.dot_general(a, b, (((0,), (0,)), ((), ())), preferred_element_type=F32)


def low(value):
    return value.astype(BF16)


def when(condition, action):
    if condition is None:
        action()
    else:
        pl.when(condition)(action)


class Place:
    def __init__(self, levels):
        self.levels = levels
        self.row, self.spot = lax.axis_index("dp"), lax.axis_index("seq")
        self.level, self.core = self.spot // 2, lax.rem(self.spot, 2)
        self.near = self.row + 1 - 2 * lax.rem(self.row, 2)
        self.far = self.row + 2 - 4 * (self.row // 2)
        self.first = self.near * (1 - self.core) + self.far * self.core
        self.second = self.far * (1 - self.core) + self.near * self.core
        self.both = 3 - self.row
        self.above, self.below = self.level + 1 < levels, self.level >= 1
        self.sibling = self.spot + 1 - 2 * self.core

    def greet(self, chain):
        barrier = pltpu.get_barrier_semaphore()
        levels, level, core = self.levels, self.level, self.core

        def signal(row, spot):
            pl.semaphore_signal(barrier, inc=1, device_id={"dp": row, "seq": spot}, device_id_type=MESH)

        signal(self.first, self.spot)
        signal(self.second, self.spot)
        signal(self.row, self.sibling)
        pl.when(self.above)(lambda: signal(self.row, self.spot + 2))
        pl.when(self.below)(lambda: signal(self.row, self.spot - 2))
        has_above = (2 * levels - 2 - level) // levels
        has_below = (level + levels - 1) // levels
        peers = 3 + has_above + has_below
        if chain > 0:
            pl.when(self.below & (core == 0))(lambda: signal(self.row, self.spot - 1))
            peers = peers + has_above * core
        if chain < 0:
            pl.when(self.above & (core == 1))(lambda: signal(self.row, self.spot + 1))
            peers = peers + has_below * (1 - core)
        pl.semaphore_wait(barrier, peers)

    def rows_of(self, owner, spot, half):
        return pl.ds(pl.multiple_of(((owner * 2 * self.levels + spot) * 2 + half) * PIECE, PIECE), PIECE)


class Sender:
    def __init__(self, semaphores):
        self.semaphores, self.used, self.pending = semaphores, 0, []

    def start(self, condition, source, target, device, arrival):
        copy = pltpu.make_async_remote_copy(
            src_ref=source, dst_ref=target, send_sem=self.semaphores.at[self.used], recv_sem=arrival,
            device_id=device, device_id_type=MESH,
        )
        self.used += 1
        when(condition, copy.start)
        self.pending.append((condition, copy))

    def arrived(self, condition, target, device, arrival):
        copy = pltpu.make_async_remote_copy(
            src_ref=target, dst_ref=target, send_sem=self.semaphores.at[0], recv_sem=arrival,
            device_id=device, device_id_type=MESH,
        )
        when(condition, copy.wait_recv)

    def drain(self):
        for condition, copy in self.pending:
            when(condition, copy.wait_send)


def advance(steps, count=1):
    for _ in range(count):
        next(steps, None)


def until(steps, mark):
    for found in steps:
        if found == mark:
            return


def gather_semaphores(levels):
    dma = pltpu.SemaphoreType.DMA
    return [dma((2, 2, levels)), dma((2, levels)), dma((2, 2, levels)), dma((2, 4, levels)), dma((8 + 34 * levels,))]


def gather_steps(at, full, columns, by_level, by_first, by_second, by_core, sends):
    levels, row, spot, level, core = at.levels, at.row, at.spot, at.level, at.core
    first, second, both, above, below = at.first, at.second, at.both, at.above, at.below
    sender = Sender(sends)
    here = {"dp": first, "seq": spot}

    def piece(half, owner, owner_level):
        return full.at[at.rows_of(owner, owner_level * 2 + core, half), columns]

    def send(condition, half, owner, owner_level, device, arrival):
        target = piece(half, owner, owner_level)
        sender.start(condition, target, target, device, arrival)

    def along(condition, up, half, side, owner, owner_level):
        device = {"dp": row, "seq": spot + 2 if up else spot - 2}
        send(condition, half, owner, owner_level, device, by_level.at[half, side, owner_level])

    def to_first(condition, half, owner_level):
        send(condition, half, row, owner_level, here, by_first.at[half, owner_level])

    def to_second(condition, half, side, owner, owner_level):
        device = {"dp": second, "seq": spot}
        send(condition, half, owner, owner_level, device, by_second.at[half, side, owner_level])

    def to_core(condition, half, owner, owner_level):
        device = {"dp": row, "seq": at.sibling}
        send(condition, half, owner, owner_level, device, by_core.at[half, owner, owner_level])

    def arrived(condition, half, owner, owner_level, arrival):
        sender.arrived(condition, piece(half, owner, owner_level), here, arrival)

    to_first(None, 1, level)
    along(above, True, 0, 0, row, level)
    along(below, False, 0, 0, row, level)
    to_second(None, 0, 0, row, level)
    to_first(None, 0, level)
    to_second(None, 1, 0, row, level)
    along(above, True, 1, 0, row, level)
    along(below, False, 1, 0, row, level)
    to_core(None, 0, row, level)
    to_core(None, 1, row, level)
    yield "started"
    arrived(None, 1, first, level, by_first.at[1, level])
    along(above, True, 1, 1, first, level)
    along(below, False, 1, 1, first, level)
    to_second(None, 1, 1, first, level)
    to_core(None, 1, first, level)
    yield "step"
    arrived(None, 0, first, level, by_first.at[0, level])
    to_second(None, 0, 1, first, level)
    to_core(None, 0, first, level)
    yield "step"

    def from_second(condition, owner_level, half):
        for side, owner in ((0, second), (1, both)):
            arrived(condition, half, owner, owner_level, by_second.at[half, side, owner_level])
            to_core(condition, half, owner, owner_level)

    waiting = [(None, level)]
    for step in range(1, levels):
        ways = ((level - step >= 0, level - step, True), (level + step < levels, level + step, False))

        def onward(up, step=step):
            if up:
                return (level - step >= 0) & above
            return (level + step < levels) & below

        for condition, source, up in ways:
            arrived(condition, 0, row, source, by_level.at[0, 0, source])
            if step < levels - 1:
                along(onward(up), up, 0, 0, row, source)
            to_first(condition, 0, source)
            to_second(condition, 0, 0, row, source)
            to_core(condition, 0, row, source)
        yield "step"
        for side, owner in ((0, row), (1, first)):
            for condition, source, up in ways:
                arrived(condition, 1, owner, source, by_level.at[1, side, source])
                if step < levels - 1:
                    along(onward(up), up, 1, side, owner, source)
                to_second(condition, 1, side, owner, source)
                to_core(condition, 1, owner, source)
            yield "step"
        for condition, source, up in ways:
            arrived(condition, 0, first, source, by_first.at[0, source])
            to_second(condition, 0, 1, first, source)
            to_core(condition, 0, first, source)
        yield "step"
        for half in range(2):
            for condition, source in waiting:
                from_second(condition, source, half)
            yield "step"
        waiting = [(condition, source) for condition, source, _ in ways]
    for half in range(2):
        for condition, source in waiting:
            from_second(condition, source, half)
        yield "step"
    yield "issued"
    for half in range(2):
        for owner in range(4):
            for source in range(levels):
                target = full.at[at.rows_of(owner, source * 2 + 1 - core, half), columns]
                sender.arrived(None, target, here, by_core.at[half, owner, source])
    yield "arrived"
    sender.drain()


def scatter_buffers(levels, width, staged):
    dma = pltpu.SemaphoreType.DMA
    buffers = [
        pltpu.VMEM((2, 4, levels, PIECE, width), BF16),
        pltpu.VMEM((2, 2, levels, PIECE, width), BF16),
        pltpu.VMEM((levels + 1, PIECE, width), BF16),
        pltpu.VMEM((3, levels + 1, PIECE, width), BF16),
        dma((2, 4, levels)),
        dma((2, 2, levels)),
        dma((levels + 1,)),
        dma((3, levels + 1)),
        dma((8 + 24 * levels,)),
    ]
    if staged:
        buffers += [pltpu.VMEM((SLOTS, PIECE, width), BF16), dma((SLOTS,))]
    return buffers


def scatter_steps(
    at, chunk, grads, targets, total, by_second, by_first, by_level,
    core_sem, second_sem, first_sem, level_sem, sends, staged=None, load_sem=None,
):
    levels, row, spot, level, core = at.levels, at.row, at.spot, at.level, at.core
    first, second, both, above, below = at.first, at.second, at.both, at.above, at.below
    sender = Sender(sends)
    here = {"dp": first, "seq": spot}
    width = grads.shape[-1]
    order = []
    for step in range((levels + 1) // 2):
        order += [levels - 1 - step] + ([step] if step < levels - 1 - step else [])

    def add(target, *others):
        def body(step, _):
            columns = pl.ds(pl.multiple_of(step * chunk, chunk), chunk)
            value = target[:, columns]
            for other in others:
                value = value + other[:, columns]
            target[:, columns] = value
            return 0

        lax.fori_loop(0, width // chunk, body, 0)

    def arrived(target, arrival):
        sender.arrived(None, target, here, arrival)

    away = [(end, half, side, owner) for end in order for half in (1, 0) for side, owner in ((0, second), (1, both))]
    stay = [(end, half, side, owner) for end in order for half in (1, 0) for side, owner in ((0, row), (1, first))]
    listed = away + stay
    for end, half, _, owner in listed:
        device = {"dp": row, "seq": at.sibling}
        source = grads.at[at.rows_of(owner, end * 2 + 1 - core, half), :]
        sender.start(None, source, total.at[half, owner, end], device, core_sem.at[half, owner, end])

    def load(number):
        end, half, _, owner = listed[number]
        slot = number % SLOTS
        source = grads.at[at.rows_of(owner, end * 2 + core, half), :]
        return pltpu.make_async_copy(source, staged.at[slot], load_sem.at[slot])

    if staged is not None:
        for slot in range(SLOTS):
            load(slot).start()
    yield "started"

    def take_listed(number):
        end, half, side, owner = listed[number]
        sums = total.at[half, owner, end]
        if staged is None:
            arrived(sums, core_sem.at[half, owner, end])
            add(sums, grads.at[at.rows_of(owner, end * 2 + core, half), :])
        else:
            load(number).wait()
            arrived(sums, core_sem.at[half, owner, end])
            add(sums, staged.at[number % SLOTS])
            if number + SLOTS < len(listed):
                load(number + SLOTS).start()
        if number < len(away):
            device = {"dp": second, "seq": spot}
            sender.start(None, sums, by_second.at[half, side, end], device, second_sem.at[half, side, end])

    for number in range(len(away)):
        take_listed(number)
        yield "step"

    def lane(half, side):
        return 0 if half == 0 else 1 + side

    def along(half, side, owner, end):
        sums = total.at[half, owner, end]
        place = lane(half, side)

        def take():
            arrived(by_level.at[place, end], level_sem.at[place, end])
            add(sums, by_level.at[place, end])

        if end > 0:
            pl.when((level < end) & below)(take)
            device = {"dp": row, "seq": spot + 2}
            sender.start(level < end, sums, by_level.at[place, end], device, level_sem.at[place, end])
        if end < levels - 1:
            pl.when((level > end) & above)(take)
            device = {"dp": row, "seq": spot - 2}
            beyond = level > end + 1
            sender.start(beyond, sums, by_level.at[place, end], device, level_sem.at[place, end])
            sender.start(
                level == end + 1, sums, by_level.at[place, levels], device, level_sem.at[place, levels]
            )

    def finish_first(end):
        sums = total.at[0, row, end]
        arrived(by_first.at[end], first_sem.at[end])
        add(sums, by_first.at[end])
        along(0, 0, row, end)

    previous = None
    for turn, end in enumerate(order):
        for number in range(4):
            take_listed(len(away) + 4 * turn + number)
            if number % 2 == 1:
                yield "step"
        for side, owner in ((0, row), (1, first)):
            arrived(by_second.at[1, side, end], second_sem.at[1, side, end])
            add(total.at[1, owner, end], by_second.at[1, side, end])
            along(1, side, owner, end)
            yield "step"
        for side, owner in ((1, first), (0, row)):
            sums = total.at[0, owner, end]
            arrived(by_second.at[0, side, end], second_sem.at[0, side, end])
            add(sums, by_second.at[0, side, end])
            if side == 1:
                sender.start(None, sums, by_first.at[end], here, first_sem.at[end])
        yield "step"
        if previous is not None:
            finish_first(previous)
            yield "step"
        previous = end
    finish_first(previous)
    yield "step"

    def collect(half, side, owner):
        sums = total.at[half, owner, level]
        place = lane(half, side)

        def take(slot):
            arrived(by_level.at[place, slot], level_sem.at[place, slot])
            add(sums, by_level.at[place, slot])

        pl.when(below)(lambda: take(level))
        pl.when(above)(lambda: take(levels))

    def final(half, *parts):
        begin = 0
        for target in targets:
            columns = pl.ds(begin, target.shape[-1])
            value = parts[0][:, columns].astype(F32)
            for part in parts[1:]:
                value = value + part[:, columns].astype(F32)
            target[pl.ds(half * PIECE, PIECE), :] = value
            begin += target.shape[-1]

    collect(1, 1, first)
    sender.start(None, total.at[1, first, level], by_first.at[levels], here, first_sem.at[levels])
    yield "step"
    collect(1, 0, row)
    yield "step"
    collect(0, 0, row)
    final(0, total.at[0, row, level])
    yield "step"
    arrived(by_first.at[levels], first_sem.at[levels])
    final(1, total.at[1, row, level], by_first.at[levels])
    sender.drain()


def segment(starts, row, places):
    total = jnp.zeros_like(places)
    for k in range(PACKED):
        begin = starts[row, k]
        total = total + jnp.where((begin > 0) & (places >= begin), 1, 0)
    return total


def row_scalars(starts, row, first):
    before = jnp.int32(0)
    last = jnp.int32(0)
    for k in range(PACKED):
        begin = starts[row, k]
        before = before + jnp.where((begin > 0) & (begin <= first - 1), 1, 0)
        last = last + jnp.where((begin > 0) & (begin <= first + TOKENS - 1), 1, 0)
    return before, last


def fill_masks(starts, first, carry_in, carry_out, taps, within, below):
    places = first + lax.broadcasted_iota(jnp.int32, (TOKENS, HEAD_SIZE), 0)
    side = lax.broadcasted_iota(jnp.int32, (TOKENS, TOKENS), 0)
    across = lax.broadcasted_iota(jnp.int32, (TOKENS, TOKENS), 1)
    within[...] = jnp.zeros_like(within)
    below[...] = jnp.zeros_like(below)
    for row in range(ROWS):
        span = pl.ds(row * TOKENS, TOKENS)
        mine = segment(starts, row, places)
        before, last = row_scalars(starts, row, first)
        carry_in[span, :] = (mine == before).astype(F32)
        carry_out[span, :] = (mine == last).astype(F32)
        for shift in range(1, KW):
            there = places - shift
            same = (segment(starts, row, there) == mine) & (there >= 0)
            taps[shift - 1, span, :] = same.astype(F32)
        same = segment(starts, row, first + side) == segment(starts, row, first + across)
        within[span, span] = (same & (side >= across)).astype(F32)
        below[span, span] = (same & (side > across)).astype(F32)


def padded(main, halo):
    return jnp.concatenate([halo, main], axis=0)


def unit_scale(values):
    return lax.rsqrt(jnp.sum(values * values, axis=-1, keepdims=True) + NEAR_ZERO)


def lane_of(values, lane):
    lanes = lax.broadcasted_iota(jnp.int32, values.shape, 1)
    return jnp.sum(jnp.where(lanes == lane, values, 0.0), axis=-1, keepdims=True)


def head_columns(part, head):
    return pl.ds(pl.multiple_of(part * MODEL_WIDTH + head * HEAD_SIZE, HEAD_SIZE), HEAD_SIZE)


def halves(value):
    high = low(value)
    return high, low(value - high.astype(F32))


def gram_of(keys):
    high, rest = halves(keys)
    return nt(high, high) + nt(high, rest) + nt(rest, high)


def per_row(function, *arrays):
    return jnp.concatenate(
        [
            function(row, *[array[row * TOKENS : (row + 1) * TOKENS] for array in arrays])
            for row in range(ROWS)
        ],
        axis=0,
    )


def invert(system, apart):
    eye = jnp.where(apart == 0, 1.0, 0.0)
    solved = eye - jnp.where(apart == 1, system, 0.0)
    size = 2
    while size < TOKENS:
        cross = low(jnp.where((apart >= size) & (apart < 2 * size), system, 0.0))
        rough = low(solved)
        solved = solved - nn(low(nn(rough, cross)), rough)
        size *= 2
    return solved


def kappa_eye(kept):
    side = lax.broadcasted_iota(jnp.int32, (HEAD_SIZE, HEAD_SIZE), 0)
    across = lax.broadcasted_iota(jnp.int32, (HEAD_SIZE, HEAD_SIZE), 1)
    return jnp.where(side == across, 1.0, 0.0) * kept


def tap_rows(small_rows):
    group = 3 * HEAD_SIZE
    side = lax.broadcasted_iota(jnp.int32, (group, group), 0)
    across = lax.broadcasted_iota(jnp.int32, (group, group), 1)
    third, device, lane = side // HEAD_SIZE, (side % HEAD_SIZE) // 32, side % 32
    move = jnp.where(across == device * 96 + third * 32 + lane, 1.0, 0.0).astype(BF16)
    wanted = []
    for block in range(MODEL_WIDTH // HEAD_SIZE):
        lanes = slice(block * HEAD_SIZE, (block + 1) * HEAD_SIZE)
        parts = [small_rows[CONV_AT + 3 * j : CONV_AT + 3 * j + 3, lanes] for j in range(KW)]
        source = jnp.concatenate(
            [jnp.concatenate([part[c : c + 1] for c in range(3)], axis=1) for part in parts], axis=0
        )
        wanted.append(nn(low(source), move))
    return wanted


def mixer_forward_kernel(routed, *refs):
    (starts, tokens, head_gain), refs = refs[:3], refs[3:]
    if routed:
        shares, refs = refs[:5], refs[5:]
    (full, normed, pre, raw, beta, solved, solved_w, fresh, state, power, outputs, gated, conv, gains), refs = refs[:14], refs[14:]
    (every, carry_in, carry_out, taps, within, below, apart), refs = refs[:7], refs[7:]
    (offset, solved_u, attend, queries, arriving, leaving, send, receive), refs = refs[:8], refs[8:]
    (mix, small, halo, halo_send, halo_receive, load_sem), refs = refs[:6], refs[6:]
    count = lax.axis_size("seq")
    index = lax.axis_index("seq")
    first = index * TOKENS
    rest = iter(())
    if routed:
        keep_sem, routes = refs[0], refs[1:]
        at = Place(count // 2)
        mine = pl.ds(pl.multiple_of((at.row * count + index) * 2 * PIECE, 2 * PIECE), 2 * PIECE)
        kept = []
        begin = 0
        for number, share in enumerate(shares):
            columns = pl.ds(begin, share.shape[-1])
            kept.append(pltpu.make_async_copy(share, full.at[mine, columns], keep_sem.at[number]))
            begin += share.shape[-1]
        for copy in kept:
            copy.start()
        at.greet(1)
    else:
        barrier = pltpu.get_barrier_semaphore()

        @pl.when(index > 0)
        def _():
            pl.semaphore_signal(barrier, inc=1, device_id={"seq": index - 1}, device_id_type=MESH)

        @pl.when(index + 1 < count)
        def _():
            pl.semaphore_wait(barrier, 1)

    def tail(row):
        return pltpu.make_async_remote_copy(
            src_ref=tokens.at[pl.ds((row + 1) * TOKENS - EDGE, EDGE), :], dst_ref=halo.at[pl.ds(row * EDGE, EDGE), :],
            send_sem=halo_send.at[row], recv_sem=halo_receive.at[row], device_id={"seq": index + 1}, device_id_type=MESH,
        )

    @pl.when(index + 1 < count)
    def _():
        for row in range(ROWS):
            tail(row).start()

    if routed:
        kept[0].wait()
        kept[1].wait()
        wanted = gather_steps(at, full, pl.ds(0, AT_OUT), *routes[:5])
        until(wanted, "started")

    @pl.when(index == 0)
    def _():
        arriving[...] = jnp.zeros_like(arriving)
        halo[...] = jnp.zeros_like(halo)

    fill_masks(starts, first, carry_in, carry_out, taps, within, below)
    side = lax.broadcasted_iota(jnp.int32, (ALL, ALL), 0)
    across = lax.broadcasted_iota(jnp.int32, (ALL, ALL), 1)
    apart[...] = jnp.bitwise_xor(side, across)
    if routed:
        until(wanted, "issued")
        for copy in kept[2:]:
            copy.wait()
        rest = gather_steps(at, full, pl.ds(AT_OUT, PACK - AT_OUT), *routes[5:])
        until(rest, "started")
        until(wanted, "arrived")

    def load(number):
        if number < 0:
            return pltpu.make_async_copy(full.at[:, pl.ds(AT_SMALL, SMALL)], small, load_sem.at[MIX // WIDE])
        columns = pl.ds(number * WIDE, WIDE)
        return pltpu.make_async_copy(full.at[:, columns], mix.at[:, columns], load_sem.at[number])

    for number in range(-1, MIX // WIDE):
        load(number).start()
    load(-1).wait()
    small_rows = small[:, pl.ds(0, HEAD_SIZE)].astype(F32).T
    gains[...] = small_rows[:8]
    for block, part in enumerate(tap_rows(small_rows)):
        conv[:, pl.ds(block * 3 * HEAD_SIZE, 3 * HEAD_SIZE)] = part

    def norm(source, target, rows):
        values = source[...].astype(F32)
        scale = lax.rsqrt(jnp.mean(values * values, axis=-1, keepdims=True) + NEAR_ZERO)
        target[rows, :] = low(values * scale * gains[0:1, :])

    norm(tokens, every, pl.ds(0, ALL))

    @pl.when(index > 0)
    def _():
        for row in range(ROWS):
            tail(row).wait_recv()

    norm(halo, every, pl.ds(ALL, ROWS * EDGE))
    normed[...] = every[pl.ds(0, ALL), :]
    beta[...] = jax.nn.sigmoid(nn(every[pl.ds(0, ALL), :], small[...]))
    for number in range(MIX // WIDE):
        load(number).wait()
        columns = pl.ds(number * WIDE, WIDE)
        pre[:, columns] = nn(every[...], mix[:, columns])
        if number % 4 == 3:
            advance(rest)

    def convolve(columns):
        weight = conv[:, columns]
        rows = []
        for row in range(ROWS):
            main = pre[pl.ds(row * TOKENS, TOKENS), columns]
            before = pre[pl.ds(ALL + (row + 1) * EDGE - HALO, HALO), columns]
            longer = padded(main, before)
            total = weight[0:1] * main
            for shift in range(1, KW):
                tap = taps[shift - 1, pl.ds(row * TOKENS, TOKENS), :]
                total = total + weight[shift : shift + 1] * longer[HALO - shift : HALO - shift + TOKENS] * tap
            rows.append(total)
        total = jnp.concatenate(rows, axis=0)
        raw[:, columns] = total
        return total * jax.nn.sigmoid(total)

    def local(head):
        active_q = convolve(head_columns(0, head))
        active_k = convolve(head_columns(1, head))
        values = convolve(head_columns(2, head))
        query = active_q * (unit_scale(active_q) * HEAD_SIZE**-0.5)
        key = active_k * unit_scale(active_k)
        strength = lane_of(beta[...], BETA_AT + head)
        columns = head_columns(0, head)
        system = below[...] * (strength * gram_of(key))
        inverse = low(invert(system, apart[...]))
        solved[head] = inverse
        enter = carry_in[...]
        w = low(nn(inverse, low(strength * enter * key)))
        u = nn(inverse, low(strength * values))
        solved_w[:, columns] = w
        solved_u[:, columns] = u
        leave = low(carry_out[...] * key)
        u_low = low(u)
        for row in range(ROWS):
            span = slice(row * TOKENS, (row + 1) * TOKENS)
            before, last = row_scalars(starts, row, first)
            kept = jnp.where(before == last, 1.0, 0.0)
            power[head, row] = low(kappa_eye(kept) - tn(leave[span], w[span]))
            offset[head, row] = tn(leave[span], u_low[span])
        attend[head] = low(within[...] * nt(low(query), low(key)))
        queries[:, columns] = low(enter * query)


    for step in range(HEADS // GROUP):
        for part in range(GROUP):
            local(step * GROUP + part)
        advance(rest, 2)

    def copy(head):
        return pltpu.make_async_remote_copy(
            src_ref=leaving.at[head], dst_ref=arriving.at[head], send_sem=send.at[head], recv_sem=receive.at[head],
            device_id={"seq": index + 1}, device_id_type=MESH,
        )

    def chain(head):
        @pl.when(index > 0)
        def _():
            copy(head).wait_recv()

        @pl.when(index + 1 < count)
        def _():
            for row in range(ROWS):
                leaving[head, row] = low(nn(power[head, row], arriving[head, row]) + offset[head, row])
            copy(head).start()

        columns = head_columns(0, head)
        w, u, query = solved_w[:, columns], solved_u[:, columns], queries[:, columns]
        x = low(u - per_row(lambda row, part: nn(part, arriving[head, row]), w))
        fresh[:, columns] = x
        output = per_row(lambda row, part: nn(part, arriving[head, row]), query) + nn(attend[head], x)
        outputs[:, columns] = output
        scale = lax.rsqrt(jnp.mean(output * output, axis=-1, keepdims=True) + HEAD_ZERO)
        gate = pre[pl.ds(0, ALL), head_columns(3, head)]
        gated[:, columns] = low(output * scale * head_gain[...] * (gate * jax.nn.sigmoid(gate)))

    for head in range(HEADS):
        chain(head)
        advance(rest)
    state[...] = arriving[...]

    @pl.when(index + 1 < count)
    def _():
        for row in range(ROWS):
            tail(row).wait_send()

        def drain(head, _):
            copy(head).wait_send()
            return 0

        lax.fori_loop(0, HEADS, drain, 0)

    until(rest, "end")
    if routed:
        until(wanted, "end")


def mixer_forward(starts, tokens, head_gain, weights):
    routed = len(weights) > 1
    vmem, anywhere = pl.BlockSpec(memory_space=pltpu.VMEM), pl.BlockSpec(memory_space=pl.ANY)
    dma = pltpu.SemaphoreType.DMA
    shape = jax.ShapeDtypeStruct
    states = (HEADS, ROWS, HEAD_SIZE, HEAD_SIZE)
    long = ALL + ROWS * EDGE
    whole = [shape((MODEL_WIDTH, PACK), BF16)] if routed else []
    levels = lax.axis_size("seq") // 2
    routes = [dma((5,))] + gather_semaphores(levels) + gather_semaphores(levels) if routed else []
    results = pl.pallas_call(
        functools.partial(mixer_forward_kernel, routed),
        out_shape=whole + [
            shape((ALL, MODEL_WIDTH), BF16),
            shape((long, MIX), F32),
            shape((ALL, QKV), F32),
            shape((ALL, SMALL), F32),
            shape((HEADS, ALL, ALL), BF16),
            shape((ALL, MODEL_WIDTH), BF16),
            shape((ALL, MODEL_WIDTH), BF16),
            shape(states, BF16),
            shape(states, BF16),
            shape((ALL, MODEL_WIDTH), F32),
            shape((ALL, MODEL_WIDTH), BF16),
            shape((KW, QKV), F32),
            shape((8, MODEL_WIDTH), F32),
        ],
        in_specs=[pl.BlockSpec(memory_space=pltpu.SMEM), vmem, vmem] + [anywhere] * len(weights),
        out_specs=[anywhere] * len(whole) + [vmem] * 13,
        scratch_shapes=[
            pltpu.VMEM((long, MODEL_WIDTH), BF16),
            pltpu.VMEM((ALL, HEAD_SIZE), F32),
            pltpu.VMEM((ALL, HEAD_SIZE), F32),
            pltpu.VMEM((KW - 1, ALL, HEAD_SIZE), F32),
            pltpu.VMEM((ALL, ALL), F32),
            pltpu.VMEM((ALL, ALL), F32),
            pltpu.VMEM((ALL, ALL), jnp.int32),
            pltpu.VMEM(states, F32),
            pltpu.VMEM((ALL, MODEL_WIDTH), F32),
            pltpu.VMEM((HEADS, ALL, ALL), BF16),
            pltpu.VMEM((ALL, MODEL_WIDTH), BF16),
            pltpu.VMEM(states, BF16),
            pltpu.VMEM(states, BF16),
            dma((HEADS,)),
            dma((HEADS,)),
            pltpu.VMEM((MODEL_WIDTH, MIX), BF16),
            pltpu.VMEM((MODEL_WIDTH, SMALL), BF16),
            pltpu.VMEM((ROWS * EDGE, MODEL_WIDTH), BF16),
            dma((ROWS,)),
            dma((ROWS,)),
            dma((MIX // WIDE + 1,)),
        ] + routes,
        compiler_params=pltpu.CompilerParams(
            collective_id=1, has_side_effects=True, vmem_limit_bytes=56 * 2**20
        ),
        name="mixer_forward",
    )(starts, tokens, head_gain, *weights)
    return results if routed else [weights[0]] + list(results)


def mixer_backward_kernel(routed, *refs):
    (starts, grad_gated, grad_mid, tokens, gains, full, conv, head_gain), refs = refs[:8], refs[8:]
    (pre, raw, beta, solved, solved_w, fresh, state, power, outputs), refs = refs[:9], refs[9:]
    if routed:
        grads, refs = refs[0], refs[1:]
    (grad_hidden, grad_project, grad_logits, grad_conv, grad_head, grad_gain), refs = refs[:6], refs[6:]
    if routed:
        targets, refs = refs[:3], refs[3:]
    (carry_in, carry_out, taps, within, below), refs = refs[:5], refs[5:]
    (grad_out, fresh_part, offset, grad_raw, grad_beta, arriving, leaving, halo_out, halo_in), refs = refs[:9], refs[9:]
    (send, receive, halo_send, halo_receive, mix, small, load_sem), refs = refs[:7], refs[7:]
    count = lax.axis_size("seq")
    index = lax.axis_index("seq")
    first = index * TOKENS
    sums = iter(())
    if routed:
        at = Place(count // 2)
        at.greet(-1)
        sums = scatter_steps(at, CHUNK_REST, grads, targets, *refs)
        until(sums, "started")
    else:
        barrier = pltpu.get_barrier_semaphore()

        @pl.when(index + 1 < count)
        def _():
            pl.semaphore_signal(barrier, inc=1, device_id={"seq": index + 1}, device_id_type=MESH)

        @pl.when(index > 0)
        def _():
            pl.semaphore_wait(barrier, 1)

    load_mix = pltpu.make_async_copy(full.at[:, pl.ds(0, MIX)], mix, load_sem.at[0])
    load_small = pltpu.make_async_copy(full.at[:, pl.ds(AT_SMALL, SMALL)], small, load_sem.at[1])
    load_mix.start()
    load_small.start()

    @pl.when(index + 1 == count)
    def _():
        arriving[...] = jnp.zeros_like(arriving)
        halo_in[...] = jnp.zeros_like(halo_in)

    fill_masks(starts, first, carry_in, carry_out, taps, within, below)
    grad_head[...] = jnp.zeros_like(grad_head)
    grad_beta[...] = jnp.zeros_like(grad_beta)

    def active_of(part, head):
        values = raw[:, head_columns(part, head)]
        return values * jax.nn.sigmoid(values)

    def prepare(head):
        columns = head_columns(0, head)
        gate_columns = head_columns(3, head)
        gate = pre[pl.ds(0, ALL), gate_columns]
        sigma = jax.nn.sigmoid(gate)
        output = outputs[:, columns]
        scale = lax.rsqrt(jnp.mean(output * output, axis=-1, keepdims=True) + HEAD_ZERO)
        sample = output * scale
        incoming = grad_gated[:, columns]
        gain = head_gain[...]
        grad_project[:, gate_columns] = low(incoming * sample * gain * (sigma * (1.0 + gate * (1.0 - sigma))))
        grad_sample = incoming * (gate * sigma)
        grad_head[0:1, :] += jnp.sum(grad_sample * sample, axis=0, keepdims=True)
        scaled = grad_sample * gain
        mean = jnp.mean(scaled * output, axis=-1, keepdims=True)
        here = low(scale * scaled - output * (scale * scale * scale * mean))
        grad_out[:, columns] = here
        active_q, active_k = active_of(0, head), active_of(1, head)
        query = active_q * (unit_scale(active_q) * HEAD_SIZE**-0.5)
        key = active_k * unit_scale(active_k)
        attend = low(within[...] * nt(low(query), low(key)))
        part = tn(attend, here)
        fresh_part[:, columns] = part
        entering = low(carry_in[...] * query)
        part_low = low(part)
        w = solved_w[:, columns]
        for row in range(ROWS):
            span = slice(row * TOKENS, (row + 1) * TOKENS)
            offset[head, row] = tn(entering[span], here[span]) - tn(w[span], part_low[span])

    for step in range(HEADS // GROUP):
        for part in range(GROUP):
            prepare(step * GROUP + part)
        advance(sums, 4)

    def copy(head):
        return pltpu.make_async_remote_copy(
            src_ref=leaving.at[head], dst_ref=arriving.at[head], send_sem=send.at[head], recv_sem=receive.at[head],
            device_id={"seq": index - 1}, device_id_type=MESH,
        )

    def chain(head):
        @pl.when(index + 1 < count)
        def _():
            copy(head).wait_recv()

        @pl.when(index > 0)
        def _():
            for row in range(ROWS):
                leaving[head, row] = low(tn(power[head, row], arriving[head, row]) + offset[head, row])
            copy(head).start()

    for head in range(HEADS):
        chain(head)
        if head % 2 == 1:
            advance(sums)

    def finish(head):
        columns = head_columns(0, head)
        raw_q, raw_k = raw[:, columns], raw[:, head_columns(1, head)]
        raw_v = raw[:, head_columns(2, head)]
        sigma_q, sigma_k, sigma_v = jax.nn.sigmoid(raw_q), jax.nn.sigmoid(raw_k), jax.nn.sigmoid(raw_v)
        active_q, active_k, values = raw_q * sigma_q, raw_k * sigma_k, raw_v * sigma_v
        scale_q, scale_k = unit_scale(active_q), unit_scale(active_k)
        query = low(active_q * (scale_q * HEAD_SIZE**-0.5))
        key_full = active_k * scale_k
        key = low(key_full)
        enter, leave = carry_in[...], carry_out[...]
        strength = lane_of(beta[...], BETA_AT + head)
        here = grad_out[:, columns]
        x = fresh[:, columns]
        leaving_keys = low(leave * key_full)
        grad_x = fresh_part[:, columns] + per_row(lambda row, part: nn(part, arriving[head, row]), leaving_keys)
        y = tn(solved[head], low(grad_x))
        y_low = low(y)
        grad_attend = low(within[...] * nt(here, x))
        gram = nt(key, key)
        grad_system = -below[...] * nt(y_low, x)
        grad_gram = low(strength * grad_system)
        grad_q = nn(grad_attend, key) + enter * per_row(lambda row, part: nt(part, state[head, row]), here)
        grad_k = (
            tn(grad_attend, query)
            + leave * per_row(lambda row, part: nt(part, arriving[head, row]), x)
            + nn(grad_gram, key)
            + tn(grad_gram, key)
            - strength * enter * per_row(lambda row, part: nt(part, state[head, row]), y_low)
        )
        z = values - enter * per_row(lambda row, part: nn(part, state[head, row]), key)
        grad_v = strength * y
        grad_strength = jnp.sum(y * z, axis=-1, keepdims=True) + jnp.sum(grad_system * gram, axis=-1, keepdims=True)
        lanes = lax.broadcasted_iota(jnp.int32, grad_beta.shape, 1)
        grad_beta[...] = jnp.where(lanes == BETA_AT + head, grad_strength, grad_beta[...])

        def through(grad, active, scale, part, sigma, extra):
            grad = grad * extra
            mean = jnp.sum(active * grad, axis=-1, keepdims=True)
            grad = scale * grad - active * (scale * scale * scale * mean)
            return grad * (sigma * (1.0 + part * (1.0 - sigma)))

        grad_raw[:, columns] = through(grad_q, active_q, scale_q, raw_q, sigma_q, HEAD_SIZE**-0.5)
        grad_raw[:, head_columns(1, head)] = through(grad_k, active_k, scale_k, raw_k, sigma_k, 1.0)
        grad_raw[:, head_columns(2, head)] = grad_v * (sigma_v * (1.0 + raw_v * (1.0 - sigma_v)))

    for step in range(HEADS // GROUP):
        for part in range(GROUP):
            finish(step * GROUP + part)
        advance(sums, 3)

    def convolve_back(step, _):
        columns = pl.ds(pl.multiple_of(step * HEAD_SIZE, HEAD_SIZE), HEAD_SIZE)
        weight = conv[:, columns]
        nothing = jnp.zeros((HALO, HEAD_SIZE), F32)
        sums = [jnp.zeros((1, HEAD_SIZE), F32) for _ in range(KW)]
        early = []
        for row in range(ROWS):
            span = pl.ds(row * TOKENS, TOKENS)
            grad = grad_raw[span, columns]
            main = pre[span, columns]
            longer = padded(main, pre[pl.ds(ALL + (row + 1) * EDGE - HALO, HALO), columns])
            total = weight[0:1] * jnp.concatenate([nothing, grad], axis=0)
            sums[0] = sums[0] + jnp.sum(grad * main, axis=0, keepdims=True)
            for shift in range(1, KW):
                masked = grad * taps[shift - 1, span, :]
                wide = jnp.concatenate([nothing, masked, nothing], axis=0)
                total = total + weight[shift : shift + 1] * wide[shift : shift + HALO + TOKENS]
                before = longer[HALO - shift : HALO - shift + TOKENS]
                sums[shift] = sums[shift] + jnp.sum(masked * before, axis=0, keepdims=True)
            early.append(total[:HALO])
            grad_raw[span, columns] = total[HALO:]
        halo_out[:, columns] = low(jnp.concatenate(early, axis=0))
        grad_conv[:, columns] = jnp.concatenate(sums, axis=0)
        return 0

    for part in range(3):
        lax.fori_loop(part * HEADS, (part + 1) * HEADS, convolve_back, 0)
        advance(sums)
    back = pltpu.make_async_remote_copy(
        src_ref=halo_out, dst_ref=halo_in, send_sem=halo_send, recv_sem=halo_receive,
        device_id={"seq": index - 1}, device_id_type=MESH,
    )

    @pl.when(index > 0)
    def _():
        back.start()

    strengths = beta[...]
    grad_logits[...] = low(grad_beta[...] * strengths * (1.0 - strengths))

    @pl.when(index + 1 < count)
    def _():
        back.wait_recv()

    for row in range(ROWS):
        end = pl.ds((row + 1) * TOKENS - HALO, HALO)
        grad_raw[end, :] += halo_in[...].astype(F32)[row * HALO : (row + 1) * HALO]
    grad_project[:, pl.ds(0, QKV)] = low(grad_raw[...])

    load_mix.wait()
    load_small.wait()
    advance(sums)

    def normed_back(step, _):
        rows = pl.ds(pl.multiple_of(step * 256, 256), 256)
        grad_hidden[:, rows] = nt(grad_project[...], mix[rows, :]) + nt(grad_logits[...], small[rows, :])
        return 0

    lax.fori_loop(0, MODEL_WIDTH // 256, normed_back, 0)
    hidden = tokens[...].astype(F32)
    scale = lax.rsqrt(jnp.mean(hidden * hidden, axis=-1, keepdims=True) + NEAR_ZERO)
    grad = grad_hidden[...]
    grad_gain[...] = jnp.sum(grad * hidden * scale, axis=0, keepdims=True)
    scaled = grad * gains[0:1, :]
    mean = jnp.mean(scaled * hidden, axis=-1, keepdims=True)
    grad_hidden[...] = grad_mid[...] + scale * scaled - hidden * (scale * scale * scale * mean)

    @pl.when(index > 0)
    def _():
        back.wait_send()

        def drain(head, _):
            copy(head).wait_send()
            return 0

        lax.fori_loop(0, HEADS, drain, 0)

    until(sums, "end")


def mixer_backward(operands, grads):
    routed = grads is not None
    vmem, anywhere = pl.BlockSpec(memory_space=pltpu.VMEM), pl.BlockSpec(memory_space=pl.ANY)
    dma = pltpu.SemaphoreType.DMA
    shape = jax.ShapeDtypeStruct
    states = (HEADS, ROWS, HEAD_SIZE, HEAD_SIZE)
    sums, buffers, more = [], [], []
    if routed:
        more = [grads]
        sums = [shape((2 * PIECE, width), F32) for width in (MODEL_WIDTH, 2 * FF, FF)]
        buffers = scatter_buffers(lax.axis_size("seq") // 2, PACK - AT_OUT, True)
    return pl.pallas_call(
        functools.partial(mixer_backward_kernel, routed),
        out_shape=[
            shape((ALL, MODEL_WIDTH), F32),
            shape((ALL, MIX), BF16),
            shape((ALL, SMALL), BF16),
            shape((KW, QKV), F32),
            shape((8, HEAD_SIZE), F32),
            shape((1, MODEL_WIDTH), F32),
        ] + sums,
        in_specs=[pl.BlockSpec(memory_space=pltpu.SMEM)] + [vmem] * 4 + [anywhere] + [vmem] * 11 + [anywhere] * len(more),
        out_specs=[vmem] * (6 + len(sums)),
        scratch_shapes=[
            pltpu.VMEM((ALL, HEAD_SIZE), F32),
            pltpu.VMEM((ALL, HEAD_SIZE), F32),
            pltpu.VMEM((KW - 1, ALL, HEAD_SIZE), F32),
            pltpu.VMEM((ALL, ALL), F32),
            pltpu.VMEM((ALL, ALL), F32),
            pltpu.VMEM((ALL, MODEL_WIDTH), BF16),
            pltpu.VMEM((ALL, MODEL_WIDTH), F32),
            pltpu.VMEM(states, F32),
            pltpu.VMEM((ALL, QKV), F32),
            pltpu.VMEM((ALL, SMALL), F32),
            pltpu.VMEM(states, BF16),
            pltpu.VMEM(states, BF16),
            pltpu.VMEM((ROWS * HALO, QKV), BF16),
            pltpu.VMEM((ROWS * HALO, QKV), BF16),
            dma((HEADS,)),
            dma((HEADS,)),
            dma,
            dma,
            pltpu.VMEM((MODEL_WIDTH, MIX), BF16),
            pltpu.VMEM((MODEL_WIDTH, SMALL), BF16),
            dma((2,)),
        ] + buffers,
        compiler_params=pltpu.CompilerParams(
            collective_id=2, has_side_effects=True, vmem_limit_bytes=60 * 2**20
        ),
        name="mixer_backward",
    )(*operands, *more)


TILE = 256
HANDS = 32
OWN = FF // HANDS
GROUP_ROWS = 4 * OWN


def mlp_kernel(
    full, tokens, cotangent, gated, gains,
    output, grad_mid, grad_gated, grad_gain, grads,
    out_w, up_w, packed, wide, down_w, hidden, normed, total, grad_normed,
    normed_t, gated_t, acted_t, up_stage, stage, load_sem, up_sem, store_sem, stage_sem,
):
    def load(number):
        columns, target = (
            (pl.ds(AT_OUT, MODEL_WIDTH), out_w),
            (pl.ds(AT_DOWN, FF), packed),
        )[number]
        return pltpu.make_async_copy(full.at[:, columns], target, load_sem.at[number])

    def load_up(tile, side):
        begin = pl.multiple_of(side * FF + tile * TILE, TILE)
        source = full.at[:, pl.ds(pl.multiple_of(AT_UP + begin, TILE), TILE)]
        return pltpu.make_async_copy(source, up_w.at[:, pl.ds(begin, TILE)], up_sem.at[side, tile])

    load(1).start()
    load(0).start()

    def start_up(tile, _):
        load_up(tile, 0).start()
        load_up(tile, 1).start()
        return 0

    lax.fori_loop(0, FF // TILE, start_up, 0)
    load(1).wait()

    def unpack(hand, _):
        for half in range(2):
            rows = pl.ds(pl.multiple_of((hand * 2 + half) * PIECE, PIECE), PIECE)
            piece = packed[rows, :].astype(F32)
            for lane in range(2):
                for step in range(11):
                    source = (lane * 11 + step) * 128
                    target = pl.ds(pl.multiple_of(hand * OWN + step * 8, 8), 8)
                    for top in range(2):
                        column = (4 * half + 2 * top + lane) * 128
                        wide[target, column : column + 128] = piece[top * 8 : top * 8 + 8, source : source + 128]
        return 0

    lax.fori_loop(0, HANDS, unpack, 0)

    def narrow(tile, _):
        rows = pl.ds(pl.multiple_of(tile * TILE, TILE), TILE)
        down_w[rows, :] = low(wide[rows, :])
        return 0

    lax.fori_loop(0, FF // TILE, narrow, 0)
    load(0).wait()
    gated_t[...] = low(gated[...].astype(F32).T)
    middle = tokens[...].astype(F32) + nn(gated[...], out_w[...])
    hidden[...] = middle
    inverse = lax.rsqrt(jnp.mean(middle * middle, axis=-1, keepdims=True) + NEAR_ZERO)
    value = middle * inverse * gains[1:2, :]
    normed[...] = low(value)
    normed_t[...] = low(value.T)
    total[...] = jnp.zeros_like(total)
    grad_normed[...] = jnp.zeros_like(grad_normed)

    def store_up(tile, slot, side):
        begin = pl.multiple_of(MODEL_WIDTH + side * FF + tile * TILE, TILE)
        return pltpu.make_async_copy(up_stage.at[slot, side], grads.at[:, pl.ds(begin, TILE)], store_sem.at[slot, side])

    def tile_step(tile, _):
        slot = lax.rem(tile, 2)
        here = pl.ds(pl.multiple_of(tile * TILE, TILE), TILE)
        there = pl.ds(pl.multiple_of(FF + tile * TILE, TILE), TILE)
        load_up(tile, 0).wait()
        load_up(tile, 1).wait()

        @pl.when(tile >= 2)
        def _():
            store_up(tile - 2, slot, 0).wait()
            store_up(tile - 2, slot, 1).wait()

        gate = nn(normed[...], up_w[:, here])
        up = nn(normed[...], up_w[:, there])
        grad = nt(cotangent[...], down_w[here, :])
        sigma = jax.nn.sigmoid(gate)
        soft = gate * sigma
        acted = soft * up
        acted_low = low(acted)
        acted_t[here, :] = low(acted.T)
        total[...] += nn(acted_low, down_w[here, :])
        grad_gate = low(grad * up * (sigma * (1.0 + gate * (1.0 - sigma))))
        grad_up = low(grad * soft)
        grad_normed[...] += nt(grad_gate, up_w[:, here]) + nt(grad_up, up_w[:, there])
        up_stage[slot, 0] = low(nn(normed_t[...], grad_gate))
        up_stage[slot, 1] = low(nn(normed_t[...], grad_up))
        store_up(tile, slot, 0).start()
        store_up(tile, slot, 1).start()
        return 0

    tiles = FF // TILE
    lax.fori_loop(0, tiles, tile_step, 0)
    middle = hidden[...]
    output[...] = low(middle + total[...])
    inverse = lax.rsqrt(jnp.mean(middle * middle, axis=-1, keepdims=True) + NEAR_ZERO)
    grad = grad_normed[...]
    grad_gain[...] = jnp.sum(grad * middle * inverse, axis=0, keepdims=True)
    scaled = grad * gains[1:2, :]
    mean = jnp.mean(scaled * middle, axis=-1, keepdims=True)
    grad = cotangent[...].astype(F32) + inverse * scaled - middle * (inverse * inverse * inverse * mean)
    grad_mid[...] = grad
    grad_low = low(grad)
    grad_gated[...] = nt(grad_low, out_w[...])
    for last in range(2):
        tile = tiles - 2 + last
        for side in range(2):
            store_up(tile, tile % 2, side).wait()

    def store_out(tile):
        slot, side = divmod(tile, 2)
        columns = pl.ds(tile * TILE, TILE)
        return pltpu.make_async_copy(up_stage.at[slot, side], grads.at[:, columns], store_sem.at[slot, side])

    for tile in range(MODEL_WIDTH // TILE):
        slot, side = divmod(tile, 2)
        up_stage[slot, side] = low(nn(gated_t[...], grad_low[:, tile * TILE : (tile + 1) * TILE]))
        store_out(tile).start()

    def store_down(group, slot):
        rows = pl.ds(pl.multiple_of(group * 128, 128), 128)
        target = grads.at[rows, pl.ds(MODEL_WIDTH + 2 * FF, FF)]
        return pltpu.make_async_copy(stage.at[slot], target, stage_sem.at[slot])

    def down_step(group, _):
        slot = lax.rem(group, 2)

        @pl.when(group >= 2)
        def _():
            store_down(group - 2, slot).wait()

        rows = pl.ds(pl.multiple_of(group * GROUP_ROWS, GROUP_ROWS), GROUP_ROWS)
        wide[pl.ds(0, GROUP_ROWS), :] = nn(acted_t[rows, :], cotangent[...])
        for hand in range(4):
            for half in range(2):
                for lane in range(2):
                    for step in range(11):
                        rows = slice(hand * OWN + step * 8, hand * OWN + step * 8 + 8)
                        first = (4 * half + lane) * 128
                        second = (4 * half + 2 + lane) * 128
                        pair = jnp.concatenate(
                            [wide[rows, first : first + 128], wide[rows, second : second + 128]], axis=0
                        )
                        target = (lane * 11 + step) * 128
                        begin = (hand * 2 + half) * PIECE
                        stage[slot, begin : begin + PIECE, target : target + 128] = low(pair)
        store_down(group, slot).start()
        return 0

    groups = HANDS // 4
    lax.fori_loop(0, groups, down_step, 0)
    for group in (groups - 2, groups - 1):
        store_down(group, group % 2).wait()
    for tile in range(MODEL_WIDTH // TILE):
        store_out(tile).wait()


def mlp(full, tokens, cotangent, gated, gains):
    vmem, anywhere = pl.BlockSpec(memory_space=pltpu.VMEM), pl.BlockSpec(memory_space=pl.ANY)
    dma = pltpu.SemaphoreType.DMA
    shape = jax.ShapeDtypeStruct
    return pl.pallas_call(
        mlp_kernel,
        out_shape=[
            shape((ALL, MODEL_WIDTH), BF16),
            shape((ALL, MODEL_WIDTH), F32),
            shape((ALL, MODEL_WIDTH), F32),
            shape((1, MODEL_WIDTH), F32),
            shape((MODEL_WIDTH, PACK - AT_OUT), BF16),
        ],
        in_specs=[anywhere] + [vmem] * 4,
        out_specs=[vmem] * 4 + [anywhere],
        scratch_shapes=[
            pltpu.VMEM((MODEL_WIDTH, MODEL_WIDTH), BF16),
            pltpu.VMEM((MODEL_WIDTH, 2 * FF), BF16),
            pltpu.VMEM((MODEL_WIDTH, FF), BF16),
            pltpu.VMEM((FF, MODEL_WIDTH), F32),
            pltpu.VMEM((FF, MODEL_WIDTH), BF16),
            pltpu.VMEM((ALL, MODEL_WIDTH), F32),
            pltpu.VMEM((ALL, MODEL_WIDTH), BF16),
            pltpu.VMEM((ALL, MODEL_WIDTH), F32),
            pltpu.VMEM((ALL, MODEL_WIDTH), F32),
            pltpu.VMEM((MODEL_WIDTH, ALL), BF16),
            pltpu.VMEM((MODEL_WIDTH, ALL), BF16),
            pltpu.VMEM((FF, ALL), BF16),
            pltpu.VMEM((2, 2, MODEL_WIDTH, TILE), BF16),
            pltpu.VMEM((2, 128, FF), BF16),
            dma((2,)),
            dma((2, FF // TILE)),
            dma((2, 2)),
            dma((2,)),
        ],
        compiler_params=pltpu.CompilerParams(vmem_limit_bytes=60 * 2**20),
        name="mlp",
    )(full, tokens, cotangent, gated, gains)


def mix_grad_kernel(
    normed, grad_project, grad_logits, extra, grad_head,
    mix_sum, small_sum, head_sum,
    grads, normed_t, parts, by_level, part_sem, level_sem, head_sends, *routes,
):
    levels = lax.axis_size("seq") // 2
    at = Place(levels)
    at.greet(0)
    sender = Sender(head_sends)

    def exchange(number, value, row, spot):
        parts[2 * number] = value
        device = {"dp": row, "seq": spot}
        sender.start(None, parts.at[2 * number], parts.at[2 * number + 1], device, part_sem.at[number])
        return lambda: sender.arrived(None, parts.at[2 * number + 1], device, part_sem.at[number])

    pending = exchange(0, grad_head[...], at.row, at.sibling)
    normed_t[...] = low(normed[...].astype(F32).T)

    for tile in range(MIX // WIDE):
        columns = pl.ds(tile * WIDE, WIDE)
        grads[:, columns] = low(nn(normed_t[...], grad_project[:, columns]))
    grads[:, pl.ds(AT_SMALL, SMALL)] = low(nn(normed_t[...], grad_logits[...]) + extra[...])
    sums = scatter_steps(at, CHUNK_MIX, grads, (mix_sum, small_sum), *routes)
    until(sums, "started")
    for number, (row, spot) in enumerate(((at.near, at.spot), (at.far, at.spot))):
        advance(sums, 4)
        pending()
        value = parts[2 * number] + parts[2 * number + 1]
        pending = exchange(number + 1, value, row, spot)
    advance(sums, 4)
    pending()
    by_level[at.level] = parts[4] + parts[5]
    here = {"dp": at.near, "seq": at.spot}

    def send(condition, up, source):
        device = {"dp": at.row, "seq": at.spot + 2 if up else at.spot - 2}
        sender.start(condition, by_level.at[source], by_level.at[source], device, level_sem.at[source])

    send(at.above, True, at.level)
    send(at.below, False, at.level)
    for step in range(1, levels):
        advance(sums, 4)
        for condition, source, up, more in (
            (at.level - step >= 0, at.level - step, True, at.above),
            (at.level + step < levels, at.level + step, False, at.below),
        ):
            sender.arrived(condition, by_level.at[source], here, level_sem.at[source])
            if step < levels - 1:
                send(condition & more, up, source)
    until(sums, "end")
    value = by_level[0]
    for level in range(1, levels):
        value = value + by_level[level]
    head_sum[...] = jnp.broadcast_to(jnp.sum(value, axis=0, keepdims=True), value.shape)
    sender.drain()


def mix_grad(normed, grad_project, grad_logits, extra, grad_head):
    vmem = pl.BlockSpec(memory_space=pltpu.VMEM)
    dma = pltpu.SemaphoreType.DMA
    shape = jax.ShapeDtypeStruct
    levels = lax.axis_size("seq") // 2
    return pl.pallas_call(
        mix_grad_kernel,
        out_shape=[
            shape((2 * PIECE, MIX), F32),
            shape((2 * PIECE, SMALL), F32),
            shape((8, HEAD_SIZE), F32),
        ],
        in_specs=[vmem] * 5,
        out_specs=[vmem] * 3,
        scratch_shapes=[
            pltpu.VMEM((MODEL_WIDTH, AT_OUT), BF16),
            pltpu.VMEM((MODEL_WIDTH, ALL), BF16),
            pltpu.VMEM((6, 8, HEAD_SIZE), F32),
            pltpu.VMEM((levels, 8, HEAD_SIZE), F32),
            dma((3,)),
            dma((levels,)),
            dma((3 + 2 * levels,)),
        ] + scatter_buffers(levels, AT_OUT, False),
        compiler_params=pltpu.CompilerParams(
            collective_id=3, has_side_effects=True, vmem_limit_bytes=56 * 2**20
        ),
        name="mix_grad",
    )(normed, grad_project, grad_logits, extra, grad_head)


def pack_down(part):
    lead = part.shape[:-2]
    tiles = part.reshape(lead + (11, 8, 4, 2, 128))
    n = len(lead)
    moved = tiles.transpose(tuple(range(n)) + (n + 2, n + 1, n + 3, n, n + 4))
    return moved.reshape(lead + (2 * PIECE, FF))


def unpack_down(part):
    lead = part.shape[:-2]
    tiles = part.reshape(lead + (4, 8, 2, 11, 128))
    n = len(lead)
    moved = tiles.transpose(tuple(range(n)) + (n + 3, n + 1, n, n + 2, n + 4))
    return moved.reshape(lead + (OWN, MODEL_WIDTH))


def pack_taps(conv):
    taps = conv.reshape(KW, -1, 3, 2 * PIECE)
    return taps.transpose(1, 3, 0, 2).reshape(-1, 3 * KW)


def unpack_taps(taps):
    taps = taps.reshape(-1, 2 * PIECE, KW, 3)
    return taps.transpose(2, 0, 3, 1).reshape(KW, -1)


def pack_small(mixer, mlp_part, beta, conv):
    parts = jnp.concatenate([mixer[:, None], mlp_part[:, None], beta, pack_taps(conv)], axis=1)
    return jnp.pad(parts, ((0, 0), (0, SMALL - parts.shape[1])))


def shards(
    tokens, cotangent, starts, mixer_gain, mix_weight, conv_weight, beta_weight, head_gain, out_weight, mlp_gain,
    upgate_weight, down_weight,
):
    rows, block, width = tokens.shape
    share = mix_weight.shape[1]
    both = ("dp", "seq")
    routed = lax.axis_size("dp") == 4 and lax.axis_size("seq") % 2 == 0 and share == 2 * PIECE
    parts = [mixer_gain[0], mlp_gain[0], beta_weight[0], conv_weight[0].T, mix_weight[0], out_weight[0], upgate_weight[0], down_weight[0]]
    if not routed:
        parts = [lax.all_gather(part, both, axis=0, tiled=True) for part in parts]
    mixer_w, mlp_w, beta_w, conv_w, mix_w, out_w, up_w, down_w = parts
    small_w = pack_small(mixer_w, mlp_w, beta_w, conv_w.T)
    down_w = pack_down(down_w.reshape(-1, OWN, width)).reshape(-1, FF)
    weights = [mix_w, small_w, out_w, up_w, down_w]
    if not routed:
        weights = [jnp.concatenate(weights, axis=1)]

    flat = tokens.reshape(rows * block, width)
    flat_grad = cotangent.reshape(rows * block, width)
    head_f = head_gain.astype(F32)
    full, normed, pre, raw, beta, solved, solved_w, fresh, state, power, outputs, gated, conv, gains = mixer_forward(
        starts, flat, head_f, weights
    )
    output, grad_mid, grad_gated, grad_mlp, grads = mlp(full, flat, flat_grad, gated, gains)
    operands = [
        starts, grad_gated, grad_mid, flat, gains, full, conv, head_f,
        pre, raw, beta, solved, solved_w, fresh, state, power, outputs,
    ]
    results = mixer_backward(operands, grads if routed else None)
    grad_hidden, grad_project, grad_logits, grad_conv, grad_head, grad_mixer = results[:6]
    extra = [grad_mixer.T, grad_mlp.T, jnp.zeros((width, HEADS), F32), pack_taps(grad_conv)]
    extra = jnp.pad(jnp.concatenate(extra, axis=1), ((0, 0), (0, SMALL - CONV_AT - 3 * KW)))
    if routed:
        out_mine, up_mine, down_mine = results[6:]
        mix_mine, small_mine, head_mine = mix_grad(normed, grad_project, grad_logits, extra, grad_head)
        head_mine = head_mine[:1]
        down_mine = unpack_down(down_mine)
        mixer_mine, mlp_mine = small_mine[:, 0], small_mine[:, 1]
        beta_mine = small_mine[:, BETA_AT:CONV_AT]
        conv_mine = unpack_taps(small_mine[:, CONV_AT : CONV_AT + 3 * KW])
    else:
        whole_mix = lax.dot_general(normed, grad_project, (((0,), (0,)), ((), ())), preferred_element_type=F32)
        whole_beta = lax.dot_general(normed, grad_logits, (((0,), (0,)), ((), ())), preferred_element_type=F32)
        whole_down = unpack_down(grads[:, MODEL_WIDTH + 2 * FF :].reshape(-1, 2 * PIECE, FF)).reshape(FF, width)
        listed = [
            whole_mix,
            grads[:, :MODEL_WIDTH],
            grads[:, MODEL_WIDTH : MODEL_WIDTH + 2 * FF],
            whole_down,
            grad_mixer[0],
            grad_mlp[0],
            whole_beta[:, BETA_AT:CONV_AT],
            grad_conv.T,
        ]
        listed = [
            lax.psum_scatter(part.astype(F32), both, scatter_dimension=0, tiled=True) for part in listed
        ]
        mix_mine, out_mine, up_mine, down_mine, mixer_mine, mlp_mine, beta_mine, conv_mine = listed
        conv_mine = conv_mine.T
        head_mine = lax.psum(jnp.sum(grad_head, axis=0, keepdims=True), both)
    return (
        output.reshape(rows, block, width),
        grad_hidden.reshape(rows, block, width),
        mixer_mine[None],
        mix_mine[None],
        conv_mine[None],
        beta_mine[None],
        head_mine,
        out_mine[None],
        mlp_mine[None],
        up_mine[None],
        down_mine[None],
    )


def solution(mesh):
    both = ("dp", "seq")
    in_specs = (
        P("dp", "seq", None),
        P("dp", "seq", None),
        P("dp", None),
        P(None, both),
        P(None, both, None),
        P(None, None, both),
        P(None, both, None),
        P(),
        P(None, both, None),
        P(None, both),
        P(None, both, None),
        P(None, both, None),
    )
    out_specs = (
        P("dp", "seq", None),
        P("dp", "seq", None),
        P(None, both),
        P(None, both, None),
        P(None, None, both),
        P(None, both, None),
        P(),
        P(None, both, None),
        P(None, both),
        P(None, both, None),
        P(None, both, None),
    )
    return jax.shard_map(shards, mesh=mesh, in_specs=in_specs, out_specs=out_specs, check_vma=False)
```

```python
import functools

import jax
import jax.numpy as jnp
from jax import lax
from jax.experimental import pallas as pl
from jax.experimental.pallas import tpu as pltpu
from jax.sharding import PartitionSpec as P

MODEL_WIDTH = 1024
HEADS = 8
HEAD_SIZE = 128
FF = 2816
KW = 4
PACKED = 4

MESH = pl.DeviceIdType.MESH
F32 = jnp.float32
BF16 = jnp.bfloat16
TOKENS = 128
ROWS = 2
ALL = ROWS * TOKENS
HALO = 8
NEAR_ZERO = 1e-06
HEAD_ZERO = 1e-05
MIX = 4 * MODEL_WIDTH
QKV = 3 * MODEL_WIDTH
SMALL = 128
BETA_AT = 2
CONV_AT = 10
AT_SMALL = MIX
AT_OUT = AT_SMALL + SMALL
AT_UP = AT_OUT + MODEL_WIDTH
AT_DOWN = AT_UP + 2 * FF
PACK = AT_DOWN + FF
HALF_REST = (PACK - AT_OUT) // 2
CHUNK_MIX = AT_OUT // 3
PIECE = 16
SLOTS = 2
WINDOW = 8
LAG = 2
EDGE = 16
WIDE = 512
GROUP = 2
AT_PREPARE = 2
AT_CHAIN = (5, 2)
AT_FINISH = (1, 2)
AT_CONV = (0, 0)
AT_NORMED = (2, 2)
AT_END = (1, 2, 3)


def nn(a, b):
    return lax.dot_general(a, b, (((1,), (0,)), ((), ())), preferred_element_type=F32)


def nt(a, b):
    return lax.dot_general(a, b, (((1,), (1,)), ((), ())), preferred_element_type=F32)


def tn(a, b):
    return lax.dot_general(a, b, (((0,), (0,)), ((), ())), preferred_element_type=F32)


def low(value):
    return value.astype(BF16)


def when(condition, action):
    if condition is None:
        action()
    else:
        pl.when(condition)(action)


class Place:
    def __init__(self, levels):
        self.levels = levels
        self.row, self.spot = lax.axis_index("dp"), lax.axis_index("seq")
        self.level, self.core = self.spot // 2, lax.rem(self.spot, 2)
        self.near = self.row + 1 - 2 * lax.rem(self.row, 2)
        self.far = self.row + 2 - 4 * (self.row // 2)
        self.first = self.near * (1 - self.core) + self.far * self.core
        self.second = self.far * (1 - self.core) + self.near * self.core
        self.both = 3 - self.row
        self.above, self.below = self.level + 1 < levels, self.level >= 1
        self.sibling = self.spot + 1 - 2 * self.core

    def greet(self, chain):
        barrier = pltpu.get_barrier_semaphore()
        levels, level, core = self.levels, self.level, self.core

        def signal(row, spot):
            pl.semaphore_signal(barrier, inc=1, device_id={"dp": row, "seq": spot}, device_id_type=MESH)

        signal(self.first, self.spot)
        signal(self.second, self.spot)
        signal(self.row, self.sibling)
        pl.when(self.above)(lambda: signal(self.row, self.spot + 2))
        pl.when(self.below)(lambda: signal(self.row, self.spot - 2))
        has_above = (2 * levels - 2 - level) // levels
        has_below = (level + levels - 1) // levels
        peers = 3 + has_above + has_below
        if chain > 0:
            pl.when(self.below & (core == 0))(lambda: signal(self.row, self.spot - 1))
            peers = peers + has_above * core
        if chain < 0:
            pl.when(self.above & (core == 1))(lambda: signal(self.row, self.spot + 1))
            peers = peers + has_below * (1 - core)
        pl.semaphore_wait(barrier, peers)

    def rows_of(self, owner, spot, half):
        return pl.ds(pl.multiple_of(((owner * 2 * self.levels + spot) * 2 + half) * PIECE, PIECE), PIECE)


class Sender:
    def __init__(self, semaphores):
        self.semaphores, self.used, self.pending = semaphores, 0, []

    def start(self, condition, source, target, device, arrival):
        copy = pltpu.make_async_remote_copy(
            src_ref=source, dst_ref=target, send_sem=self.semaphores.at[self.used], recv_sem=arrival,
            device_id=device, device_id_type=MESH,
        )
        self.used += 1
        when(condition, copy.start)
        self.pending.append((condition, copy))

    def arrived(self, condition, target, device, arrival):
        copy = pltpu.make_async_remote_copy(
            src_ref=target, dst_ref=target, send_sem=self.semaphores.at[0], recv_sem=arrival,
            device_id=device, device_id_type=MESH,
        )
        when(condition, copy.wait_recv)

    def drain(self):
        for condition, copy in self.pending:
            when(condition, copy.wait_send)


def advance(steps, count=1):
    for _ in range(count):
        next(steps, None)


def both_advance(counts, *listed):
    for steps, count in zip(listed, counts):
        advance(steps, count)


def until(steps, mark):
    for found in steps:
        if found == mark:
            return


def gather_semaphores(levels):
    dma = pltpu.SemaphoreType.DMA
    return [dma((2, 2, levels)), dma((2, levels)), dma((2, 2, levels)), dma((2, 4, levels)), dma((8 + 34 * levels,))]


def gather_steps(at, full, columns, by_level, by_first, by_second, by_core, sends):
    levels, row, spot, level, core = at.levels, at.row, at.spot, at.level, at.core
    first, second, both, above, below = at.first, at.second, at.both, at.above, at.below
    sender = Sender(sends)
    here = {"dp": first, "seq": spot}

    def piece(half, owner, owner_level):
        return full.at[at.rows_of(owner, owner_level * 2 + core, half), columns]

    def send(condition, half, owner, owner_level, device, arrival):
        target = piece(half, owner, owner_level)
        sender.start(condition, target, target, device, arrival)

    def along(condition, up, half, side, owner, owner_level):
        device = {"dp": row, "seq": spot + 2 if up else spot - 2}
        send(condition, half, owner, owner_level, device, by_level.at[half, side, owner_level])

    def to_first(condition, half, owner_level):
        send(condition, half, row, owner_level, here, by_first.at[half, owner_level])

    def to_second(condition, half, side, owner, owner_level):
        device = {"dp": second, "seq": spot}
        send(condition, half, owner, owner_level, device, by_second.at[half, side, owner_level])

    def to_core(condition, half, owner, owner_level):
        device = {"dp": row, "seq": at.sibling}
        send(condition, half, owner, owner_level, device, by_core.at[half, owner, owner_level])

    def arrived(condition, half, owner, owner_level, arrival):
        sender.arrived(condition, piece(half, owner, owner_level), here, arrival)

    to_first(None, 1, level)
    along(above, True, 0, 0, row, level)
    along(below, False, 0, 0, row, level)
    to_second(None, 0, 0, row, level)
    to_first(None, 0, level)
    to_second(None, 1, 0, row, level)
    along(above, True, 1, 0, row, level)
    along(below, False, 1, 0, row, level)
    to_core(None, 0, row, level)
    to_core(None, 1, row, level)
    yield "started"
    arrived(None, 1, first, level, by_first.at[1, level])
    along(above, True, 1, 1, first, level)
    along(below, False, 1, 1, first, level)
    to_second(None, 1, 1, first, level)
    to_core(None, 1, first, level)
    yield "step"
    arrived(None, 0, first, level, by_first.at[0, level])
    to_second(None, 0, 1, first, level)
    to_core(None, 0, first, level)
    yield "step"

    def from_second(condition, owner_level, half):
        for side, owner in ((0, second), (1, both)):
            arrived(condition, half, owner, owner_level, by_second.at[half, side, owner_level])
            to_core(condition, half, owner, owner_level)

    waiting = [(None, level)]
    for step in range(1, levels):
        ways = ((level - step >= 0, level - step, True), (level + step < levels, level + step, False))

        def onward(up, step=step):
            if up:
                return (level - step >= 0) & above
            return (level + step < levels) & below

        for condition, source, up in ways:
            arrived(condition, 0, row, source, by_level.at[0, 0, source])
            if step < levels - 1:
                along(onward(up), up, 0, 0, row, source)
            to_first(condition, 0, source)
            to_second(condition, 0, 0, row, source)
            to_core(condition, 0, row, source)
        yield "step"
        for side, owner in ((0, row), (1, first)):
            for condition, source, up in ways:
                arrived(condition, 1, owner, source, by_level.at[1, side, source])
                if step < levels - 1:
                    along(onward(up), up, 1, side, owner, source)
                to_second(condition, 1, side, owner, source)
                to_core(condition, 1, owner, source)
            yield "step"
        for condition, source, up in ways:
            arrived(condition, 0, first, source, by_first.at[0, source])
            to_second(condition, 0, 1, first, source)
            to_core(condition, 0, first, source)
        yield "step"
        if step == levels - 1:
            yield "leveled"
        for half in range(2):
            for condition, source in waiting:
                from_second(condition, source, half)
            yield "step"
        waiting = [(condition, source) for condition, source, _ in ways]
    for half in range(2):
        for condition, source in waiting:
            from_second(condition, source, half)
        yield "step"
    yield "issued"
    for half in range(2):
        for owner in range(4):
            for source in range(levels):
                target = full.at[at.rows_of(owner, source * 2 + 1 - core, half), columns]
                sender.arrived(None, target, here, by_core.at[half, owner, source])
    yield "arrived"
    sender.drain()


def scatter_buffers(levels, width, staged):
    dma = pltpu.SemaphoreType.DMA
    buffers = [
        pltpu.VMEM((2, 4, levels, PIECE, width), BF16),
        pltpu.VMEM((2, 2, levels, PIECE, width), BF16),
        pltpu.VMEM((levels + 1, PIECE, width), BF16),
        pltpu.VMEM((3, levels + 1, PIECE, width), BF16),
        dma((2, 4, levels)),
        dma((2, 2, levels)),
        dma((levels + 1,)),
        dma((3, levels + 1)),
        dma((8 + 44 * levels,)),
    ]
    if staged:
        buffers += [pltpu.VMEM((SLOTS, PIECE, width), BF16), dma((SLOTS,))]
    return buffers


def scatter_steps(
    at, columns, chunk, grads, targets, total, by_second, by_first, by_level,
    core_sem, second_sem, first_sem, level_sem, sends, staged=None, load_sem=None,
):
    levels, row, spot, level, core = at.levels, at.row, at.spot, at.level, at.core
    first, second, both, above, below = at.first, at.second, at.both, at.above, at.below
    sender = Sender(sends)
    here = {"dp": first, "seq": spot}
    begin, width = columns
    columns = pl.ds(begin, width)
    ways = [(far, up) for far in range(levels - 1, 0, -1) for up in (True, False)] + [(0, True)]

    def there(way):
        far, up = way
        if far == 0:
            return None, level
        return (level + far < levels, level + far) if up else (level - far >= 0, level - far)

    def add(target, other):
        def body(step, _):
            part = pl.ds(pl.multiple_of(step * chunk, chunk), chunk)
            target[:, part] = target[:, part] + other[:, part]
            return 0

        lax.fori_loop(0, width // chunk, body, 0)

    def arrived(target, arrival):
        sender.arrived(None, target, here, arrival)

    def listing(one, two):
        out = []
        for turn in range(len(ways) + LAG):
            if turn < len(ways):
                out += [(True, ways[turn], half, side, owner) for half in (1, 0) for side, owner in ((0, one), (1, both))]
            if turn >= LAG:
                out += [(False, ways[turn - LAG], half, side, owner) for half in (1, 0) for side, owner in ((0, row), (1, two))]
        return out

    listed = listing(second, first)
    given = listing(first, second)

    def to_core(number):
        _, way, half, _, owner = given[number]
        condition, end = there(way)
        device = {"dp": row, "seq": at.sibling}
        source = grads.at[at.rows_of(owner, end * 2 + 1 - core, half), columns]
        sender.start(condition, source, total.at[half, owner, end], device, core_sem.at[half, owner, end])

    for number in range(WINDOW):
        to_core(number)

    def load(number):
        _, way, half, _, owner = listed[number]
        slot = number % SLOTS
        source = grads.at[at.rows_of(owner, there(way)[1] * 2 + core, half), columns]
        return pltpu.make_async_copy(source, staged.at[slot], load_sem.at[slot])

    def start_load(number):
        if staged is not None and number < len(listed):
            when(there(listed[number][1])[0], lambda: load(number).start())

    for slot in range(SLOTS):
        start_load(slot)
    yield "started"

    def take_listed(number):
        leaves, way, half, side, owner = listed[number]
        if number + WINDOW < len(listed):
            to_core(number + WINDOW)
        condition, end = there(way)
        sums = total.at[half, owner, end]

        def take():
            if staged is not None:
                load(number).wait()
            arrived(sums, core_sem.at[half, owner, end])
            if staged is None:
                add(sums, grads.at[at.rows_of(owner, end * 2 + core, half), columns])
            else:
                add(sums, staged.at[number % SLOTS])

        when(condition, take)
        start_load(number + SLOTS)
        if leaves:
            device = {"dp": second, "seq": spot}
            sender.start(condition, sums, by_second.at[half, side, end], device, second_sem.at[half, side, end])

    for number in range(len(listed)):
        take_listed(number)
        if number % 4 == 3:
            yield "step"
    yield "sent"

    def along(half, side, owner, way):
        far, up = way
        if far == 0:
            return
        condition, end = there(way)
        sums = total.at[half, owner, end]
        place = 0 if half == 0 else 1 + side
        if far < levels - 1:

            def take():
                arrived(by_level.at[place, end], level_sem.at[place, end])
                add(sums, by_level.at[place, end])

            pl.when(condition & (below if up else above))(take)
        slot = end if up or far > 1 else levels
        device = {"dp": row, "seq": spot + 2 if up else spot - 2}
        sender.start(condition, sums, by_level.at[place, slot], device, level_sem.at[place, slot])

    def from_second(half, side, owner, way):
        condition, end = there(way)

        def take():
            arrived(by_second.at[half, side, end], second_sem.at[half, side, end])
            add(total.at[half, owner, end], by_second.at[half, side, end])

        when(condition, take)

    def from_first(way):
        condition, end = there(way)

        def take():
            arrived(by_first.at[end], first_sem.at[end])
            add(total.at[0, row, end], by_first.at[end])

        when(condition, take)
        along(0, 0, row, way)

    previous = None
    for way in ways:
        condition, end = there(way)
        for side, owner in ((0, row), (1, first)):
            from_second(1, side, owner, way)
            along(1, side, owner, way)
        yield "step"
        from_second(0, 1, first, way)
        sender.start(condition, total.at[0, first, end], by_first.at[end], here, first_sem.at[end])
        from_second(0, 0, row, way)
        yield "step"
        if previous is not None:
            from_first(previous)
            yield "step"
        previous = way
    from_first(previous)
    yield "step"

    def collect(half, side, owner):
        sums = total.at[half, owner, level]
        place = 0 if half == 0 else 1 + side

        def take(slot):
            arrived(by_level.at[place, slot], level_sem.at[place, slot])
            add(sums, by_level.at[place, slot])

        pl.when(below)(lambda: take(level))
        pl.when(above)(lambda: take(levels))

    def final(half, *parts):
        rows, at_part = pl.ds(half * PIECE, PIECE), 0
        for target, start, length in targets:
            part = pl.ds(at_part, length)
            value = parts[0][:, part].astype(F32)
            for other in parts[1:]:
                value = value + other[:, part].astype(F32)
            target[rows, pl.ds(start, length)] = value
            at_part += length

    collect(1, 1, first)
    sender.start(None, total.at[1, first, level], by_first.at[levels], here, first_sem.at[levels])
    yield "step"
    collect(1, 0, row)
    yield "step"
    collect(0, 0, row)
    final(0, total.at[0, row, level])
    yield "step"
    arrived(by_first.at[levels], first_sem.at[levels])
    final(1, total.at[1, row, level], by_first.at[levels])
    sender.drain()


def segment(starts, row, places):
    total = jnp.zeros_like(places)
    for k in range(PACKED):
        begin = starts[row, k]
        total = total + jnp.where((begin > 0) & (places >= begin), 1, 0)
    return total


def row_scalars(starts, row, first):
    before = jnp.int32(0)
    last = jnp.int32(0)
    for k in range(PACKED):
        begin = starts[row, k]
        before = before + jnp.where((begin > 0) & (begin <= first - 1), 1, 0)
        last = last + jnp.where((begin > 0) & (begin <= first + TOKENS - 1), 1, 0)
    return before, last


def fill_masks(starts, first, carry_in, carry_out, taps, within, below):
    places = first + lax.broadcasted_iota(jnp.int32, (TOKENS, HEAD_SIZE), 0)
    side = lax.broadcasted_iota(jnp.int32, (TOKENS, TOKENS), 0)
    across = lax.broadcasted_iota(jnp.int32, (TOKENS, TOKENS), 1)
    within[...] = jnp.zeros_like(within)
    below[...] = jnp.zeros_like(below)
    for row in range(ROWS):
        span = pl.ds(row * TOKENS, TOKENS)
        mine = segment(starts, row, places)
        before, last = row_scalars(starts, row, first)
        carry_in[span, :] = (mine == before).astype(F32)
        carry_out[span, :] = (mine == last).astype(F32)
        for shift in range(1, KW):
            there = places - shift
            same = (segment(starts, row, there) == mine) & (there >= 0)
            taps[shift - 1, span, :] = same.astype(F32)
        same = segment(starts, row, first + side) == segment(starts, row, first + across)
        within[span, span] = (same & (side >= across)).astype(F32)
        below[span, span] = (same & (side > across)).astype(F32)


def padded(main, halo):
    return jnp.concatenate([halo, main], axis=0)


def unit_scale(values):
    return lax.rsqrt(jnp.sum(values * values, axis=-1, keepdims=True) + NEAR_ZERO)


def lane_of(values, lane):
    lanes = lax.broadcasted_iota(jnp.int32, values.shape, 1)
    return jnp.sum(jnp.where(lanes == lane, values, 0.0), axis=-1, keepdims=True)


def head_columns(part, head):
    return pl.ds(pl.multiple_of(part * MODEL_WIDTH + head * HEAD_SIZE, HEAD_SIZE), HEAD_SIZE)


def halves(value):
    high = low(value)
    return high, low(value - high.astype(F32))


def gram_of(keys):
    high, rest = halves(keys)
    return nt(high, high) + nt(high, rest) + nt(rest, high)


def per_row(function, *arrays):
    return jnp.concatenate(
        [
            function(row, *[array[row * TOKENS : (row + 1) * TOKENS] for array in arrays])
            for row in range(ROWS)
        ],
        axis=0,
    )


def invert(system, apart):
    eye = jnp.where(apart == 0, 1.0, 0.0)
    solved = eye - jnp.where(apart == 1, system, 0.0)
    size = 2
    while size < TOKENS:
        cross = low(jnp.where((apart >= size) & (apart < 2 * size), system, 0.0))
        rough = low(solved)
        solved = solved - nn(low(nn(rough, cross)), rough)
        size *= 2
    return solved


def kappa_eye(kept):
    side = lax.broadcasted_iota(jnp.int32, (HEAD_SIZE, HEAD_SIZE), 0)
    across = lax.broadcasted_iota(jnp.int32, (HEAD_SIZE, HEAD_SIZE), 1)
    return jnp.where(side == across, 1.0, 0.0) * kept


def tap_moves():
    group = 3 * HEAD_SIZE
    side = lax.broadcasted_iota(jnp.int32, (group, group), 0)
    across = lax.broadcasted_iota(jnp.int32, (group, group), 1)
    third, device, lane = side // HEAD_SIZE, (side % HEAD_SIZE) // 32, side % 32
    return jnp.where(across == device * 96 + third * 32 + lane, 1.0, 0.0).astype(BF16)


def tap_rows(small_rows):
    move = tap_moves()
    wanted = []
    for block in range(MODEL_WIDTH // HEAD_SIZE):
        lanes = slice(block * HEAD_SIZE, (block + 1) * HEAD_SIZE)
        parts = [small_rows[CONV_AT + 3 * j : CONV_AT + 3 * j + 3, lanes] for j in range(KW)]
        source = jnp.concatenate(
            [jnp.concatenate([part[c : c + 1] for c in range(3)], axis=1) for part in parts], axis=0
        )
        wanted.append(nn(low(source), move))
    return wanted


def mixer_forward_kernel(routed, *refs):
    (starts, tokens, head_gain), refs = refs[:3], refs[3:]
    if routed:
        shares, refs = refs[:5], refs[5:]
    (full, normed, pre_low, raw, beta, solved, solved_w, fresh, state, power, outputs, gated, conv, gains), refs = refs[:14], refs[14:]
    (every, carry_in, carry_out, taps, within, below, apart), refs = refs[:7], refs[7:]
    (offset, solved_u, attend, queries, arriving, leaving, send, receive), refs = refs[:8], refs[8:]
    (mix, small, halo, halo_send, halo_receive, load_sem, pre), refs = refs[:7], refs[7:]
    count = lax.axis_size("seq")
    index = lax.axis_index("seq")
    first = index * TOKENS
    rest = iter(())
    if routed:
        keep_sem, routes = refs[0], refs[1:]
        at = Place(count // 2)
        mine = pl.ds(pl.multiple_of((at.row * count + index) * 2 * PIECE, 2 * PIECE), 2 * PIECE)
        kept = []
        begin = 0
        for number, share in enumerate(shares):
            columns = pl.ds(begin, share.shape[-1])
            kept.append(pltpu.make_async_copy(share, full.at[mine, columns], keep_sem.at[number]))
            begin += share.shape[-1]
        for copy in kept:
            copy.start()
        at.greet(1)
    else:
        barrier = pltpu.get_barrier_semaphore()

        @pl.when(index > 0)
        def _():
            pl.semaphore_signal(barrier, inc=1, device_id={"seq": index - 1}, device_id_type=MESH)

        @pl.when(index + 1 < count)
        def _():
            pl.semaphore_wait(barrier, 1)

    def tail(row):
        return pltpu.make_async_remote_copy(
            src_ref=tokens.at[pl.ds((row + 1) * TOKENS - EDGE, EDGE), :], dst_ref=halo.at[pl.ds(row * EDGE, EDGE), :],
            send_sem=halo_send.at[row], recv_sem=halo_receive.at[row], device_id={"seq": index + 1}, device_id_type=MESH,
        )

    @pl.when(index + 1 < count)
    def _():
        for row in range(ROWS):
            tail(row).start()

    if routed:
        kept[0].wait()
        kept[1].wait()
        wanted = gather_steps(at, full, pl.ds(0, AT_OUT), *routes[:5])
        until(wanted, "started")

    @pl.when(index == 0)
    def _():
        arriving[...] = jnp.zeros_like(arriving)
        halo[...] = jnp.zeros_like(halo)

    fill_masks(starts, first, carry_in, carry_out, taps, within, below)
    side = lax.broadcasted_iota(jnp.int32, (ALL, ALL), 0)
    across = lax.broadcasted_iota(jnp.int32, (ALL, ALL), 1)
    apart[...] = jnp.bitwise_xor(side, across)
    if routed:
        until(wanted, "issued")
        for copy in kept[2:]:
            copy.wait()
        rest = gather_steps(at, full, pl.ds(AT_OUT, PACK - AT_OUT), *routes[5:])
        until(rest, "started")
        until(wanted, "arrived")

    def load(number):
        if number < 0:
            return pltpu.make_async_copy(full.at[:, pl.ds(AT_SMALL, SMALL)], small, load_sem.at[MIX // WIDE])
        columns = pl.ds(number * WIDE, WIDE)
        return pltpu.make_async_copy(full.at[:, columns], mix.at[:, columns], load_sem.at[number])

    for number in range(-1, MIX // WIDE):
        load(number).start()
    load(-1).wait()
    small_rows = small[:, pl.ds(0, HEAD_SIZE)].astype(F32).T
    gains[...] = small_rows[:8]
    for block, part in enumerate(tap_rows(small_rows)):
        conv[:, pl.ds(block * 3 * HEAD_SIZE, 3 * HEAD_SIZE)] = part

    def norm(source, target, rows):
        values = source[...].astype(F32)
        scale = lax.rsqrt(jnp.mean(values * values, axis=-1, keepdims=True) + NEAR_ZERO)
        target[rows, :] = low(values * scale * gains[0:1, :])

    norm(tokens, every, pl.ds(0, ALL))

    @pl.when(index > 0)
    def _():
        for row in range(ROWS):
            tail(row).wait_recv()

    norm(halo, every, pl.ds(ALL, ROWS * EDGE))
    normed[...] = low(every[pl.ds(0, ALL), :].astype(F32).T)
    beta[...] = jax.nn.sigmoid(nn(every[pl.ds(0, ALL), :], small[...]))
    for number in range(MIX // WIDE):
        load(number).wait()
        columns = pl.ds(number * WIDE, WIDE)
        wide = nn(every[...], mix[:, columns])
        pre[:, columns] = wide
        pre_low[:, columns] = low(wide)
        if number % 4 == 3:
            advance(rest)

    def convolve(columns):
        weight = conv[:, columns]
        rows = []
        for row in range(ROWS):
            main = pre[pl.ds(row * TOKENS, TOKENS), columns]
            before = pre[pl.ds(ALL + (row + 1) * EDGE - HALO, HALO), columns]
            longer = padded(main, before)
            total = weight[0:1] * main
            for shift in range(1, KW):
                tap = taps[shift - 1, pl.ds(row * TOKENS, TOKENS), :]
                total = total + weight[shift : shift + 1] * longer[HALO - shift : HALO - shift + TOKENS] * tap
            rows.append(total)
        total = jnp.concatenate(rows, axis=0)
        raw[:, columns] = low(total)
        return total * jax.nn.sigmoid(total)

    def local(head):
        active_q = convolve(head_columns(0, head))
        active_k = convolve(head_columns(1, head))
        values = convolve(head_columns(2, head))
        query = active_q * (unit_scale(active_q) * HEAD_SIZE**-0.5)
        key = active_k * unit_scale(active_k)
        strength = lane_of(beta[...], BETA_AT + head)
        columns = head_columns(0, head)
        system = below[...] * (strength * gram_of(key))
        inverse = low(invert(system, apart[...]))
        solved[head] = inverse
        enter = carry_in[...]
        w = low(nn(inverse, low(strength * enter * key)))
        u = nn(inverse, low(strength * values))
        solved_w[:, columns] = w
        solved_u[:, columns] = u
        leave = low(carry_out[...] * key)
        u_low = low(u)
        for row in range(ROWS):
            span = slice(row * TOKENS, (row + 1) * TOKENS)
            before, last = row_scalars(starts, row, first)
            kept = jnp.where(before == last, 1.0, 0.0)
            power[head, row] = low(kappa_eye(kept) - tn(leave[span], w[span]))
            offset[head, row] = tn(leave[span], u_low[span])
        attend[head] = low(within[...] * nt(low(query), low(key)))
        queries[:, columns] = low(enter * query)


    for step in range(HEADS // GROUP):
        for part in range(GROUP):
            local(step * GROUP + part)
        advance(rest, 2)

    def copy(head):
        return pltpu.make_async_remote_copy(
            src_ref=leaving.at[head], dst_ref=arriving.at[head], send_sem=send.at[head], recv_sem=receive.at[head],
            device_id={"seq": index + 1}, device_id_type=MESH,
        )

    def chain(head):
        @pl.when(index > 0)
        def _():
            copy(head).wait_recv()

        @pl.when(index + 1 < count)
        def _():
            for row in range(ROWS):
                leaving[head, row] = low(nn(power[head, row], arriving[head, row]) + offset[head, row])
            copy(head).start()

        columns = head_columns(0, head)
        w, u, query = solved_w[:, columns], solved_u[:, columns], queries[:, columns]
        x = low(u - per_row(lambda row, part: nn(part, arriving[head, row]), w))
        fresh[:, columns] = x
        output = per_row(lambda row, part: nn(part, arriving[head, row]), query) + nn(attend[head], x)
        outputs[:, columns] = output
        scale = lax.rsqrt(jnp.mean(output * output, axis=-1, keepdims=True) + HEAD_ZERO)
        gate = pre[pl.ds(0, ALL), head_columns(3, head)]
        gated[:, columns] = low(output * scale * head_gain[...] * (gate * jax.nn.sigmoid(gate)))

    until(rest, "leveled")
    for head in range(HEADS):
        chain(head)
        if head % 2 == 1:
            advance(rest)
    state[...] = arriving[...]

    @pl.when(index + 1 < count)
    def _():
        for row in range(ROWS):
            tail(row).wait_send()

        def drain(head, _):
            copy(head).wait_send()
            return 0

        lax.fori_loop(0, HEADS, drain, 0)

    until(rest, "end")
    if routed:
        until(wanted, "end")


def mixer_forward(starts, tokens, head_gain, weights):
    routed = len(weights) > 1
    vmem, anywhere = pl.BlockSpec(memory_space=pltpu.VMEM), pl.BlockSpec(memory_space=pl.ANY)
    dma = pltpu.SemaphoreType.DMA
    shape = jax.ShapeDtypeStruct
    states = (HEADS, ROWS, HEAD_SIZE, HEAD_SIZE)
    long = ALL + ROWS * EDGE
    whole = [shape((MODEL_WIDTH, PACK), BF16)] if routed else []
    levels = lax.axis_size("seq") // 2
    routes = [dma((5,))] + gather_semaphores(levels) + gather_semaphores(levels) if routed else []
    results = pl.pallas_call(
        functools.partial(mixer_forward_kernel, routed),
        out_shape=whole + [
            shape((MODEL_WIDTH, ALL), BF16),
            shape((long, MIX), BF16),
            shape((ALL, QKV), BF16),
            shape((ALL, SMALL), F32),
            shape((HEADS, ALL, ALL), BF16),
            shape((ALL, MODEL_WIDTH), BF16),
            shape((ALL, MODEL_WIDTH), BF16),
            shape(states, BF16),
            shape(states, BF16),
            shape((ALL, MODEL_WIDTH), F32),
            shape((ALL, MODEL_WIDTH), BF16),
            shape((KW, QKV), F32),
            shape((8, MODEL_WIDTH), F32),
        ],
        in_specs=[pl.BlockSpec(memory_space=pltpu.SMEM), vmem, vmem] + [anywhere] * len(weights),
        out_specs=[anywhere] * len(whole) + [vmem] * 13,
        scratch_shapes=[
            pltpu.VMEM((long, MODEL_WIDTH), BF16),
            pltpu.VMEM((ALL, HEAD_SIZE), F32),
            pltpu.VMEM((ALL, HEAD_SIZE), F32),
            pltpu.VMEM((KW - 1, ALL, HEAD_SIZE), F32),
            pltpu.VMEM((ALL, ALL), F32),
            pltpu.VMEM((ALL, ALL), F32),
            pltpu.VMEM((ALL, ALL), jnp.int32),
            pltpu.VMEM(states, F32),
            pltpu.VMEM((ALL, MODEL_WIDTH), F32),
            pltpu.VMEM((HEADS, ALL, ALL), BF16),
            pltpu.VMEM((ALL, MODEL_WIDTH), BF16),
            pltpu.VMEM(states, BF16),
            pltpu.VMEM(states, BF16),
            dma((HEADS,)),
            dma((HEADS,)),
            pltpu.VMEM((MODEL_WIDTH, MIX), BF16),
            pltpu.VMEM((MODEL_WIDTH, SMALL), BF16),
            pltpu.VMEM((ROWS * EDGE, MODEL_WIDTH), BF16),
            dma((ROWS,)),
            dma((ROWS,)),
            dma((MIX // WIDE + 1,)),
            pltpu.VMEM((long, MIX), F32),
        ] + routes,
        compiler_params=pltpu.CompilerParams(
            collective_id=1, has_side_effects=True, vmem_limit_bytes=56 * 2**20
        ),
        name="mixer_forward",
    )(starts, tokens, head_gain, *weights)
    return results if routed else [weights[0]] + list(results)


def mixer_backward_kernel(routed, *refs):
    (starts, grad_gated, grad_mid, tokens, gains, full, conv, head_gain), refs = refs[:8], refs[8:]
    (pre, raw, beta, solved, solved_w, fresh, state, power, outputs), refs = refs[:9], refs[9:]
    if routed:
        (normed_t, grad_mlp, grads), refs = refs[:3], refs[3:]
        (grad_hidden, *targets), refs = refs[:4], refs[4:]
        (mix_sum, small_sum, head_sum), refs = refs[:3], refs[3:]
        (grad_project, grad_logits, grad_conv, grad_head, grad_gain), refs = refs[:5], refs[5:]
    else:
        (grad_hidden, grad_project, grad_logits, grad_conv, grad_head, grad_gain), refs = refs[:6], refs[6:]
    (carry_in, carry_out, taps, within, below), refs = refs[:5], refs[5:]
    (grad_out, grad_raw, grad_beta, arriving, leaving, halo_out, halo_in), refs = refs[:7], refs[7:]
    (send, receive, halo_send, halo_receive, mix, load_sem), refs = refs[:6], refs[6:]
    fresh_part, offset = grad_hidden, grad_raw
    small = mix.at[:, pl.ds(AT_SMALL, SMALL)]
    count = lax.axis_size("seq")
    index = lax.axis_index("seq")
    first = index * TOKENS
    sums = after = iter(())
    if routed:
        at = Place(count // 2)
        at.greet(-1)
        parts, by_level, part_sem, level_sem, head_sends = refs[:5]
        refs = refs[5:]
        out_sum, up_sum, down_sum = targets
        cut = HALF_REST - MODEL_WIDTH
        sums = scatter_steps(
            at, (0, HALF_REST), HALF_REST, grads, ((out_sum, 0, MODEL_WIDTH), (up_sum, 0, cut)), *refs[:11]
        )
        after = scatter_steps(
            at, (HALF_REST, HALF_REST), HALF_REST, grads, ((up_sum, cut, 2 * FF - cut), (down_sum, 0, FF)), *refs[11:22]
        )
        until(sums, "started")
    else:
        barrier = pltpu.get_barrier_semaphore()

        @pl.when(index + 1 < count)
        def _():
            pl.semaphore_signal(barrier, inc=1, device_id={"seq": index + 1}, device_id_type=MESH)

        @pl.when(index > 0)
        def _():
            pl.semaphore_wait(barrier, 1)

    load_mix = pltpu.make_async_copy(full.at[:, pl.ds(0, AT_OUT)], mix, load_sem)
    load_mix.start()

    @pl.when(index + 1 == count)
    def _():
        arriving[...] = jnp.zeros_like(arriving)
        halo_in[...] = jnp.zeros_like(halo_in)

    fill_masks(starts, first, carry_in, carry_out, taps, within, below)
    grad_head[...] = jnp.zeros_like(grad_head)
    grad_beta[...] = jnp.zeros_like(grad_beta)

    def active_of(part, head):
        values = raw[:, head_columns(part, head)].astype(F32)
        return values * jax.nn.sigmoid(values)

    def prepare(head):
        columns = head_columns(0, head)
        gate_columns = head_columns(3, head)
        gate = pre[pl.ds(0, ALL), gate_columns].astype(F32)
        sigma = jax.nn.sigmoid(gate)
        output = outputs[:, columns]
        scale = lax.rsqrt(jnp.mean(output * output, axis=-1, keepdims=True) + HEAD_ZERO)
        sample = output * scale
        incoming = grad_gated[:, columns]
        gain = head_gain[...]
        grad_project[:, gate_columns] = low(incoming * sample * gain * (sigma * (1.0 + gate * (1.0 - sigma))))
        grad_sample = incoming * (gate * sigma)
        grad_head[0:1, :] += jnp.sum(grad_sample * sample, axis=0, keepdims=True)
        scaled = grad_sample * gain
        mean = jnp.mean(scaled * output, axis=-1, keepdims=True)
        here = low(scale * scaled - output * (scale * scale * scale * mean))
        grad_out[:, columns] = here
        active_q, active_k = active_of(0, head), active_of(1, head)
        query = active_q * (unit_scale(active_q) * HEAD_SIZE**-0.5)
        key = active_k * unit_scale(active_k)
        attend = low(within[...] * nt(low(query), low(key)))
        part = tn(attend, here)
        fresh_part[:, columns] = part
        entering = low(carry_in[...] * query)
        part_low = low(part)
        w = solved_w[:, columns]
        for row in range(ROWS):
            span = slice(row * TOKENS, (row + 1) * TOKENS)
            offset[span, columns] = tn(entering[span], here[span]) - tn(w[span], part_low[span])

    for head in range(HEADS):
        prepare(head)
        advance(sums, AT_PREPARE)

    def copy(head):
        return pltpu.make_async_remote_copy(
            src_ref=leaving.at[head], dst_ref=arriving.at[head], send_sem=send.at[head], recv_sem=receive.at[head],
            device_id={"seq": index - 1}, device_id_type=MESH,
        )

    def chain(head):
        @pl.when(index + 1 < count)
        def _():
            copy(head).wait_recv()

        @pl.when(index > 0)
        def _():
            for row in range(ROWS):
                start = offset[pl.ds(row * TOKENS, TOKENS), head_columns(0, head)]
                leaving[head, row] = low(tn(power[head, row], arriving[head, row]) + start)
            copy(head).start()

    until(after, "started")
    both_advance(AT_CHAIN, sums, after)
    more = iter(())
    if routed:
        sender = Sender(head_sends)

        def exchange(number, value, row, spot):
            parts[2 * number] = value
            device = {"dp": row, "seq": spot}
            sender.start(None, parts.at[2 * number], parts.at[2 * number + 1], device, part_sem.at[number])
            return lambda: sender.arrived(None, parts.at[2 * number + 1], device, part_sem.at[number])

        pending = exchange(0, grad_head[...], at.row, at.sibling)

    for head in range(HEADS):
        chain(head)

    def finish(head):
        columns = head_columns(0, head)
        raw_q, raw_k = raw[:, columns].astype(F32), raw[:, head_columns(1, head)].astype(F32)
        raw_v = raw[:, head_columns(2, head)].astype(F32)
        sigma_q, sigma_k, sigma_v = jax.nn.sigmoid(raw_q), jax.nn.sigmoid(raw_k), jax.nn.sigmoid(raw_v)
        active_q, active_k, values = raw_q * sigma_q, raw_k * sigma_k, raw_v * sigma_v
        scale_q, scale_k = unit_scale(active_q), unit_scale(active_k)
        query = low(active_q * (scale_q * HEAD_SIZE**-0.5))
        key_full = active_k * scale_k
        key = low(key_full)
        enter, leave = carry_in[...], carry_out[...]
        strength = lane_of(beta[...], BETA_AT + head)
        here = grad_out[:, columns]
        x = fresh[:, columns]
        leaving_keys = low(leave * key_full)
        grad_x = fresh_part[:, columns] + per_row(lambda row, part: nn(part, arriving[head, row]), leaving_keys)
        y = tn(solved[head], low(grad_x))
        y_low = low(y)
        grad_attend = low(within[...] * nt(here, x))
        gram = nt(key, key)
        grad_system = -below[...] * nt(y_low, x)
        grad_gram = low(strength * grad_system)
        grad_q = nn(grad_attend, key) + enter * per_row(lambda row, part: nt(part, state[head, row]), here)
        grad_k = (
            tn(grad_attend, query)
            + leave * per_row(lambda row, part: nt(part, arriving[head, row]), x)
            + nn(grad_gram, key)
            + tn(grad_gram, key)
            - strength * enter * per_row(lambda row, part: nt(part, state[head, row]), y_low)
        )
        z = values - enter * per_row(lambda row, part: nn(part, state[head, row]), key)
        grad_v = strength * y
        grad_strength = jnp.sum(y * z, axis=-1, keepdims=True) + jnp.sum(grad_system * gram, axis=-1, keepdims=True)
        lanes = lax.broadcasted_iota(jnp.int32, grad_beta.shape, 1)
        grad_beta[...] = jnp.where(lanes == BETA_AT + head, grad_strength, grad_beta[...])

        def through(grad, active, scale, part, sigma, extra):
            grad = grad * extra
            mean = jnp.sum(active * grad, axis=-1, keepdims=True)
            grad = scale * grad - active * (scale * scale * scale * mean)
            return grad * (sigma * (1.0 + part * (1.0 - sigma)))

        grad_raw[:, columns] = through(grad_q, active_q, scale_q, raw_q, sigma_q, HEAD_SIZE**-0.5)
        grad_raw[:, head_columns(1, head)] = through(grad_k, active_k, scale_k, raw_k, sigma_k, 1.0)
        grad_raw[:, head_columns(2, head)] = grad_v * (sigma_v * (1.0 + raw_v * (1.0 - sigma_v)))

    for head in range(HEADS):
        finish(head)
        both_advance(AT_FINISH, sums, after)

    def convolve_back(step, _):
        columns = pl.ds(pl.multiple_of(step * HEAD_SIZE, HEAD_SIZE), HEAD_SIZE)
        weight = conv[:, columns]
        nothing = jnp.zeros((HALO, HEAD_SIZE), F32)
        sums = [jnp.zeros((1, HEAD_SIZE), F32) for _ in range(KW)]
        early = []
        for row in range(ROWS):
            span = pl.ds(row * TOKENS, TOKENS)
            grad = grad_raw[span, columns]
            main = pre[span, columns].astype(F32)
            edge = pre[pl.ds(ALL + row * EDGE, EDGE), columns].astype(F32)
            longer = padded(main, edge[EDGE - HALO :])
            total = weight[0:1] * jnp.concatenate([nothing, grad], axis=0)
            sums[0] = sums[0] + jnp.sum(grad * main, axis=0, keepdims=True)
            for shift in range(1, KW):
                masked = grad * taps[shift - 1, span, :]
                wide = jnp.concatenate([nothing, masked, nothing], axis=0)
                total = total + weight[shift : shift + 1] * wide[shift : shift + HALO + TOKENS]
                before = longer[HALO - shift : HALO - shift + TOKENS]
                sums[shift] = sums[shift] + jnp.sum(masked * before, axis=0, keepdims=True)
            early.append(total[:HALO])
            grad_raw[span, columns] = total[HALO:]
        halo_out[:, columns] = low(jnp.concatenate(early, axis=0))
        grad_conv[:, columns] = jnp.concatenate(sums, axis=0)
        return 0

    for part in range(3):
        lax.fori_loop(part * HEADS, (part + 1) * HEADS, convolve_back, 0)
        both_advance(AT_CONV, sums, after)
    back = pltpu.make_async_remote_copy(
        src_ref=halo_out, dst_ref=halo_in, send_sem=halo_send, recv_sem=halo_receive,
        device_id={"seq": index - 1}, device_id_type=MESH,
    )

    @pl.when(index > 0)
    def _():
        back.start()

    strengths = beta[...]
    grad_logits[...] = low(grad_beta[...] * strengths * (1.0 - strengths))

    @pl.when(index + 1 < count)
    def _():
        back.wait_recv()

    for row in range(ROWS):
        end = pl.ds((row + 1) * TOKENS - HALO, HALO)
        grad_raw[end, :] += halo_in[...].astype(F32)[row * HALO : (row + 1) * HALO]

    def narrow(step, _):
        rows = pl.ds(pl.multiple_of(step * 32, 32), 32)
        grad_project[rows, pl.ds(0, QKV)] = low(grad_raw[rows, :])
        return 0

    lax.fori_loop(0, ALL // 32, narrow, 0)

    load_mix.wait()
    both_advance(AT_NORMED, sums, after)

    def normed_back(step, _):
        rows = pl.ds(pl.multiple_of(step * 256, 256), 256)
        grad_hidden[:, rows] = nt(grad_project[...], mix[rows, pl.ds(0, MIX)]) + nt(grad_logits[...], small[rows, :])
        return 0

    lax.fori_loop(0, MODEL_WIDTH // 256, normed_back, 0)
    grad_gain[...] = jnp.zeros_like(grad_gain)

    def hidden_back(step, _):
        rows = pl.ds(pl.multiple_of(step * 32, 32), 32)
        hidden = tokens[rows, :].astype(F32)
        scale = lax.rsqrt(jnp.mean(hidden * hidden, axis=-1, keepdims=True) + NEAR_ZERO)
        grad = grad_hidden[rows, :]
        grad_gain[...] += jnp.sum(grad * hidden * scale, axis=0, keepdims=True)
        scaled = grad * gains[0:1, :]
        mean = jnp.mean(scaled * hidden, axis=-1, keepdims=True)
        grad_hidden[rows, :] = grad_mid[rows, :] + scale * scaled - hidden * (scale * scale * scale * mean)
        return 0

    lax.fori_loop(0, ALL // 32, hidden_back, 0)
    if routed:
        turned = grad_raw.at[pl.ds(0, HEAD_SIZE), pl.ds(0, MODEL_WIDTH)]
        turned[...] = jnp.zeros_like(turned)
        turned[0:1, :] = grad_gain[...]
        turned[1:2, :] = grad_mlp[...]
        move = tap_moves()
        for block in range(MODEL_WIDTH // HEAD_SIZE):
            wide = nt(low(grad_conv[:, pl.ds(block * 3 * HEAD_SIZE, 3 * HEAD_SIZE)]), move)
            lanes = pl.ds(block * HEAD_SIZE, HEAD_SIZE)
            for tap in range(KW):
                for third in range(3):
                    place = CONV_AT + 3 * tap + third
                    turned[place : place + 1, lanes] = wide[tap : tap + 1, third * HEAD_SIZE : (third + 1) * HEAD_SIZE]

        def weigh(tile, _):
            columns = pl.ds(pl.multiple_of(tile * 256, 256), 256)
            mix[:, columns] = low(nn(normed_t[...], grad_project[:, columns]))
            return 0

        lax.fori_loop(0, MIX // 256, weigh, 0)
        mix[:, pl.ds(AT_SMALL, SMALL)] = low(nn(normed_t[...], grad_logits[...]) + turned[...].T)
        more = scatter_steps(
            at, (0, AT_OUT), CHUNK_MIX, mix, ((mix_sum, 0, MIX), (small_sum, 0, SMALL)), *refs[22:]
        )
        until(more, "started")
        for number, (row, spot) in enumerate(((at.near, at.spot), (at.far, at.spot))):
            both_advance(AT_END, sums, after, more)
            pending()
            value = parts[2 * number] + parts[2 * number + 1]
            pending = exchange(number + 1, value, row, spot)
        both_advance(AT_END, sums, after, more)
        pending()
        by_level[at.level] = parts[4] + parts[5]
        here = {"dp": at.near, "seq": at.spot}

        def pass_on(condition, up, source):
            device = {"dp": at.row, "seq": at.spot + 2 if up else at.spot - 2}
            sender.start(condition, by_level.at[source], by_level.at[source], device, level_sem.at[source])

        pass_on(at.above, True, at.level)
        pass_on(at.below, False, at.level)
        for step in range(1, at.levels):
            both_advance(AT_END, sums, after, more)
            for condition, source, up, onward in (
                (at.level - step >= 0, at.level - step, True, at.above),
                (at.level + step < at.levels, at.level + step, False, at.below),
            ):
                sender.arrived(condition, by_level.at[source], here, level_sem.at[source])
                if step < at.levels - 1:
                    pass_on(condition & onward, up, source)
        value = by_level[0]
        for level in range(1, at.levels):
            value = value + by_level[level]
        head_sum[...] = jnp.broadcast_to(jnp.sum(value, axis=0, keepdims=True), value.shape)
        for _ in range(12):
            both_advance(AT_END, sums, after, more)
        until(sums, "end")
        until(after, "end")
        until(more, "end")
        sender.drain()

    @pl.when(index > 0)
    def _():
        back.wait_send()

        def drain(head, _):
            copy(head).wait_send()
            return 0

        lax.fori_loop(0, HEADS, drain, 0)


def mixer_backward(operands, normed, grad_mlp, grads, routed):
    vmem, anywhere = pl.BlockSpec(memory_space=pltpu.VMEM), pl.BlockSpec(memory_space=pl.ANY)
    dma = pltpu.SemaphoreType.DMA
    shape = jax.ShapeDtypeStruct
    states = (HEADS, ROWS, HEAD_SIZE, HEAD_SIZE)
    levels = lax.axis_size("seq") // 2
    local = [
        ((ALL, MIX), BF16),
        ((ALL, SMALL), BF16),
        ((KW, QKV), F32),
        ((8, HEAD_SIZE), F32),
        ((1, MODEL_WIDTH), F32),
    ]
    scratch = [
        pltpu.VMEM((ALL, HEAD_SIZE), F32),
        pltpu.VMEM((ALL, HEAD_SIZE), F32),
        pltpu.VMEM((KW - 1, ALL, HEAD_SIZE), F32),
        pltpu.VMEM((ALL, ALL), F32),
        pltpu.VMEM((ALL, ALL), F32),
        pltpu.VMEM((ALL, MODEL_WIDTH), BF16),
        pltpu.VMEM((ALL, QKV), F32),
        pltpu.VMEM((ALL, SMALL), F32),
        pltpu.VMEM(states, BF16),
        pltpu.VMEM(states, BF16),
        pltpu.VMEM((ROWS * HALO, QKV), BF16),
        pltpu.VMEM((ROWS * HALO, QKV), BF16),
        dma((HEADS,)),
        dma((HEADS,)),
        dma,
        dma,
        pltpu.VMEM((MODEL_WIDTH, AT_OUT), BF16),
        dma,
    ]
    more = []
    out_shape = [shape((ALL, MODEL_WIDTH), F32)]
    if routed:
        more = [normed, grad_mlp, grads]
        out_shape += [shape((2 * PIECE, width), F32) for width in (MODEL_WIDTH, 2 * FF, FF, MIX, SMALL)]
        out_shape += [shape((8, HEAD_SIZE), F32)]
        scratch = [pltpu.VMEM(*entry) for entry in local] + scratch
        scratch += [
            pltpu.VMEM((6, 8, HEAD_SIZE), F32),
            pltpu.VMEM((levels, 8, HEAD_SIZE), F32),
            dma((3,)),
            dma((levels,)),
            dma((3 + 2 * levels,)),
        ]
        scratch += scatter_buffers(levels, HALF_REST, True) + scatter_buffers(levels, HALF_REST, True)
        scratch += scatter_buffers(levels, AT_OUT, False)
    else:
        out_shape += [shape(*entry) for entry in local]
    in_specs = [pl.BlockSpec(memory_space=pltpu.SMEM)] + [vmem] * 4 + [anywhere] + [vmem] * 11
    in_specs += [vmem, vmem, anywhere] if routed else []
    return pl.pallas_call(
        functools.partial(mixer_backward_kernel, routed),
        out_shape=out_shape,
        in_specs=in_specs,
        out_specs=[vmem] * len(out_shape),
        scratch_shapes=scratch,
        compiler_params=pltpu.CompilerParams(
            collective_id=2, has_side_effects=True, vmem_limit_bytes=63 * 2**20
        ),
        name="mixer_backward",
    )(*operands, *more)


TILE = 256
HANDS = 32
OWN = FF // HANDS
GROUP_ROWS = 4 * OWN


def mlp_kernel(
    full, tokens, cotangent, gated, gains,
    output, grad_mid, grad_gated, grad_gain, grads,
    out_w, up_w, packed, wide, down_w, hidden, normed, total, grad_normed,
    normed_t, gated_t, acted_t, up_stage, stage, load_sem, up_sem, store_sem, stage_sem,
):
    def load(number):
        columns, target = (
            (pl.ds(AT_OUT, MODEL_WIDTH), out_w),
            (pl.ds(AT_DOWN, FF), packed),
        )[number]
        return pltpu.make_async_copy(full.at[:, columns], target, load_sem.at[number])

    def load_up(tile, side):
        begin = pl.multiple_of(side * FF + tile * TILE, TILE)
        source = full.at[:, pl.ds(pl.multiple_of(AT_UP + begin, 128), TILE)]
        return pltpu.make_async_copy(source, up_w.at[:, pl.ds(begin, TILE)], up_sem.at[side, tile])

    load(1).start()
    load(0).start()

    def start_up(tile, _):
        load_up(tile, 0).start()
        load_up(tile, 1).start()
        return 0

    lax.fori_loop(0, FF // TILE, start_up, 0)
    load(1).wait()

    def unpack(hand, _):
        for half in range(2):
            rows = pl.ds(pl.multiple_of((hand * 2 + half) * PIECE, PIECE), PIECE)
            piece = packed[rows, :].astype(F32)
            for lane in range(2):
                for step in range(11):
                    source = (lane * 11 + step) * 128
                    target = pl.ds(pl.multiple_of(hand * OWN + step * 8, 8), 8)
                    for top in range(2):
                        column = (4 * half + 2 * top + lane) * 128
                        wide[target, column : column + 128] = piece[top * 8 : top * 8 + 8, source : source + 128]
        return 0

    lax.fori_loop(0, HANDS, unpack, 0)

    def narrow(tile, _):
        rows = pl.ds(pl.multiple_of(tile * TILE, TILE), TILE)
        down_w[rows, :] = low(wide[rows, :])
        return 0

    lax.fori_loop(0, FF // TILE, narrow, 0)
    load(0).wait()
    gated_t[...] = low(gated[...].astype(F32).T)
    middle = tokens[...].astype(F32) + nn(gated[...], out_w[...])
    hidden[...] = middle
    inverse = lax.rsqrt(jnp.mean(middle * middle, axis=-1, keepdims=True) + NEAR_ZERO)
    value = middle * inverse * gains[1:2, :]
    normed[...] = low(value)
    normed_t[...] = low(value.T)
    total[...] = jnp.zeros_like(total)
    grad_normed[...] = jnp.zeros_like(grad_normed)

    def store_up(tile, slot, side):
        begin = pl.multiple_of(MODEL_WIDTH + side * FF + tile * TILE, TILE)
        return pltpu.make_async_copy(up_stage.at[slot, side], grads.at[:, pl.ds(begin, TILE)], store_sem.at[slot, side])

    def tile_step(tile, _):
        slot = lax.rem(tile, 2)
        here = pl.ds(pl.multiple_of(tile * TILE, TILE), TILE)
        there = pl.ds(pl.multiple_of(FF + tile * TILE, TILE), TILE)
        load_up(tile, 0).wait()
        load_up(tile, 1).wait()

        @pl.when(tile >= 2)
        def _():
            store_up(tile - 2, slot, 0).wait()
            store_up(tile - 2, slot, 1).wait()

        gate = nn(normed[...], up_w[:, here])
        up = nn(normed[...], up_w[:, there])
        grad = nt(cotangent[...], down_w[here, :])
        sigma = jax.nn.sigmoid(gate)
        soft = gate * sigma
        acted = soft * up
        acted_low = low(acted)
        acted_t[here, :] = low(acted.T)
        total[...] += nn(acted_low, down_w[here, :])
        grad_gate = low(grad * up * (sigma * (1.0 + gate * (1.0 - sigma))))
        grad_up = low(grad * soft)
        grad_normed[...] += nt(grad_gate, up_w[:, here]) + nt(grad_up, up_w[:, there])
        up_stage[slot, 0] = low(nn(normed_t[...], grad_gate))
        up_stage[slot, 1] = low(nn(normed_t[...], grad_up))
        store_up(tile, slot, 0).start()
        store_up(tile, slot, 1).start()
        return 0

    tiles = FF // TILE
    lax.fori_loop(0, tiles, tile_step, 0)
    middle = hidden[...]
    output[...] = low(middle + total[...])
    inverse = lax.rsqrt(jnp.mean(middle * middle, axis=-1, keepdims=True) + NEAR_ZERO)
    grad = grad_normed[...]
    grad_gain[...] = jnp.sum(grad * middle * inverse, axis=0, keepdims=True)
    scaled = grad * gains[1:2, :]
    mean = jnp.mean(scaled * middle, axis=-1, keepdims=True)
    grad = cotangent[...].astype(F32) + inverse * scaled - middle * (inverse * inverse * inverse * mean)
    grad_mid[...] = grad
    grad_low = low(grad)
    grad_gated[...] = nt(grad_low, out_w[...])
    for last in range(2):
        tile = tiles - 2 + last
        for side in range(2):
            store_up(tile, tile % 2, side).wait()

    def store_out(tile):
        slot, side = divmod(tile, 2)
        columns = pl.ds(tile * TILE, TILE)
        return pltpu.make_async_copy(up_stage.at[slot, side], grads.at[:, columns], store_sem.at[slot, side])

    for tile in range(MODEL_WIDTH // TILE):
        slot, side = divmod(tile, 2)
        up_stage[slot, side] = low(nn(gated_t[...], grad_low[:, tile * TILE : (tile + 1) * TILE]))
        store_out(tile).start()

    def store_down(group, slot):
        rows = pl.ds(pl.multiple_of(group * 128, 128), 128)
        target = grads.at[rows, pl.ds(MODEL_WIDTH + 2 * FF, FF)]
        return pltpu.make_async_copy(stage.at[slot], target, stage_sem.at[slot])

    def down_step(group, _):
        slot = lax.rem(group, 2)

        @pl.when(group >= 2)
        def _():
            store_down(group - 2, slot).wait()

        rows = pl.ds(pl.multiple_of(group * GROUP_ROWS, GROUP_ROWS), GROUP_ROWS)
        wide[pl.ds(0, GROUP_ROWS), :] = nn(acted_t[rows, :], cotangent[...])
        for hand in range(4):
            for half in range(2):
                for lane in range(2):
                    for step in range(11):
                        rows = slice(hand * OWN + step * 8, hand * OWN + step * 8 + 8)
                        first = (4 * half + lane) * 128
                        second = (4 * half + 2 + lane) * 128
                        pair = jnp.concatenate(
                            [wide[rows, first : first + 128], wide[rows, second : second + 128]], axis=0
                        )
                        target = (lane * 11 + step) * 128
                        begin = (hand * 2 + half) * PIECE
                        stage[slot, begin : begin + PIECE, target : target + 128] = low(pair)
        store_down(group, slot).start()
        return 0

    groups = HANDS // 4
    lax.fori_loop(0, groups, down_step, 0)
    for group in (groups - 2, groups - 1):
        store_down(group, group % 2).wait()
    for tile in range(MODEL_WIDTH // TILE):
        store_out(tile).wait()


def mlp(full, tokens, cotangent, gated, gains):
    vmem, anywhere = pl.BlockSpec(memory_space=pltpu.VMEM), pl.BlockSpec(memory_space=pl.ANY)
    dma = pltpu.SemaphoreType.DMA
    shape = jax.ShapeDtypeStruct
    return pl.pallas_call(
        mlp_kernel,
        out_shape=[
            shape((ALL, MODEL_WIDTH), BF16),
            shape((ALL, MODEL_WIDTH), F32),
            shape((ALL, MODEL_WIDTH), F32),
            shape((1, MODEL_WIDTH), F32),
            shape((MODEL_WIDTH, PACK - AT_OUT), BF16),
        ],
        in_specs=[anywhere] + [vmem] * 4,
        out_specs=[vmem] * 4 + [anywhere],
        scratch_shapes=[
            pltpu.VMEM((MODEL_WIDTH, MODEL_WIDTH), BF16),
            pltpu.VMEM((MODEL_WIDTH, 2 * FF), BF16),
            pltpu.VMEM((MODEL_WIDTH, FF), BF16),
            pltpu.VMEM((FF, MODEL_WIDTH), F32),
            pltpu.VMEM((FF, MODEL_WIDTH), BF16),
            pltpu.VMEM((ALL, MODEL_WIDTH), F32),
            pltpu.VMEM((ALL, MODEL_WIDTH), BF16),
            pltpu.VMEM((ALL, MODEL_WIDTH), F32),
            pltpu.VMEM((ALL, MODEL_WIDTH), F32),
            pltpu.VMEM((MODEL_WIDTH, ALL), BF16),
            pltpu.VMEM((MODEL_WIDTH, ALL), BF16),
            pltpu.VMEM((FF, ALL), BF16),
            pltpu.VMEM((2, 2, MODEL_WIDTH, TILE), BF16),
            pltpu.VMEM((2, 128, FF), BF16),
            dma((2,)),
            dma((2, FF // TILE)),
            dma((2, 2)),
            dma((2,)),
        ],
        compiler_params=pltpu.CompilerParams(vmem_limit_bytes=60 * 2**20),
        name="mlp",
    )(full, tokens, cotangent, gated, gains)


def pack_down(part):
    lead = part.shape[:-2]
    tiles = part.reshape(lead + (11, 8, 4, 2, 128))
    n = len(lead)
    moved = tiles.transpose(tuple(range(n)) + (n + 2, n + 1, n + 3, n, n + 4))
    return moved.reshape(lead + (2 * PIECE, FF))


def unpack_down(part):
    lead = part.shape[:-2]
    tiles = part.reshape(lead + (4, 8, 2, 11, 128))
    n = len(lead)
    moved = tiles.transpose(tuple(range(n)) + (n + 3, n + 1, n, n + 2, n + 4))
    return moved.reshape(lead + (OWN, MODEL_WIDTH))


def pack_taps(conv):
    taps = conv.reshape(KW, -1, 3, 2 * PIECE)
    return taps.transpose(1, 3, 0, 2).reshape(-1, 3 * KW)


def unpack_taps(taps):
    taps = taps.reshape(-1, 2 * PIECE, KW, 3)
    return taps.transpose(2, 0, 3, 1).reshape(KW, -1)


def pack_small(mixer, mlp_part, beta, conv):
    parts = jnp.concatenate([mixer[:, None], mlp_part[:, None], beta, pack_taps(conv)], axis=1)
    return jnp.pad(parts, ((0, 0), (0, SMALL - parts.shape[1])))


def shards(
    tokens, cotangent, starts, mixer_gain, mix_weight, conv_weight, beta_weight, head_gain, out_weight, mlp_gain,
    upgate_weight, down_weight,
):
    rows, block, width = tokens.shape
    share = mix_weight.shape[1]
    both = ("dp", "seq")
    routed = lax.axis_size("dp") == 4 and lax.axis_size("seq") % 2 == 0 and share == 2 * PIECE
    parts = [mixer_gain[0], mlp_gain[0], beta_weight[0], conv_weight[0].T, mix_weight[0], out_weight[0], upgate_weight[0], down_weight[0]]
    if not routed:
        parts = [lax.all_gather(part, both, axis=0, tiled=True) for part in parts]
    mixer_w, mlp_w, beta_w, conv_w, mix_w, out_w, up_w, down_w = parts
    small_w = pack_small(mixer_w, mlp_w, beta_w, conv_w.T)
    down_w = pack_down(down_w.reshape(-1, OWN, width)).reshape(-1, FF)
    weights = [mix_w, small_w, out_w, up_w, down_w]
    if not routed:
        weights = [jnp.concatenate(weights, axis=1)]

    flat = tokens.reshape(rows * block, width)
    flat_grad = cotangent.reshape(rows * block, width)
    head_f = head_gain.astype(F32)
    full, normed, pre, raw, beta, solved, solved_w, fresh, state, power, outputs, gated, conv, gains = mixer_forward(
        starts, flat, head_f, weights
    )
    output, grad_mid, grad_gated, grad_mlp, grads = mlp(full, flat, flat_grad, gated, gains)
    operands = [
        starts, grad_gated, grad_mid, flat, gains, full, conv, head_f,
        pre, raw, beta, solved, solved_w, fresh, state, power, outputs,
    ]
    results = mixer_backward(operands, normed, grad_mlp, grads, routed)
    if routed:
        grad_hidden, out_mine, up_mine, down_mine, mix_mine, small_mine, head_mine = results
        head_mine = head_mine[:1]
        down_mine = unpack_down(down_mine)
        mixer_mine, mlp_mine = small_mine[:, 0], small_mine[:, 1]
        beta_mine = small_mine[:, BETA_AT:CONV_AT]
        conv_mine = unpack_taps(small_mine[:, CONV_AT : CONV_AT + 3 * KW])
    else:
        grad_hidden, grad_project, grad_logits, grad_conv, grad_head, grad_mixer = results
        whole_mix = lax.dot_general(normed, grad_project, (((1,), (0,)), ((), ())), preferred_element_type=F32)
        whole_beta = lax.dot_general(normed, grad_logits, (((1,), (0,)), ((), ())), preferred_element_type=F32)
        whole_down = unpack_down(grads[:, MODEL_WIDTH + 2 * FF :].reshape(-1, 2 * PIECE, FF)).reshape(FF, width)
        listed = [
            whole_mix,
            grads[:, :MODEL_WIDTH],
            grads[:, MODEL_WIDTH : MODEL_WIDTH + 2 * FF],
            whole_down,
            grad_mixer[0],
            grad_mlp[0],
            whole_beta[:, BETA_AT:CONV_AT],
            grad_conv.T,
        ]
        listed = [
            lax.psum_scatter(part.astype(F32), both, scatter_dimension=0, tiled=True) for part in listed
        ]
        mix_mine, out_mine, up_mine, down_mine, mixer_mine, mlp_mine, beta_mine, conv_mine = listed
        conv_mine = conv_mine.T
        head_mine = lax.psum(jnp.sum(grad_head, axis=0, keepdims=True), both)
    return (
        output.reshape(rows, block, width),
        grad_hidden.reshape(rows, block, width),
        mixer_mine[None],
        mix_mine[None],
        conv_mine[None],
        beta_mine[None],
        head_mine,
        out_mine[None],
        mlp_mine[None],
        up_mine[None],
        down_mine[None],
    )


def solution(mesh):
    both = ("dp", "seq")
    in_specs = (
        P("dp", "seq", None),
        P("dp", "seq", None),
        P("dp", None),
        P(None, both),
        P(None, both, None),
        P(None, None, both),
        P(None, both, None),
        P(),
        P(None, both, None),
        P(None, both),
        P(None, both, None),
        P(None, both, None),
    )
    out_specs = (
        P("dp", "seq", None),
        P("dp", "seq", None),
        P(None, both),
        P(None, both, None),
        P(None, None, both),
        P(None, both, None),
        P(),
        P(None, both, None),
        P(None, both),
        P(None, both, None),
        P(None, both, None),
    )
    return jax.shard_map(shards, mesh=mesh, in_specs=in_specs, out_specs=out_specs, check_vma=False)
```

```python
import functools

import jax
import jax.numpy as jnp
from jax import lax
from jax.experimental import pallas as pl
from jax.experimental.pallas import tpu as pltpu
from jax.sharding import PartitionSpec as P

MODEL_WIDTH = 1024
HEADS = 8
HEAD_SIZE = 128
FF = 2816
KW = 4
PACKED = 4

MESH = pl.DeviceIdType.MESH
F32 = jnp.float32
BF16 = jnp.bfloat16
TOKENS = 128
ROWS = 2
ALL = ROWS * TOKENS
HALO = 8
NEAR_ZERO = 1e-06
HEAD_ZERO = 1e-05
MIX = 4 * MODEL_WIDTH
QKV = 3 * MODEL_WIDTH
SMALL = 128
BETA_AT = 2
CONV_AT = 10
AT_SMALL = MIX
AT_OUT = AT_SMALL + SMALL
AT_UP = AT_OUT + MODEL_WIDTH
AT_DOWN = AT_UP + 2 * FF
PACK = AT_DOWN + FF
HALF_REST = (PACK - AT_OUT) // 2
CHUNK_MIX = AT_OUT // 3
PIECE = 16
SLOTS = 2
WINDOW = 8
LAG = 2
EDGE = 16
WIDE = 512
GROUP = 2
AT_PREPARE = 2
AT_CHAIN = (5, 2)
AT_FINISH = (1, 2)
AT_CONV = (0, 0)
AT_NORMED = (2, 2)
AT_END = (1, 2, 3)


def nn(a, b):
    return lax.dot_general(a, b, (((1,), (0,)), ((), ())), preferred_element_type=F32)


def nt(a, b):
    return lax.dot_general(a, b, (((1,), (1,)), ((), ())), preferred_element_type=F32)


def tn(a, b):
    return lax.dot_general(a, b, (((0,), (0,)), ((), ())), preferred_element_type=F32)


def low(value):
    return value.astype(BF16)


def when(condition, action):
    if condition is None:
        action()
    else:
        pl.when(condition)(action)


class Place:
    def __init__(self, levels):
        self.levels = levels
        self.row, self.spot = lax.axis_index("dp"), lax.axis_index("seq")
        self.level, self.core = self.spot // 2, lax.rem(self.spot, 2)
        self.near = self.row + 1 - 2 * lax.rem(self.row, 2)
        self.far = self.row + 2 - 4 * (self.row // 2)
        self.first = self.near * (1 - self.core) + self.far * self.core
        self.second = self.far * (1 - self.core) + self.near * self.core
        self.both = 3 - self.row
        self.above, self.below = self.level + 1 < levels, self.level >= 1
        self.sibling = self.spot + 1 - 2 * self.core

    def greet(self, chain):
        barrier = pltpu.get_barrier_semaphore()
        levels, level, core = self.levels, self.level, self.core

        def signal(row, spot):
            pl.semaphore_signal(barrier, inc=1, device_id={"dp": row, "seq": spot}, device_id_type=MESH)

        signal(self.first, self.spot)
        signal(self.second, self.spot)
        signal(self.row, self.sibling)
        pl.when(self.above)(lambda: signal(self.row, self.spot + 2))
        pl.when(self.below)(lambda: signal(self.row, self.spot - 2))
        has_above = (2 * levels - 2 - level) // levels
        has_below = (level + levels - 1) // levels
        peers = 3 + has_above + has_below
        if chain > 0:
            pl.when(self.below & (core == 0))(lambda: signal(self.row, self.spot - 1))
            peers = peers + has_above * core
        if chain < 0:
            pl.when(self.above & (core == 1))(lambda: signal(self.row, self.spot + 1))
            peers = peers + has_below * (1 - core)
        pl.semaphore_wait(barrier, peers)

    def rows_of(self, owner, spot, half):
        return pl.ds(pl.multiple_of(((owner * 2 * self.levels + spot) * 2 + half) * PIECE, PIECE), PIECE)


class Sender:
    def __init__(self, semaphores):
        self.semaphores, self.used, self.pending = semaphores, 0, []

    def start(self, condition, source, target, device, arrival):
        copy = pltpu.make_async_remote_copy(
            src_ref=source, dst_ref=target, send_sem=self.semaphores.at[self.used], recv_sem=arrival,
            device_id=device, device_id_type=MESH,
        )
        self.used += 1
        when(condition, copy.start)
        self.pending.append((condition, copy))

    def arrived(self, condition, target, device, arrival):
        copy = pltpu.make_async_remote_copy(
            src_ref=target, dst_ref=target, send_sem=self.semaphores.at[0], recv_sem=arrival,
            device_id=device, device_id_type=MESH,
        )
        when(condition, copy.wait_recv)

    def drain(self):
        for condition, copy in self.pending:
            when(condition, copy.wait_send)


def advance(steps, count=1):
    for _ in range(count):
        next(steps, None)


def both_advance(counts, *listed):
    for steps, count in zip(listed, counts):
        advance(steps, count)


def until(steps, mark):
    for found in steps:
        if found == mark:
            return


def gather_semaphores(levels):
    dma = pltpu.SemaphoreType.DMA
    return [dma((2, 2, levels)), dma((2, levels)), dma((2, 2, levels)), dma((2, 4, levels)), dma((8 + 34 * levels,))]


def gather_steps(at, share, full, columns, by_level, by_first, by_second, by_core, sends):
    levels, row, spot, level, core = at.levels, at.row, at.spot, at.level, at.core
    first, second, both, above, below = at.first, at.second, at.both, at.above, at.below
    sender = Sender(sends)
    here = {"dp": first, "seq": spot}

    def piece(half, owner, owner_level):
        return full.at[at.rows_of(owner, owner_level * 2 + core, half), columns]

    def send(condition, half, owner, owner_level, device, arrival):
        target = piece(half, owner, owner_level)
        own = owner is row and owner_level is level
        source = share.at[pl.ds(half * PIECE, PIECE), columns] if own else target
        sender.start(condition, source, target, device, arrival)

    def along(condition, up, half, side, owner, owner_level):
        device = {"dp": row, "seq": spot + 2 if up else spot - 2}
        send(condition, half, owner, owner_level, device, by_level.at[half, side, owner_level])

    def to_first(condition, half, owner_level):
        send(condition, half, row, owner_level, here, by_first.at[half, owner_level])

    def to_second(condition, half, side, owner, owner_level):
        device = {"dp": second, "seq": spot}
        send(condition, half, owner, owner_level, device, by_second.at[half, side, owner_level])

    def to_core(condition, half, owner, owner_level):
        device = {"dp": row, "seq": at.sibling}
        send(condition, half, owner, owner_level, device, by_core.at[half, owner, owner_level])

    def arrived(condition, half, owner, owner_level, arrival):
        sender.arrived(condition, piece(half, owner, owner_level), here, arrival)

    to_first(None, 1, level)
    along(above, True, 0, 0, row, level)
    along(below, False, 0, 0, row, level)
    to_second(None, 0, 0, row, level)
    to_first(None, 0, level)
    to_second(None, 1, 0, row, level)
    along(above, True, 1, 0, row, level)
    along(below, False, 1, 0, row, level)
    to_core(None, 0, row, level)
    to_core(None, 1, row, level)
    yield "started"
    arrived(None, 1, first, level, by_first.at[1, level])
    along(above, True, 1, 1, first, level)
    along(below, False, 1, 1, first, level)
    to_second(None, 1, 1, first, level)
    to_core(None, 1, first, level)
    yield "step"
    arrived(None, 0, first, level, by_first.at[0, level])
    to_second(None, 0, 1, first, level)
    to_core(None, 0, first, level)
    yield "step"

    def from_second(condition, owner_level, half):
        for side, owner in ((0, second), (1, both)):
            arrived(condition, half, owner, owner_level, by_second.at[half, side, owner_level])
            to_core(condition, half, owner, owner_level)

    waiting = [(None, level)]
    for step in range(1, levels):
        ways = ((level - step >= 0, level - step, True), (level + step < levels, level + step, False))

        def onward(up, step=step):
            if up:
                return (level - step >= 0) & above
            return (level + step < levels) & below

        for condition, source, up in ways:
            arrived(condition, 0, row, source, by_level.at[0, 0, source])
            if step < levels - 1:
                along(onward(up), up, 0, 0, row, source)
            to_first(condition, 0, source)
            to_second(condition, 0, 0, row, source)
            to_core(condition, 0, row, source)
        yield "step"
        for side, owner in ((0, row), (1, first)):
            for condition, source, up in ways:
                arrived(condition, 1, owner, source, by_level.at[1, side, source])
                if step < levels - 1:
                    along(onward(up), up, 1, side, owner, source)
                to_second(condition, 1, side, owner, source)
                to_core(condition, 1, owner, source)
            yield "step"
        for condition, source, up in ways:
            arrived(condition, 0, first, source, by_first.at[0, source])
            to_second(condition, 0, 1, first, source)
            to_core(condition, 0, first, source)
        yield "step"
        if step == levels - 1:
            yield "leveled"
        for half in range(2):
            for condition, source in waiting:
                from_second(condition, source, half)
            yield "step"
        waiting = [(condition, source) for condition, source, _ in ways]
    for half in range(2):
        for condition, source in waiting:
            from_second(condition, source, half)
        yield "step"
    yield "issued"
    for half in range(2):
        for owner in range(4):
            for source in range(levels):
                target = full.at[at.rows_of(owner, source * 2 + 1 - core, half), columns]
                sender.arrived(None, target, here, by_core.at[half, owner, source])
    yield "arrived"
    sender.drain()


def scatter_buffers(levels, width, staged):
    dma = pltpu.SemaphoreType.DMA
    buffers = [
        pltpu.VMEM((2, 4, levels, PIECE, width), BF16),
        pltpu.VMEM((2, 2, levels, PIECE, width), BF16),
        pltpu.VMEM((levels + 1, PIECE, width), BF16),
        pltpu.VMEM((3, levels + 1, PIECE, width), BF16),
        dma((2, 4, levels)),
        dma((2, 2, levels)),
        dma((levels + 1,)),
        dma((3, levels + 1)),
        dma((8 + 44 * levels,)),
    ]
    if staged:
        buffers += [pltpu.VMEM((SLOTS, PIECE, width), BF16), dma((SLOTS,))]
    return buffers


def scatter_steps(
    at, columns, chunk, grads, targets, total, by_second, by_first, by_level,
    core_sem, second_sem, first_sem, level_sem, sends, staged=None, load_sem=None,
):
    levels, row, spot, level, core = at.levels, at.row, at.spot, at.level, at.core
    first, second, both, above, below = at.first, at.second, at.both, at.above, at.below
    sender = Sender(sends)
    here = {"dp": first, "seq": spot}
    begin, width = columns
    columns = pl.ds(begin, width)
    ways = [(far, up) for far in range(levels - 1, 0, -1) for up in (True, False)] + [(0, True)]

    def there(way):
        far, up = way
        if far == 0:
            return None, level
        return (level + far < levels, level + far) if up else (level - far >= 0, level - far)

    def add(target, other):
        def body(step, _):
            part = pl.ds(pl.multiple_of(step * chunk, chunk), chunk)
            target[:, part] = target[:, part] + other[:, part]
            return 0

        lax.fori_loop(0, width // chunk, body, 0)

    def arrived(target, arrival):
        sender.arrived(None, target, here, arrival)

    def listing(one, two):
        out = []
        for turn in range(len(ways) + LAG):
            if turn < len(ways):
                out += [(True, ways[turn], half, side, owner) for half in (1, 0) for side, owner in ((0, one), (1, both))]
            if turn >= LAG:
                out += [(False, ways[turn - LAG], half, side, owner) for half in (1, 0) for side, owner in ((0, row), (1, two))]
        return out

    listed = listing(second, first)
    given = listing(first, second)

    def to_core(number):
        _, way, half, _, owner = given[number]
        condition, end = there(way)
        device = {"dp": row, "seq": at.sibling}
        source = grads.at[at.rows_of(owner, end * 2 + 1 - core, half), columns]
        sender.start(condition, source, total.at[half, owner, end], device, core_sem.at[half, owner, end])

    for number in range(WINDOW):
        to_core(number)

    def load(number):
        _, way, half, _, owner = listed[number]
        slot = number % SLOTS
        source = grads.at[at.rows_of(owner, there(way)[1] * 2 + core, half), columns]
        return pltpu.make_async_copy(source, staged.at[slot], load_sem.at[slot])

    def start_load(number):
        if staged is not None and number < len(listed):
            when(there(listed[number][1])[0], lambda: load(number).start())

    for slot in range(SLOTS):
        start_load(slot)
    yield "started"

    def take_listed(number):
        leaves, way, half, side, owner = listed[number]
        if number + WINDOW < len(listed):
            to_core(number + WINDOW)
        condition, end = there(way)
        sums = total.at[half, owner, end]

        def take():
            if staged is not None:
                load(number).wait()
            arrived(sums, core_sem.at[half, owner, end])
            if staged is None:
                add(sums, grads.at[at.rows_of(owner, end * 2 + core, half), columns])
            else:
                add(sums, staged.at[number % SLOTS])

        when(condition, take)
        start_load(number + SLOTS)
        if leaves:
            device = {"dp": second, "seq": spot}
            sender.start(condition, sums, by_second.at[half, side, end], device, second_sem.at[half, side, end])

    for number in range(len(listed)):
        take_listed(number)
        if number % 4 == 3:
            yield "step"
    yield "sent"

    def along(half, side, owner, way):
        far, up = way
        if far == 0:
            return
        condition, end = there(way)
        sums = total.at[half, owner, end]
        place = 0 if half == 0 else 1 + side
        if far < levels - 1:

            def take():
                arrived(by_level.at[place, end], level_sem.at[place, end])
                add(sums, by_level.at[place, end])

            pl.when(condition & (below if up else above))(take)
        slot = end if up or far > 1 else levels
        device = {"dp": row, "seq": spot + 2 if up else spot - 2}
        sender.start(condition, sums, by_level.at[place, slot], device, level_sem.at[place, slot])

    def from_second(half, side, owner, way):
        condition, end = there(way)

        def take():
            arrived(by_second.at[half, side, end], second_sem.at[half, side, end])
            add(total.at[half, owner, end], by_second.at[half, side, end])

        when(condition, take)

    def from_first(way):
        condition, end = there(way)

        def take():
            arrived(by_first.at[end], first_sem.at[end])
            add(total.at[0, row, end], by_first.at[end])

        when(condition, take)
        along(0, 0, row, way)

    previous = None
    for way in ways:
        condition, end = there(way)
        for side, owner in ((0, row), (1, first)):
            from_second(1, side, owner, way)
            along(1, side, owner, way)
        yield "step"
        from_second(0, 1, first, way)
        sender.start(condition, total.at[0, first, end], by_first.at[end], here, first_sem.at[end])
        from_second(0, 0, row, way)
        yield "step"
        if previous is not None:
            from_first(previous)
            yield "step"
        previous = way
    from_first(previous)
    yield "step"

    def collect(half, side, owner):
        sums = total.at[half, owner, level]
        place = 0 if half == 0 else 1 + side

        def take(slot):
            arrived(by_level.at[place, slot], level_sem.at[place, slot])
            add(sums, by_level.at[place, slot])

        pl.when(below)(lambda: take(level))
        pl.when(above)(lambda: take(levels))

    def final(half, *parts):
        rows, at_part = pl.ds(half * PIECE, PIECE), 0
        for target, start, length in targets:
            part = pl.ds(at_part, length)
            value = parts[0][:, part].astype(F32)
            for other in parts[1:]:
                value = value + other[:, part].astype(F32)
            target[rows, pl.ds(start, length)] = value
            at_part += length

    collect(1, 1, first)
    sender.start(None, total.at[1, first, level], by_first.at[levels], here, first_sem.at[levels])
    yield "step"
    collect(1, 0, row)
    yield "step"
    collect(0, 0, row)
    final(0, total.at[0, row, level])
    yield "step"
    arrived(by_first.at[levels], first_sem.at[levels])
    final(1, total.at[1, row, level], by_first.at[levels])
    sender.drain()


def segment(starts, row, places):
    total = jnp.zeros_like(places)
    for k in range(PACKED):
        begin = starts[row, k]
        total = total + jnp.where((begin > 0) & (places >= begin), 1, 0)
    return total


def row_scalars(starts, row, first):
    before = jnp.int32(0)
    last = jnp.int32(0)
    for k in range(PACKED):
        begin = starts[row, k]
        before = before + jnp.where((begin > 0) & (begin <= first - 1), 1, 0)
        last = last + jnp.where((begin > 0) & (begin <= first + TOKENS - 1), 1, 0)
    return before, last


def fill_masks(starts, first, carry_in, carry_out, taps, within, below):
    places = first + lax.broadcasted_iota(jnp.int32, (TOKENS, HEAD_SIZE), 0)
    side = lax.broadcasted_iota(jnp.int32, (TOKENS, TOKENS), 0)
    across = lax.broadcasted_iota(jnp.int32, (TOKENS, TOKENS), 1)
    within[...] = jnp.zeros_like(within)
    below[...] = jnp.zeros_like(below)
    for row in range(ROWS):
        span = pl.ds(row * TOKENS, TOKENS)
        mine = segment(starts, row, places)
        before, last = row_scalars(starts, row, first)
        carry_in[span, :] = (mine == before).astype(F32)
        carry_out[span, :] = (mine == last).astype(F32)
        for shift in range(1, KW):
            there = places - shift
            same = (segment(starts, row, there) == mine) & (there >= 0)
            taps[shift - 1, span, :] = same.astype(F32)
        same = segment(starts, row, first + side) == segment(starts, row, first + across)
        within[span, span] = (same & (side >= across)).astype(F32)
        below[span, span] = (same & (side > across)).astype(F32)


def padded(main, halo):
    return jnp.concatenate([halo, main], axis=0)


def unit_scale(values):
    return lax.rsqrt(jnp.sum(values * values, axis=-1, keepdims=True) + NEAR_ZERO)


def lane_of(values, lane):
    lanes = lax.broadcasted_iota(jnp.int32, values.shape, 1)
    return jnp.sum(jnp.where(lanes == lane, values, 0.0), axis=-1, keepdims=True)


def head_columns(part, head):
    return pl.ds(pl.multiple_of(part * MODEL_WIDTH + head * HEAD_SIZE, HEAD_SIZE), HEAD_SIZE)


def halves(value):
    high = low(value)
    return high, low(value - high.astype(F32))


def gram_of(keys):
    high, rest = halves(keys)
    return nt(high, high) + nt(high, rest) + nt(rest, high)


def per_row(function, *arrays):
    return jnp.concatenate(
        [
            function(row, *[array[row * TOKENS : (row + 1) * TOKENS] for array in arrays])
            for row in range(ROWS)
        ],
        axis=0,
    )


def invert(system, apart):
    eye = jnp.where(apart == 0, 1.0, 0.0)
    solved = eye - jnp.where(apart == 1, system, 0.0)
    size = 2
    while size < TOKENS:
        cross = low(jnp.where((apart >= size) & (apart < 2 * size), system, 0.0))
        rough = low(solved)
        solved = solved - nn(low(nn(rough, cross)), rough)
        size *= 2
    return solved


def kappa_eye(kept):
    side = lax.broadcasted_iota(jnp.int32, (HEAD_SIZE, HEAD_SIZE), 0)
    across = lax.broadcasted_iota(jnp.int32, (HEAD_SIZE, HEAD_SIZE), 1)
    return jnp.where(side == across, 1.0, 0.0) * kept


def tap_moves():
    group = 3 * HEAD_SIZE
    side = lax.broadcasted_iota(jnp.int32, (group, group), 0)
    across = lax.broadcasted_iota(jnp.int32, (group, group), 1)
    third, device, lane = side // HEAD_SIZE, (side % HEAD_SIZE) // 32, side % 32
    return jnp.where(across == device * 96 + third * 32 + lane, 1.0, 0.0).astype(BF16)


def tap_rows(small_rows):
    move = tap_moves()
    wanted = []
    for block in range(MODEL_WIDTH // HEAD_SIZE):
        lanes = slice(block * HEAD_SIZE, (block + 1) * HEAD_SIZE)
        parts = [small_rows[CONV_AT + 3 * j : CONV_AT + 3 * j + 3, lanes] for j in range(KW)]
        source = jnp.concatenate(
            [jnp.concatenate([part[c : c + 1] for c in range(3)], axis=1) for part in parts], axis=0
        )
        wanted.append(nn(low(source), move))
    return wanted


def pack_few(target, turned, mixer_gain, mlp_gain, beta, conv):
    turned[...] = jnp.zeros_like(turned)
    share = 2 * PIECE
    turned[0:1, 0:share] = mixer_gain[...].astype(F32)
    turned[1:2, 0:share] = mlp_gain[...].astype(F32)
    taps = conv[...].astype(F32)
    for tap in range(KW):
        for third in range(3):
            place = CONV_AT + 3 * tap + third
            turned[place : place + 1, 0:share] = taps[tap : tap + 1, third * share : (third + 1) * share]
    value = turned[...].T[:share]
    turned[...] = jnp.zeros_like(turned)
    turned[0:share, BETA_AT:CONV_AT] = beta[...].astype(F32)
    target[:, AT_SMALL:AT_OUT] = low(value + turned[0:share, :])


def mixer_forward_kernel(routed, *refs):
    (starts, tokens, head_gain), refs = refs[:3], refs[3:]
    if routed:
        (mix_share, out_share, up_share, down_share, *few), refs = refs[:8], refs[8:]
    (full, normed, pre_low, raw, beta, solved, solved_w, fresh, state, power, outputs, gated, conv, gains), refs = refs[:14], refs[14:]
    (every, carry_in, carry_out, taps, within, below, apart), refs = refs[:7], refs[7:]
    (offset, solved_u, attend, queries, arriving, leaving, send, receive), refs = refs[:8], refs[8:]
    (mix, small, halo, halo_send, halo_receive, load_sem, pre), refs = refs[:7], refs[7:]
    count = lax.axis_size("seq")
    index = lax.axis_index("seq")
    first = index * TOKENS
    rest = iter(())
    if routed:
        keep_sem, packed, turned = refs[:3]
        routes = refs[3:]
        at = Place(count // 2)

        def keep(number, share, begin):
            columns = pl.ds(begin, share.shape[-1])
            copy = pltpu.make_async_copy(share, packed.at[:, columns], keep_sem.at[number])
            copy.start()
            return copy

        kept = [keep(0, mix_share, 0), keep(1, out_share, AT_OUT), keep(2, up_share, AT_UP)]
        pack_few(packed, turned, *few)
        at.greet(1)
    else:
        barrier = pltpu.get_barrier_semaphore()

        @pl.when(index > 0)
        def _():
            pl.semaphore_signal(barrier, inc=1, device_id={"seq": index - 1}, device_id_type=MESH)

        @pl.when(index + 1 < count)
        def _():
            pl.semaphore_wait(barrier, 1)

    def tail(row):
        return pltpu.make_async_remote_copy(
            src_ref=tokens.at[pl.ds((row + 1) * TOKENS - EDGE, EDGE), :], dst_ref=halo.at[pl.ds(row * EDGE, EDGE), :],
            send_sem=halo_send.at[row], recv_sem=halo_receive.at[row], device_id={"seq": index + 1}, device_id_type=MESH,
        )

    @pl.when(index + 1 < count)
    def _():
        for row in range(ROWS):
            tail(row).start()

    if routed:
        kept[0].wait()
        wanted = gather_steps(at, packed, full, pl.ds(0, AT_OUT), *routes[:5])
        until(wanted, "started")
        rows = down_share[...].astype(F32)

        def store(row, column, value):
            packed[row : row + PIECE, AT_DOWN + column : AT_DOWN + column + 128] = low(value)

        pack_hand(rows, 0, store)

    @pl.when(index == 0)
    def _():
        arriving[...] = jnp.zeros_like(arriving)
        halo[...] = jnp.zeros_like(halo)

    fill_masks(starts, first, carry_in, carry_out, taps, within, below)
    side = lax.broadcasted_iota(jnp.int32, (ALL, ALL), 0)
    across = lax.broadcasted_iota(jnp.int32, (ALL, ALL), 1)
    apart[...] = jnp.bitwise_xor(side, across)
    if routed:
        kept[1].wait()
        kept[2].wait()
        mine = pl.ds(pl.multiple_of((at.row * count + index) * 2 * PIECE, 2 * PIECE), 2 * PIECE)
        own = pltpu.make_async_copy(packed, full.at[mine, :], keep_sem.at[3])
        own.start()
        until(wanted, "issued")
        rest = gather_steps(at, packed, full, pl.ds(AT_OUT, PACK - AT_OUT), *routes[5:])
        until(rest, "started")
        until(wanted, "arrived")
        own.wait()

    def load(number):
        if number < 0:
            return pltpu.make_async_copy(full.at[:, pl.ds(AT_SMALL, SMALL)], small, load_sem.at[MIX // WIDE])
        columns = pl.ds(number * WIDE, WIDE)
        return pltpu.make_async_copy(full.at[:, columns], mix.at[:, columns], load_sem.at[number])

    for number in range(-1, MIX // WIDE):
        load(number).start()
    load(-1).wait()
    small_rows = small[:, pl.ds(0, HEAD_SIZE)].astype(F32).T
    gains[...] = small_rows[:8]
    for block, part in enumerate(tap_rows(small_rows)):
        conv[:, pl.ds(block * 3 * HEAD_SIZE, 3 * HEAD_SIZE)] = part

    def norm(source, target, rows):
        values = source[...].astype(F32)
        scale = lax.rsqrt(jnp.mean(values * values, axis=-1, keepdims=True) + NEAR_ZERO)
        target[rows, :] = low(values * scale * gains[0:1, :])

    norm(tokens, every, pl.ds(0, ALL))

    @pl.when(index > 0)
    def _():
        for row in range(ROWS):
            tail(row).wait_recv()

    norm(halo, every, pl.ds(ALL, ROWS * EDGE))
    normed[...] = low(every[pl.ds(0, ALL), :].astype(F32).T)
    beta[...] = jax.nn.sigmoid(nn(every[pl.ds(0, ALL), :], small[...]))
    for number in range(MIX // WIDE):
        load(number).wait()
        columns = pl.ds(number * WIDE, WIDE)
        wide = nn(every[...], mix[:, columns])
        pre[:, columns] = wide
        pre_low[:, columns] = low(wide)

    def convolve(columns):
        weight = conv[:, columns]
        rows = []
        for row in range(ROWS):
            main = pre[pl.ds(row * TOKENS, TOKENS), columns]
            before = pre[pl.ds(ALL + (row + 1) * EDGE - HALO, HALO), columns]
            longer = padded(main, before)
            total = weight[0:1] * main
            for shift in range(1, KW):
                tap = taps[shift - 1, pl.ds(row * TOKENS, TOKENS), :]
                total = total + weight[shift : shift + 1] * longer[HALO - shift : HALO - shift + TOKENS] * tap
            rows.append(total)
        total = jnp.concatenate(rows, axis=0)
        raw[:, columns] = low(total)
        return total * jax.nn.sigmoid(total)

    def local(head):
        active_q = convolve(head_columns(0, head))
        active_k = convolve(head_columns(1, head))
        values = convolve(head_columns(2, head))
        query = active_q * (unit_scale(active_q) * HEAD_SIZE**-0.5)
        key = active_k * unit_scale(active_k)
        strength = lane_of(beta[...], BETA_AT + head)
        columns = head_columns(0, head)
        system = below[...] * (strength * gram_of(key))
        inverse = low(invert(system, apart[...]))
        solved[head] = inverse
        enter = carry_in[...]
        w = low(nn(inverse, low(strength * enter * key)))
        u = nn(inverse, low(strength * values))
        solved_w[:, columns] = w
        solved_u[:, columns] = u
        leave = low(carry_out[...] * key)
        u_low = low(u)
        for row in range(ROWS):
            span = slice(row * TOKENS, (row + 1) * TOKENS)
            before, last = row_scalars(starts, row, first)
            kept = jnp.where(before == last, 1.0, 0.0)
            power[head, row] = low(kappa_eye(kept) - tn(leave[span], w[span]))
            offset[head, row] = tn(leave[span], u_low[span])
        attend[head] = low(within[...] * nt(low(query), low(key)))
        queries[:, columns] = low(enter * query)


    for step in range(HEADS // GROUP):
        for part in range(GROUP):
            local(step * GROUP + part)
        advance(rest, 2)

    def copy(head):
        return pltpu.make_async_remote_copy(
            src_ref=leaving.at[head], dst_ref=arriving.at[head], send_sem=send.at[head], recv_sem=receive.at[head],
            device_id={"seq": index + 1}, device_id_type=MESH,
        )

    def chain(head):
        @pl.when(index > 0)
        def _():
            copy(head).wait_recv()

        @pl.when(index + 1 < count)
        def _():
            for row in range(ROWS):
                leaving[head, row] = low(nn(power[head, row], arriving[head, row]) + offset[head, row])
            copy(head).start()

        columns = head_columns(0, head)
        w, u, query = solved_w[:, columns], solved_u[:, columns], queries[:, columns]
        x = low(u - per_row(lambda row, part: nn(part, arriving[head, row]), w))
        fresh[:, columns] = x
        output = per_row(lambda row, part: nn(part, arriving[head, row]), query) + nn(attend[head], x)
        outputs[:, columns] = output
        scale = lax.rsqrt(jnp.mean(output * output, axis=-1, keepdims=True) + HEAD_ZERO)
        gate = pre[pl.ds(0, ALL), head_columns(3, head)]
        gated[:, columns] = low(output * scale * head_gain[...].astype(F32) * (gate * jax.nn.sigmoid(gate)))

    advance(rest, 8)
    for head in range(HEADS):
        chain(head)
        advance(rest)
    state[...] = arriving[...]

    @pl.when(index + 1 < count)
    def _():
        for row in range(ROWS):
            tail(row).wait_send()

        def drain(head, _):
            copy(head).wait_send()
            return 0

        lax.fori_loop(0, HEADS, drain, 0)

    until(rest, "end")
    if routed:
        until(wanted, "end")


def mixer_forward(starts, tokens, head_gain, weights):
    routed = len(weights) > 1
    vmem, anywhere = pl.BlockSpec(memory_space=pltpu.VMEM), pl.BlockSpec(memory_space=pl.ANY)
    dma = pltpu.SemaphoreType.DMA
    shape = jax.ShapeDtypeStruct
    states = (HEADS, ROWS, HEAD_SIZE, HEAD_SIZE)
    long = ALL + ROWS * EDGE
    whole = [shape((MODEL_WIDTH, PACK), BF16)] if routed else []
    levels = lax.axis_size("seq") // 2
    routes = []
    if routed:
        routes = [
            dma((4,)),
            pltpu.VMEM((2 * PIECE, PACK), BF16),
            pltpu.VMEM((SMALL, SMALL), F32),
        ]
        routes += gather_semaphores(levels) + gather_semaphores(levels)
    results = pl.pallas_call(
        functools.partial(mixer_forward_kernel, routed),
        out_shape=whole + [
            shape((MODEL_WIDTH, ALL), BF16),
            shape((long, MIX), BF16),
            shape((ALL, QKV), BF16),
            shape((ALL, SMALL), F32),
            shape((HEADS, ALL, ALL), BF16),
            shape((ALL, MODEL_WIDTH), BF16),
            shape((ALL, MODEL_WIDTH), BF16),
            shape(states, BF16),
            shape(states, BF16),
            shape((ALL, MODEL_WIDTH), F32),
            shape((ALL, MODEL_WIDTH), BF16),
            shape((KW, QKV), F32),
            shape((8, MODEL_WIDTH), F32),
        ],
        in_specs=[pl.BlockSpec(memory_space=pltpu.SMEM), vmem, vmem] + ([anywhere] * 3 + [vmem] * 5 if routed else [anywhere]),
        out_specs=[anywhere] * len(whole) + [vmem] * 13,
        scratch_shapes=[
            pltpu.VMEM((long, MODEL_WIDTH), BF16),
            pltpu.VMEM((ALL, HEAD_SIZE), F32),
            pltpu.VMEM((ALL, HEAD_SIZE), F32),
            pltpu.VMEM((KW - 1, ALL, HEAD_SIZE), F32),
            pltpu.VMEM((ALL, ALL), F32),
            pltpu.VMEM((ALL, ALL), F32),
            pltpu.VMEM((ALL, ALL), jnp.int32),
            pltpu.VMEM(states, F32),
            pltpu.VMEM((ALL, MODEL_WIDTH), F32),
            pltpu.VMEM((HEADS, ALL, ALL), BF16),
            pltpu.VMEM((ALL, MODEL_WIDTH), BF16),
            pltpu.VMEM(states, BF16),
            pltpu.VMEM(states, BF16),
            dma((HEADS,)),
            dma((HEADS,)),
            pltpu.VMEM((MODEL_WIDTH, MIX), BF16),
            pltpu.VMEM((MODEL_WIDTH, SMALL), BF16),
            pltpu.VMEM((ROWS * EDGE, MODEL_WIDTH), BF16),
            dma((ROWS,)),
            dma((ROWS,)),
            dma((MIX // WIDE + 1,)),
            pltpu.VMEM((long, MIX), F32),
        ] + routes,
        compiler_params=pltpu.CompilerParams(
            collective_id=1, has_side_effects=True, vmem_limit_bytes=56 * 2**20
        ),
        name="mixer_forward",
    )(starts, tokens, head_gain, *weights)
    return results if routed else [weights[0]] + list(results)


def mixer_backward_kernel(routed, *refs):
    (starts, grad_gated, grad_mid, tokens, gains, full, conv, head_gain), refs = refs[:8], refs[8:]
    (pre, raw, beta, solved, solved_w, fresh, state, power, outputs), refs = refs[:9], refs[9:]
    if routed:
        (normed_t, grad_mlp, grads), refs = refs[:3], refs[3:]
        (grad_hidden, *targets), refs = refs[:4], refs[4:]
        (mix_sum, small_sum, head_sum), refs = refs[:3], refs[3:]
        (grad_project, grad_logits, grad_conv, grad_head, grad_gain), refs = refs[:5], refs[5:]
    else:
        (grad_hidden, grad_project, grad_logits, grad_conv, grad_head, grad_gain), refs = refs[:6], refs[6:]
    (carry_in, carry_out, taps, within, below), refs = refs[:5], refs[5:]
    (grad_out, grad_raw, grad_beta, arriving, leaving, halo_out, halo_in), refs = refs[:7], refs[7:]
    (send, receive, halo_send, halo_receive, mix, load_sem), refs = refs[:6], refs[6:]
    fresh_part, offset = grad_hidden, grad_raw
    small = mix.at[:, pl.ds(AT_SMALL, SMALL)]
    count = lax.axis_size("seq")
    index = lax.axis_index("seq")
    first = index * TOKENS
    sums = after = iter(())
    if routed:
        at = Place(count // 2)
        at.greet(-1)
        parts, by_level, part_sem, level_sem, head_sends = refs[:5]
        refs = refs[5:]
        out_sum, up_sum, down_sum = targets
        cut = HALF_REST - MODEL_WIDTH
        sums = scatter_steps(
            at, (0, HALF_REST), HALF_REST, grads, ((out_sum, 0, MODEL_WIDTH), (up_sum, 0, cut)), *refs[:11]
        )
        after = scatter_steps(
            at, (HALF_REST, HALF_REST), HALF_REST, grads, ((up_sum, cut, 2 * FF - cut), (down_sum, 0, FF)), *refs[11:22]
        )
        until(sums, "started")
    else:
        barrier = pltpu.get_barrier_semaphore()

        @pl.when(index + 1 < count)
        def _():
            pl.semaphore_signal(barrier, inc=1, device_id={"seq": index + 1}, device_id_type=MESH)

        @pl.when(index > 0)
        def _():
            pl.semaphore_wait(barrier, 1)

    load_mix = pltpu.make_async_copy(full.at[:, pl.ds(0, AT_OUT)], mix, load_sem)
    load_mix.start()

    @pl.when(index + 1 == count)
    def _():
        arriving[...] = jnp.zeros_like(arriving)
        halo_in[...] = jnp.zeros_like(halo_in)

    fill_masks(starts, first, carry_in, carry_out, taps, within, below)
    grad_head[...] = jnp.zeros_like(grad_head)
    grad_beta[...] = jnp.zeros_like(grad_beta)

    def active_of(part, head):
        values = raw[:, head_columns(part, head)].astype(F32)
        return values * jax.nn.sigmoid(values)

    def prepare(head):
        columns = head_columns(0, head)
        gate_columns = head_columns(3, head)
        gate = pre[pl.ds(0, ALL), gate_columns].astype(F32)
        sigma = jax.nn.sigmoid(gate)
        output = outputs[:, columns]
        scale = lax.rsqrt(jnp.mean(output * output, axis=-1, keepdims=True) + HEAD_ZERO)
        sample = output * scale
        incoming = grad_gated[:, columns]
        gain = head_gain[...].astype(F32)
        grad_project[:, gate_columns] = low(incoming * sample * gain * (sigma * (1.0 + gate * (1.0 - sigma))))
        grad_sample = incoming * (gate * sigma)
        grad_head[0:1, :] += jnp.sum(grad_sample * sample, axis=0, keepdims=True)
        scaled = grad_sample * gain
        mean = jnp.mean(scaled * output, axis=-1, keepdims=True)
        here = low(scale * scaled - output * (scale * scale * scale * mean))
        grad_out[:, columns] = here
        active_q, active_k = active_of(0, head), active_of(1, head)
        query = active_q * (unit_scale(active_q) * HEAD_SIZE**-0.5)
        key = active_k * unit_scale(active_k)
        attend = low(within[...] * nt(low(query), low(key)))
        part = tn(attend, here)
        fresh_part[:, columns] = part
        entering = low(carry_in[...] * query)
        part_low = low(part)
        w = solved_w[:, columns]
        for row in range(ROWS):
            span = slice(row * TOKENS, (row + 1) * TOKENS)
            offset[span, columns] = tn(entering[span], here[span]) - tn(w[span], part_low[span])

    for head in range(HEADS):
        prepare(head)
        advance(sums, AT_PREPARE)

    def copy(head):
        return pltpu.make_async_remote_copy(
            src_ref=leaving.at[head], dst_ref=arriving.at[head], send_sem=send.at[head], recv_sem=receive.at[head],
            device_id={"seq": index - 1}, device_id_type=MESH,
        )

    def chain(head):
        @pl.when(index + 1 < count)
        def _():
            copy(head).wait_recv()

        @pl.when(index > 0)
        def _():
            for row in range(ROWS):
                start = offset[pl.ds(row * TOKENS, TOKENS), head_columns(0, head)]
                leaving[head, row] = low(tn(power[head, row], arriving[head, row]) + start)
            copy(head).start()

    until(after, "started")
    both_advance(AT_CHAIN, sums, after)
    more = iter(())
    if routed:
        sender = Sender(head_sends)

        def exchange(number, value, row, spot):
            parts[2 * number] = value
            device = {"dp": row, "seq": spot}
            sender.start(None, parts.at[2 * number], parts.at[2 * number + 1], device, part_sem.at[number])
            return lambda: sender.arrived(None, parts.at[2 * number + 1], device, part_sem.at[number])

        pending = exchange(0, grad_head[...], at.row, at.sibling)

    for head in range(HEADS):
        chain(head)

    def finish(head):
        columns = head_columns(0, head)
        raw_q, raw_k = raw[:, columns].astype(F32), raw[:, head_columns(1, head)].astype(F32)
        raw_v = raw[:, head_columns(2, head)].astype(F32)
        sigma_q, sigma_k, sigma_v = jax.nn.sigmoid(raw_q), jax.nn.sigmoid(raw_k), jax.nn.sigmoid(raw_v)
        active_q, active_k, values = raw_q * sigma_q, raw_k * sigma_k, raw_v * sigma_v
        scale_q, scale_k = unit_scale(active_q), unit_scale(active_k)
        query = low(active_q * (scale_q * HEAD_SIZE**-0.5))
        key_full = active_k * scale_k
        key = low(key_full)
        enter, leave = carry_in[...], carry_out[...]
        strength = lane_of(beta[...], BETA_AT + head)
        here = grad_out[:, columns]
        x = fresh[:, columns]
        leaving_keys = low(leave * key_full)
        grad_x = fresh_part[:, columns] + per_row(lambda row, part: nn(part, arriving[head, row]), leaving_keys)
        y = tn(solved[head], low(grad_x))
        y_low = low(y)
        grad_attend = low(within[...] * nt(here, x))
        gram = nt(key, key)
        grad_system = -below[...] * nt(y_low, x)
        grad_gram = low(strength * grad_system)
        grad_q = nn(grad_attend, key) + enter * per_row(lambda row, part: nt(part, state[head, row]), here)
        grad_k = (
            tn(grad_attend, query)
            + leave * per_row(lambda row, part: nt(part, arriving[head, row]), x)
            + nn(grad_gram, key)
            + tn(grad_gram, key)
            - strength * enter * per_row(lambda row, part: nt(part, state[head, row]), y_low)
        )
        z = values - enter * per_row(lambda row, part: nn(part, state[head, row]), key)
        grad_v = strength * y
        grad_strength = jnp.sum(y * z, axis=-1, keepdims=True) + jnp.sum(grad_system * gram, axis=-1, keepdims=True)
        lanes = lax.broadcasted_iota(jnp.int32, grad_beta.shape, 1)
        grad_beta[...] = jnp.where(lanes == BETA_AT + head, grad_strength, grad_beta[...])

        def through(grad, active, scale, part, sigma, extra):
            grad = grad * extra
            mean = jnp.sum(active * grad, axis=-1, keepdims=True)
            grad = scale * grad - active * (scale * scale * scale * mean)
            return grad * (sigma * (1.0 + part * (1.0 - sigma)))

        grad_raw[:, columns] = through(grad_q, active_q, scale_q, raw_q, sigma_q, HEAD_SIZE**-0.5)
        grad_raw[:, head_columns(1, head)] = through(grad_k, active_k, scale_k, raw_k, sigma_k, 1.0)
        grad_raw[:, head_columns(2, head)] = grad_v * (sigma_v * (1.0 + raw_v * (1.0 - sigma_v)))

    for head in range(HEADS):
        finish(head)
        both_advance(AT_FINISH, sums, after)

    def convolve_back(step, _):
        columns = pl.ds(pl.multiple_of(step * HEAD_SIZE, HEAD_SIZE), HEAD_SIZE)
        weight = conv[:, columns]
        nothing = jnp.zeros((HALO, HEAD_SIZE), F32)
        sums = [jnp.zeros((1, HEAD_SIZE), F32) for _ in range(KW)]
        early = []
        for row in range(ROWS):
            span = pl.ds(row * TOKENS, TOKENS)
            grad = grad_raw[span, columns]
            main = pre[span, columns].astype(F32)
            edge = pre[pl.ds(ALL + row * EDGE, EDGE), columns].astype(F32)
            longer = padded(main, edge[EDGE - HALO :])
            total = weight[0:1] * jnp.concatenate([nothing, grad], axis=0)
            sums[0] = sums[0] + jnp.sum(grad * main, axis=0, keepdims=True)
            for shift in range(1, KW):
                masked = grad * taps[shift - 1, span, :]
                wide = jnp.concatenate([nothing, masked, nothing], axis=0)
                total = total + weight[shift : shift + 1] * wide[shift : shift + HALO + TOKENS]
                before = longer[HALO - shift : HALO - shift + TOKENS]
                sums[shift] = sums[shift] + jnp.sum(masked * before, axis=0, keepdims=True)
            early.append(total[:HALO])
            grad_raw[span, columns] = total[HALO:]
        halo_out[:, columns] = low(jnp.concatenate(early, axis=0))
        grad_conv[:, columns] = jnp.concatenate(sums, axis=0)
        return 0

    for part in range(3):
        lax.fori_loop(part * HEADS, (part + 1) * HEADS, convolve_back, 0)
        both_advance(AT_CONV, sums, after)
    back = pltpu.make_async_remote_copy(
        src_ref=halo_out, dst_ref=halo_in, send_sem=halo_send, recv_sem=halo_receive,
        device_id={"seq": index - 1}, device_id_type=MESH,
    )

    @pl.when(index > 0)
    def _():
        back.start()

    strengths = beta[...]
    grad_logits[...] = low(grad_beta[...] * strengths * (1.0 - strengths))

    @pl.when(index + 1 < count)
    def _():
        back.wait_recv()

    for row in range(ROWS):
        end = pl.ds((row + 1) * TOKENS - HALO, HALO)
        grad_raw[end, :] += halo_in[...].astype(F32)[row * HALO : (row + 1) * HALO]

    def narrow(step, _):
        rows = pl.ds(pl.multiple_of(step * 32, 32), 32)
        grad_project[rows, pl.ds(0, QKV)] = low(grad_raw[rows, :])
        return 0

    lax.fori_loop(0, ALL // 32, narrow, 0)

    load_mix.wait()
    both_advance(AT_NORMED, sums, after)

    def normed_back(step, _):
        rows = pl.ds(pl.multiple_of(step * 256, 256), 256)
        grad_hidden[:, rows] = nt(grad_project[...], mix[rows, pl.ds(0, MIX)]) + nt(grad_logits[...], small[rows, :])
        return 0

    lax.fori_loop(0, MODEL_WIDTH // 256, normed_back, 0)
    grad_gain[...] = jnp.zeros_like(grad_gain)

    def hidden_back(step, _):
        rows = pl.ds(pl.multiple_of(step * 32, 32), 32)
        hidden = tokens[rows, :].astype(F32)
        scale = lax.rsqrt(jnp.mean(hidden * hidden, axis=-1, keepdims=True) + NEAR_ZERO)
        grad = grad_hidden[rows, :]
        grad_gain[...] += jnp.sum(grad * hidden * scale, axis=0, keepdims=True)
        scaled = grad * gains[0:1, :]
        mean = jnp.mean(scaled * hidden, axis=-1, keepdims=True)
        grad_hidden[rows, :] = grad_mid[rows, :] + scale * scaled - hidden * (scale * scale * scale * mean)
        return 0

    lax.fori_loop(0, ALL // 32, hidden_back, 0)
    if routed:
        turned = grad_raw.at[pl.ds(0, HEAD_SIZE), pl.ds(0, MODEL_WIDTH)]
        turned[...] = jnp.zeros_like(turned)
        turned[0:1, :] = grad_gain[...]
        turned[1:2, :] = grad_mlp[...]
        move = tap_moves()
        for block in range(MODEL_WIDTH // HEAD_SIZE):
            wide = nt(low(grad_conv[:, pl.ds(block * 3 * HEAD_SIZE, 3 * HEAD_SIZE)]), move)
            lanes = pl.ds(block * HEAD_SIZE, HEAD_SIZE)
            for tap in range(KW):
                for third in range(3):
                    place = CONV_AT + 3 * tap + third
                    turned[place : place + 1, lanes] = wide[tap : tap + 1, third * HEAD_SIZE : (third + 1) * HEAD_SIZE]

        def weigh(tile, _):
            columns = pl.ds(pl.multiple_of(tile * 256, 256), 256)
            mix[:, columns] = low(nn(normed_t[...], grad_project[:, columns]))
            return 0

        lax.fori_loop(0, MIX // 256, weigh, 0)
        mix[:, pl.ds(AT_SMALL, SMALL)] = low(nn(normed_t[...], grad_logits[...]) + turned[...].T)
        more = scatter_steps(
            at, (0, AT_OUT), CHUNK_MIX, mix, ((mix_sum, 0, MIX), (small_sum, 0, SMALL)), *refs[22:]
        )
        until(more, "started")
        for number, (row, spot) in enumerate(((at.near, at.spot), (at.far, at.spot))):
            both_advance(AT_END, sums, after, more)
            pending()
            value = parts[2 * number] + parts[2 * number + 1]
            pending = exchange(number + 1, value, row, spot)
        both_advance(AT_END, sums, after, more)
        pending()
        by_level[at.level] = parts[4] + parts[5]
        here = {"dp": at.near, "seq": at.spot}

        def pass_on(condition, up, source):
            device = {"dp": at.row, "seq": at.spot + 2 if up else at.spot - 2}
            sender.start(condition, by_level.at[source], by_level.at[source], device, level_sem.at[source])

        pass_on(at.above, True, at.level)
        pass_on(at.below, False, at.level)
        for step in range(1, at.levels):
            both_advance(AT_END, sums, after, more)
            for condition, source, up, onward in (
                (at.level - step >= 0, at.level - step, True, at.above),
                (at.level + step < at.levels, at.level + step, False, at.below),
            ):
                sender.arrived(condition, by_level.at[source], here, level_sem.at[source])
                if step < at.levels - 1:
                    pass_on(condition & onward, up, source)
        value = by_level[0]
        for level in range(1, at.levels):
            value = value + by_level[level]
        head_sum[...] = jnp.broadcast_to(jnp.sum(value, axis=0, keepdims=True), value.shape)
        for _ in range(12):
            both_advance(AT_END, sums, after, more)
        until(sums, "end")
        until(after, "end")
        until(more, "end")
        sender.drain()

    @pl.when(index > 0)
    def _():
        back.wait_send()

        def drain(head, _):
            copy(head).wait_send()
            return 0

        lax.fori_loop(0, HEADS, drain, 0)


def mixer_backward(operands, normed, grad_mlp, grads, routed):
    vmem, anywhere = pl.BlockSpec(memory_space=pltpu.VMEM), pl.BlockSpec(memory_space=pl.ANY)
    dma = pltpu.SemaphoreType.DMA
    shape = jax.ShapeDtypeStruct
    states = (HEADS, ROWS, HEAD_SIZE, HEAD_SIZE)
    levels = lax.axis_size("seq") // 2
    local = [
        ((ALL, MIX), BF16),
        ((ALL, SMALL), BF16),
        ((KW, QKV), F32),
        ((8, HEAD_SIZE), F32),
        ((1, MODEL_WIDTH), F32),
    ]
    scratch = [
        pltpu.VMEM((ALL, HEAD_SIZE), F32),
        pltpu.VMEM((ALL, HEAD_SIZE), F32),
        pltpu.VMEM((KW - 1, ALL, HEAD_SIZE), F32),
        pltpu.VMEM((ALL, ALL), F32),
        pltpu.VMEM((ALL, ALL), F32),
        pltpu.VMEM((ALL, MODEL_WIDTH), BF16),
        pltpu.VMEM((ALL, QKV), F32),
        pltpu.VMEM((ALL, SMALL), F32),
        pltpu.VMEM(states, BF16),
        pltpu.VMEM(states, BF16),
        pltpu.VMEM((ROWS * HALO, QKV), BF16),
        pltpu.VMEM((ROWS * HALO, QKV), BF16),
        dma((HEADS,)),
        dma((HEADS,)),
        dma,
        dma,
        pltpu.VMEM((MODEL_WIDTH, AT_OUT), BF16),
        dma,
    ]
    more = []
    out_shape = [shape((ALL, MODEL_WIDTH), F32)]
    if routed:
        more = [normed, grad_mlp, grads]
        out_shape += [shape((2 * PIECE, width), F32) for width in (MODEL_WIDTH, 2 * FF, FF, MIX, SMALL)]
        out_shape += [shape((8, HEAD_SIZE), F32)]
        scratch = [pltpu.VMEM(*entry) for entry in local] + scratch
        scratch += [
            pltpu.VMEM((6, 8, HEAD_SIZE), F32),
            pltpu.VMEM((levels, 8, HEAD_SIZE), F32),
            dma((3,)),
            dma((levels,)),
            dma((3 + 2 * levels,)),
        ]
        scratch += scatter_buffers(levels, HALF_REST, True) + scatter_buffers(levels, HALF_REST, True)
        scratch += scatter_buffers(levels, AT_OUT, False)
    else:
        out_shape += [shape(*entry) for entry in local]
    in_specs = [pl.BlockSpec(memory_space=pltpu.SMEM)] + [vmem] * 4 + [anywhere] + [vmem] * 11
    in_specs += [vmem, vmem, anywhere] if routed else []
    return pl.pallas_call(
        functools.partial(mixer_backward_kernel, routed),
        out_shape=out_shape,
        in_specs=in_specs,
        out_specs=[vmem] * len(out_shape),
        scratch_shapes=scratch,
        compiler_params=pltpu.CompilerParams(
            collective_id=2, has_side_effects=True, vmem_limit_bytes=63 * 2**20
        ),
        name="mixer_backward",
    )(*operands, *more)


TILE = 256
HANDS = 32
OWN = FF // HANDS
GROUP_ROWS = 4 * OWN


def pack_hand(source, begin, store):
    for half in range(2):
        for lane in range(2):
            for step in range(11):
                rows = slice(begin + step * 8, begin + step * 8 + 8)
                first = (4 * half + lane) * 128
                second = (4 * half + 2 + lane) * 128
                pair = jnp.concatenate([source[rows, first : first + 128], source[rows, second : second + 128]], axis=0)
                store(half * PIECE, (lane * 11 + step) * 128, pair)


def mlp_kernel(
    full, tokens, cotangent, gated, gains,
    output, grad_mid, grad_gated, grad_gain, grads,
    out_w, up_w, packed, wide, down_w, hidden, normed, total, grad_normed,
    normed_t, gated_t, acted_t, up_stage, stage, load_sem, up_sem, store_sem, stage_sem,
):
    def load(number):
        columns, target = (
            (pl.ds(AT_OUT, MODEL_WIDTH), out_w),
            (pl.ds(AT_DOWN, FF), packed),
        )[number]
        return pltpu.make_async_copy(full.at[:, columns], target, load_sem.at[number])

    def load_up(tile, side):
        begin = pl.multiple_of(side * FF + tile * TILE, TILE)
        source = full.at[:, pl.ds(pl.multiple_of(AT_UP + begin, 128), TILE)]
        return pltpu.make_async_copy(source, up_w.at[:, pl.ds(begin, TILE)], up_sem.at[side, tile])

    load(1).start()
    load(0).start()

    def start_up(tile, _):
        load_up(tile, 0).start()
        load_up(tile, 1).start()
        return 0

    lax.fori_loop(0, FF // TILE, start_up, 0)
    load(1).wait()

    def unpack(hand, _):
        for half in range(2):
            rows = pl.ds(pl.multiple_of((hand * 2 + half) * PIECE, PIECE), PIECE)
            piece = packed[rows, :].astype(F32)
            for lane in range(2):
                for step in range(11):
                    source = (lane * 11 + step) * 128
                    target = pl.ds(pl.multiple_of(hand * OWN + step * 8, 8), 8)
                    for top in range(2):
                        column = (4 * half + 2 * top + lane) * 128
                        wide[target, column : column + 128] = piece[top * 8 : top * 8 + 8, source : source + 128]
        return 0

    lax.fori_loop(0, HANDS, unpack, 0)

    def narrow(tile, _):
        rows = pl.ds(pl.multiple_of(tile * TILE, TILE), TILE)
        down_w[rows, :] = low(wide[rows, :])
        return 0

    lax.fori_loop(0, FF // TILE, narrow, 0)
    load(0).wait()
    gated_t[...] = low(gated[...].astype(F32).T)
    middle = tokens[...].astype(F32) + nn(gated[...], out_w[...])
    hidden[...] = middle
    inverse = lax.rsqrt(jnp.mean(middle * middle, axis=-1, keepdims=True) + NEAR_ZERO)
    value = middle * inverse * gains[1:2, :]
    normed[...] = low(value)
    normed_t[...] = low(value.T)
    total[...] = jnp.zeros_like(total)
    grad_normed[...] = jnp.zeros_like(grad_normed)

    def store_up(tile, slot, side):
        begin = pl.multiple_of(MODEL_WIDTH + side * FF + tile * TILE, TILE)
        return pltpu.make_async_copy(up_stage.at[slot, side], grads.at[:, pl.ds(begin, TILE)], store_sem.at[slot, side])

    def tile_step(tile, _):
        slot = lax.rem(tile, 2)
        here = pl.ds(pl.multiple_of(tile * TILE, TILE), TILE)
        there = pl.ds(pl.multiple_of(FF + tile * TILE, TILE), TILE)
        load_up(tile, 0).wait()
        load_up(tile, 1).wait()

        @pl.when(tile >= 2)
        def _():
            store_up(tile - 2, slot, 0).wait()
            store_up(tile - 2, slot, 1).wait()

        gate = nn(normed[...], up_w[:, here])
        up = nn(normed[...], up_w[:, there])
        grad = nt(cotangent[...], down_w[here, :])
        sigma = jax.nn.sigmoid(gate)
        soft = gate * sigma
        acted = soft * up
        acted_low = low(acted)
        acted_t[here, :] = low(acted.T)
        total[...] += nn(acted_low, down_w[here, :])
        grad_gate = low(grad * up * (sigma * (1.0 + gate * (1.0 - sigma))))
        grad_up = low(grad * soft)
        grad_normed[...] += nt(grad_gate, up_w[:, here]) + nt(grad_up, up_w[:, there])
        up_stage[slot, 0] = low(nn(normed_t[...], grad_gate))
        up_stage[slot, 1] = low(nn(normed_t[...], grad_up))
        store_up(tile, slot, 0).start()
        store_up(tile, slot, 1).start()
        return 0

    tiles = FF // TILE
    lax.fori_loop(0, tiles, tile_step, 0)
    middle = hidden[...]
    output[...] = low(middle + total[...])
    inverse = lax.rsqrt(jnp.mean(middle * middle, axis=-1, keepdims=True) + NEAR_ZERO)
    grad = grad_normed[...]
    grad_gain[...] = jnp.sum(grad * middle * inverse, axis=0, keepdims=True)
    scaled = grad * gains[1:2, :]
    mean = jnp.mean(scaled * middle, axis=-1, keepdims=True)
    grad = cotangent[...].astype(F32) + inverse * scaled - middle * (inverse * inverse * inverse * mean)
    grad_mid[...] = grad
    grad_low = low(grad)
    grad_gated[...] = nt(grad_low, out_w[...])
    for last in range(2):
        tile = tiles - 2 + last
        for side in range(2):
            store_up(tile, tile % 2, side).wait()

    def store_out(tile):
        slot, side = divmod(tile, 2)
        columns = pl.ds(tile * TILE, TILE)
        return pltpu.make_async_copy(up_stage.at[slot, side], grads.at[:, columns], store_sem.at[slot, side])

    for tile in range(MODEL_WIDTH // TILE):
        slot, side = divmod(tile, 2)
        up_stage[slot, side] = low(nn(gated_t[...], grad_low[:, tile * TILE : (tile + 1) * TILE]))
        store_out(tile).start()

    def store_down(group, slot):
        rows = pl.ds(pl.multiple_of(group * 128, 128), 128)
        target = grads.at[rows, pl.ds(MODEL_WIDTH + 2 * FF, FF)]
        return pltpu.make_async_copy(stage.at[slot], target, stage_sem.at[slot])

    def down_step(group, _):
        slot = lax.rem(group, 2)

        @pl.when(group >= 2)
        def _():
            store_down(group - 2, slot).wait()

        rows = pl.ds(pl.multiple_of(group * GROUP_ROWS, GROUP_ROWS), GROUP_ROWS)
        wide[pl.ds(0, GROUP_ROWS), :] = nn(acted_t[rows, :], cotangent[...])
        for hand in range(4):

            def store(row, column, value, hand=hand):
                stage[slot, hand * 2 * PIECE + row : hand * 2 * PIECE + row + PIECE, column : column + 128] = low(value)

            pack_hand(wide, hand * OWN, store)
        store_down(group, slot).start()
        return 0

    groups = HANDS // 4
    lax.fori_loop(0, groups, down_step, 0)
    for group in (groups - 2, groups - 1):
        store_down(group, group % 2).wait()
    for tile in range(MODEL_WIDTH // TILE):
        store_out(tile).wait()


def mlp(full, tokens, cotangent, gated, gains):
    vmem, anywhere = pl.BlockSpec(memory_space=pltpu.VMEM), pl.BlockSpec(memory_space=pl.ANY)
    dma = pltpu.SemaphoreType.DMA
    shape = jax.ShapeDtypeStruct
    return pl.pallas_call(
        mlp_kernel,
        out_shape=[
            shape((ALL, MODEL_WIDTH), BF16),
            shape((ALL, MODEL_WIDTH), F32),
            shape((ALL, MODEL_WIDTH), F32),
            shape((1, MODEL_WIDTH), F32),
            shape((MODEL_WIDTH, PACK - AT_OUT), BF16),
        ],
        in_specs=[anywhere] + [vmem] * 4,
        out_specs=[vmem] * 4 + [anywhere],
        scratch_shapes=[
            pltpu.VMEM((MODEL_WIDTH, MODEL_WIDTH), BF16),
            pltpu.VMEM((MODEL_WIDTH, 2 * FF), BF16),
            pltpu.VMEM((MODEL_WIDTH, FF), BF16),
            pltpu.VMEM((FF, MODEL_WIDTH), F32),
            pltpu.VMEM((FF, MODEL_WIDTH), BF16),
            pltpu.VMEM((ALL, MODEL_WIDTH), F32),
            pltpu.VMEM((ALL, MODEL_WIDTH), BF16),
            pltpu.VMEM((ALL, MODEL_WIDTH), F32),
            pltpu.VMEM((ALL, MODEL_WIDTH), F32),
            pltpu.VMEM((MODEL_WIDTH, ALL), BF16),
            pltpu.VMEM((MODEL_WIDTH, ALL), BF16),
            pltpu.VMEM((FF, ALL), BF16),
            pltpu.VMEM((2, 2, MODEL_WIDTH, TILE), BF16),
            pltpu.VMEM((2, 128, FF), BF16),
            dma((2,)),
            dma((2, FF // TILE)),
            dma((2, 2)),
            dma((2,)),
        ],
        compiler_params=pltpu.CompilerParams(vmem_limit_bytes=60 * 2**20),
        name="mlp",
    )(full, tokens, cotangent, gated, gains)


def result_kernel(
    hidden, mix, out, up, down, small, head,
    hidden_to, mixer_to, mix_to, conv_to, beta_to, head_to, out_to, mlp_to, up_to, down_to,
):
    for source, target in ((mix, mix_to), (out, out_to), (up, up_to)):
        target[...] = source[...]

    def move(step, _):
        rows = pl.ds(pl.multiple_of(step * 32, 32), 32)
        hidden_to[rows, :] = hidden[rows, :]
        return 0

    lax.fori_loop(0, ALL // 32, move, 0)
    for group in range(4):
        for lane in range(2):
            for step in range(11):
                source = (lane * 11 + step) * 128
                target = (2 * group + lane) * 128
                down_to[step * 8 : step * 8 + 8, target : target + 128] = down[
                    group * 8 : group * 8 + 8, source : source + 128
                ]
    values = small[...]
    beta_to[...] = values[:, BETA_AT:CONV_AT]
    turned = jnp.concatenate([values, jnp.zeros((SMALL - 2 * PIECE, SMALL), F32)], axis=0).T
    mixer_to[...] = turned[0:1, : 2 * PIECE]
    mlp_to[...] = turned[1:2, : 2 * PIECE]
    for tap in range(KW):
        for third in range(3):
            place = CONV_AT + 3 * tap + third
            conv_to[tap : tap + 1, third * 2 * PIECE : (third + 1) * 2 * PIECE] = turned[place : place + 1, : 2 * PIECE]
    head_to[...] = head[0:1, :]


def result(hidden, mix, out, up, down, small, head):
    vmem = pl.BlockSpec(memory_space=pltpu.VMEM)
    shape = jax.ShapeDtypeStruct
    share = 2 * PIECE
    return pl.pallas_call(
        result_kernel,
        out_shape=[
            shape(hidden.shape, F32),
            shape((1, share), F32),
            shape(mix.shape, F32),
            shape((KW, 3 * share), F32),
            shape((share, HEADS), F32),
            shape((1, HEAD_SIZE), F32),
            shape(out.shape, F32),
            shape((1, share), F32),
            shape(up.shape, F32),
            shape((OWN, MODEL_WIDTH), F32),
        ],
        in_specs=[vmem] * 7,
        out_specs=[vmem] * 10,
        name="result",
    )(hidden, mix, out, up, down, small, head)


def pack_down(part):
    lead = part.shape[:-2]
    tiles = part.reshape(lead + (11, 8, 4, 2, 128))
    n = len(lead)
    moved = tiles.transpose(tuple(range(n)) + (n + 2, n + 1, n + 3, n, n + 4))
    return moved.reshape(lead + (2 * PIECE, FF))


def unpack_down(part):
    lead = part.shape[:-2]
    tiles = part.reshape(lead + (4, 8, 2, 11, 128))
    n = len(lead)
    moved = tiles.transpose(tuple(range(n)) + (n + 3, n + 1, n, n + 2, n + 4))
    return moved.reshape(lead + (OWN, MODEL_WIDTH))


def pack_taps(conv):
    taps = conv.reshape(KW, -1, 3, 2 * PIECE)
    return taps.transpose(1, 3, 0, 2).reshape(-1, 3 * KW)


def pack_small(mixer, mlp_part, beta, conv):
    parts = jnp.concatenate([mixer[:, None], mlp_part[:, None], beta, pack_taps(conv)], axis=1)
    return jnp.pad(parts, ((0, 0), (0, SMALL - parts.shape[1])))


def shards(
    tokens, cotangent, starts, mixer_gain, mix_weight, conv_weight, beta_weight, head_gain, out_weight, mlp_gain,
    upgate_weight, down_weight,
):
    rows, block, width = tokens.shape
    share = mix_weight.shape[1]
    both = ("dp", "seq")
    routed = lax.axis_size("dp") == 4 and lax.axis_size("seq") % 2 == 0 and share == 2 * PIECE
    if routed:
        weights = [
            mix_weight[0], out_weight[0], upgate_weight[0], down_weight[0], mixer_gain, mlp_gain, beta_weight[0],
            conv_weight[0],
        ]
    else:
        parts = [
            mixer_gain[0], mlp_gain[0], beta_weight[0], conv_weight[0].T, mix_weight[0], out_weight[0], upgate_weight[0],
            down_weight[0],
        ]
        parts = [lax.all_gather(part, both, axis=0, tiled=True) for part in parts]
        mixer_w, mlp_w, beta_w, conv_w, mix_w, out_w, up_w, down_w = parts
        small_w = pack_small(mixer_w, mlp_w, beta_w, conv_w.T)
        down_w = pack_down(down_w.reshape(-1, OWN, width)).reshape(-1, FF)
        weights = [jnp.concatenate([mix_w, small_w, out_w, up_w, down_w], axis=1)]

    flat = tokens.reshape(rows * block, width)
    flat_grad = cotangent.reshape(rows * block, width)
    full, normed, pre, raw, beta, solved, solved_w, fresh, state, power, outputs, gated, conv, gains = mixer_forward(
        starts, flat, head_gain, weights
    )
    output, grad_mid, grad_gated, grad_mlp, grads = mlp(full, flat, flat_grad, gated, gains)
    operands = [
        starts, grad_gated, grad_mid, flat, gains, full, conv, head_gain,
        pre, raw, beta, solved, solved_w, fresh, state, power, outputs,
    ]
    results = mixer_backward(operands, normed, grad_mlp, grads, routed)
    if routed:
        grad_hidden, out_sum, up_sum, down_sum, mix_sum, small_sum, head_sum = results
        parts = result(grad_hidden, mix_sum, out_sum, up_sum, down_sum, small_sum, head_sum)
        grad_hidden, mixer_mine, mix_mine, conv_mine, beta_mine, head_mine, out_mine, mlp_mine, up_mine, down_mine = parts
        mixer_mine, mlp_mine = mixer_mine[0], mlp_mine[0]
    else:
        grad_hidden, grad_project, grad_logits, grad_conv, grad_head, grad_mixer = results
        whole_mix = lax.dot_general(normed, grad_project, (((1,), (0,)), ((), ())), preferred_element_type=F32)
        whole_beta = lax.dot_general(normed, grad_logits, (((1,), (0,)), ((), ())), preferred_element_type=F32)
        whole_down = unpack_down(grads[:, MODEL_WIDTH + 2 * FF :].reshape(-1, 2 * PIECE, FF)).reshape(FF, width)
        listed = [
            whole_mix,
            grads[:, :MODEL_WIDTH],
            grads[:, MODEL_WIDTH : MODEL_WIDTH + 2 * FF],
            whole_down,
            grad_mixer[0],
            grad_mlp[0],
            whole_beta[:, BETA_AT:CONV_AT],
            grad_conv.T,
        ]
        listed = [
            lax.psum_scatter(part.astype(F32), both, scatter_dimension=0, tiled=True) for part in listed
        ]
        mix_mine, out_mine, up_mine, down_mine, mixer_mine, mlp_mine, beta_mine, conv_mine = listed
        conv_mine = conv_mine.T
        head_mine = lax.psum(jnp.sum(grad_head, axis=0, keepdims=True), both)
    return (
        output.reshape(rows, block, width),
        grad_hidden.reshape(rows, block, width),
        mixer_mine[None],
        mix_mine[None],
        conv_mine[None],
        beta_mine[None],
        head_mine,
        out_mine[None],
        mlp_mine[None],
        up_mine[None],
        down_mine[None],
    )


def solution(mesh):
    both = ("dp", "seq")
    in_specs = (
        P("dp", "seq", None),
        P("dp", "seq", None),
        P("dp", None),
        P(None, both),
        P(None, both, None),
        P(None, None, both),
        P(None, both, None),
        P(),
        P(None, both, None),
        P(None, both),
        P(None, both, None),
        P(None, both, None),
    )
    out_specs = (
        P("dp", "seq", None),
        P("dp", "seq", None),
        P(None, both),
        P(None, both, None),
        P(None, None, both),
        P(None, both, None),
        P(),
        P(None, both, None),
        P(None, both),
        P(None, both, None),
        P(None, both, None),
    )
    return jax.shard_map(shards, mesh=mesh, in_specs=in_specs, out_specs=out_specs, check_vma=False)
```

```python
import functools

import jax
import jax.numpy as jnp
from jax import lax
from jax.experimental import pallas as pl
from jax.experimental.pallas import tpu as pltpu
from jax.sharding import PartitionSpec as P

MODEL_WIDTH = 1024
HEADS = 8
HEAD_SIZE = 128
FF = 2816
KW = 4
PACKED = 4

MESH = pl.DeviceIdType.MESH
F32 = jnp.float32
BF16 = jnp.bfloat16
TOKENS = 128
ROWS = 2
ALL = ROWS * TOKENS
HALO = 8
NEAR_ZERO = 1e-06
HEAD_ZERO = 1e-05
MIX = 4 * MODEL_WIDTH
QKV = 3 * MODEL_WIDTH
SMALL = 128
BETA_AT = 2
CONV_AT = 10
AT_SMALL = MIX
AT_OUT = AT_SMALL + SMALL
AT_UP = AT_OUT + MODEL_WIDTH
AT_DOWN = AT_UP + 2 * FF
PACK = AT_DOWN + FF
FIRST_REST = 5504
LAST_REST = PACK - AT_OUT - FIRST_REST
CHUNK_MIX = AT_OUT // 3
PIECE = 16
SLOTS = 2
WINDOW = 24
LAG = 2
EDGE = 16
WIDE = 512
GROUP = 2
AT_PREPARE = 2
AT_CHAIN = (5, 2)
AT_FINISH = (1, 2)
AT_CONV = (0, 0)
AT_NORMED = (4, 4)
AT_END = (1, 2, 3)


def nn(a, b):
    return lax.dot_general(a, b, (((1,), (0,)), ((), ())), preferred_element_type=F32)


def nt(a, b):
    return lax.dot_general(a, b, (((1,), (1,)), ((), ())), preferred_element_type=F32)


def tn(a, b):
    return lax.dot_general(a, b, (((0,), (0,)), ((), ())), preferred_element_type=F32)


def low(value):
    return value.astype(BF16)


def when(condition, action):
    if condition is None:
        action()
    else:
        pl.when(condition)(action)


class Place:
    def __init__(self, levels):
        self.levels = levels
        self.row, self.spot = lax.axis_index("dp"), lax.axis_index("seq")
        self.level, self.core = self.spot // 2, lax.rem(self.spot, 2)
        self.near = self.row + 1 - 2 * lax.rem(self.row, 2)
        self.far = self.row + 2 - 4 * (self.row // 2)
        self.first = self.near * (1 - self.core) + self.far * self.core
        self.second = self.far * (1 - self.core) + self.near * self.core
        self.both = 3 - self.row
        self.above, self.below = self.level + 1 < levels, self.level >= 1
        self.sibling = self.spot + 1 - 2 * self.core

    def greet(self, chain):
        barrier = pltpu.get_barrier_semaphore()
        levels, level, core = self.levels, self.level, self.core

        def signal(row, spot):
            pl.semaphore_signal(barrier, inc=1, device_id={"dp": row, "seq": spot}, device_id_type=MESH)

        signal(self.first, self.spot)
        signal(self.second, self.spot)
        signal(self.row, self.sibling)
        pl.when(self.above)(lambda: signal(self.row, self.spot + 2))
        pl.when(self.below)(lambda: signal(self.row, self.spot - 2))
        has_above = (2 * levels - 2 - level) // levels
        has_below = (level + levels - 1) // levels
        peers = 3 + has_above + has_below
        if chain > 0:
            pl.when(self.below & (core == 0))(lambda: signal(self.row, self.spot - 1))
            peers = peers + has_above * core
        if chain < 0:
            pl.when(self.above & (core == 1))(lambda: signal(self.row, self.spot + 1))
            peers = peers + has_below * (1 - core)
        pl.semaphore_wait(barrier, peers)

    def rows_of(self, owner, spot, half):
        return pl.ds(pl.multiple_of(((owner * 2 * self.levels + spot) * 2 + half) * PIECE, PIECE), PIECE)


class Sender:
    def __init__(self, semaphores):
        self.semaphores, self.used, self.pending = semaphores, 0, []

    def start(self, condition, source, target, device, arrival):
        copy = pltpu.make_async_remote_copy(
            src_ref=source, dst_ref=target, send_sem=self.semaphores.at[self.used], recv_sem=arrival,
            device_id=device, device_id_type=MESH,
        )
        self.used += 1
        when(condition, copy.start)
        self.pending.append((condition, copy))

    def arrived(self, condition, target, device, arrival):
        copy = pltpu.make_async_remote_copy(
            src_ref=target, dst_ref=target, send_sem=self.semaphores.at[0], recv_sem=arrival,
            device_id=device, device_id_type=MESH,
        )
        when(condition, copy.wait_recv)

    def drain(self):
        for condition, copy in self.pending:
            when(condition, copy.wait_send)


def advance(steps, count=1):
    for _ in range(count):
        next(steps, None)


def both_advance(counts, *listed):
    for steps, count in zip(listed, counts):
        advance(steps, count)


def until(steps, mark):
    for found in steps:
        if found == mark:
            return


def gather_semaphores(levels):
    dma = pltpu.SemaphoreType.DMA
    return [dma((2, 2, levels)), dma((2, levels)), dma((2, 2, levels)), dma((2, 4, levels)), dma((8 + 34 * levels,))]


def gather_steps(at, share, full, columns, by_level, by_first, by_second, by_core, sends):
    levels, row, spot, level, core = at.levels, at.row, at.spot, at.level, at.core
    first, second, both, above, below = at.first, at.second, at.both, at.above, at.below
    sender = Sender(sends)
    here = {"dp": first, "seq": spot}

    def piece(half, owner, owner_level):
        return full.at[at.rows_of(owner, owner_level * 2 + core, half), columns]

    def send(condition, half, owner, owner_level, device, arrival):
        target = piece(half, owner, owner_level)
        own = owner is row and owner_level is level
        source = share.at[pl.ds(half * PIECE, PIECE), columns] if own else target
        sender.start(condition, source, target, device, arrival)

    def along(condition, up, half, side, owner, owner_level):
        device = {"dp": row, "seq": spot + 2 if up else spot - 2}
        send(condition, half, owner, owner_level, device, by_level.at[half, side, owner_level])

    def to_first(condition, half, owner_level):
        send(condition, half, row, owner_level, here, by_first.at[half, owner_level])

    def to_second(condition, half, side, owner, owner_level):
        device = {"dp": second, "seq": spot}
        send(condition, half, owner, owner_level, device, by_second.at[half, side, owner_level])

    def to_core(condition, half, owner, owner_level):
        device = {"dp": row, "seq": at.sibling}
        send(condition, half, owner, owner_level, device, by_core.at[half, owner, owner_level])

    def arrived(condition, half, owner, owner_level, arrival):
        sender.arrived(condition, piece(half, owner, owner_level), here, arrival)

    to_first(None, 1, level)
    along(above, True, 0, 0, row, level)
    along(below, False, 0, 0, row, level)
    to_second(None, 0, 0, row, level)
    to_first(None, 0, level)
    to_second(None, 1, 0, row, level)
    along(above, True, 1, 0, row, level)
    along(below, False, 1, 0, row, level)
    to_core(None, 0, row, level)
    to_core(None, 1, row, level)
    yield "started"
    arrived(None, 1, first, level, by_first.at[1, level])
    along(above, True, 1, 1, first, level)
    along(below, False, 1, 1, first, level)
    to_second(None, 1, 1, first, level)
    to_core(None, 1, first, level)
    yield "step"
    arrived(None, 0, first, level, by_first.at[0, level])
    to_second(None, 0, 1, first, level)
    to_core(None, 0, first, level)
    yield "step"

    def from_second(condition, owner_level, half):
        for side, owner in ((0, second), (1, both)):
            arrived(condition, half, owner, owner_level, by_second.at[half, side, owner_level])
            to_core(condition, half, owner, owner_level)

    waiting = [(None, level)]
    for step in range(1, levels):
        ways = ((level - step >= 0, level - step, True), (level + step < levels, level + step, False))

        def onward(up, step=step):
            if up:
                return (level - step >= 0) & above
            return (level + step < levels) & below

        for condition, source, up in ways:
            arrived(condition, 0, row, source, by_level.at[0, 0, source])
            if step < levels - 1:
                along(onward(up), up, 0, 0, row, source)
            to_first(condition, 0, source)
            to_second(condition, 0, 0, row, source)
            to_core(condition, 0, row, source)
        yield "step"
        for side, owner in ((0, row), (1, first)):
            for condition, source, up in ways:
                arrived(condition, 1, owner, source, by_level.at[1, side, source])
                if step < levels - 1:
                    along(onward(up), up, 1, side, owner, source)
                to_second(condition, 1, side, owner, source)
                to_core(condition, 1, owner, source)
            yield "step"
        for condition, source, up in ways:
            arrived(condition, 0, first, source, by_first.at[0, source])
            to_second(condition, 0, 1, first, source)
            to_core(condition, 0, first, source)
        yield "step"
        if step == levels - 1:
            yield "leveled"
        for half in range(2):
            for condition, source in waiting:
                from_second(condition, source, half)
            yield "step"
        waiting = [(condition, source) for condition, source, _ in ways]
    for half in range(2):
        for condition, source in waiting:
            from_second(condition, source, half)
        yield "step"
    yield "issued"
    for half in range(2):
        for owner in range(4):
            for source in range(levels):
                target = full.at[at.rows_of(owner, source * 2 + 1 - core, half), columns]
                sender.arrived(None, target, here, by_core.at[half, owner, source])
    yield "arrived"
    sender.drain()


def scatter_buffers(levels, width, staged):
    dma = pltpu.SemaphoreType.DMA
    buffers = [
        pltpu.VMEM((2, 4, levels, PIECE, width), BF16),
        pltpu.VMEM((2, 2, levels, PIECE, width), BF16),
        pltpu.VMEM((levels + 1, PIECE, width), BF16),
        pltpu.VMEM((3, levels + 1, PIECE, width), BF16),
        dma((2, 4, levels)),
        dma((2, 2, levels)),
        dma((levels + 1,)),
        dma((3, levels + 1)),
        dma((8 + 44 * levels,)),
    ]
    if staged:
        buffers += [pltpu.VMEM((SLOTS, PIECE, width), BF16), dma((SLOTS,))]
    return buffers


def scatter_steps(
    at, columns, chunk, grads, targets, total, by_second, by_first, by_level,
    core_sem, second_sem, first_sem, level_sem, sends, staged=None, load_sem=None,
):
    levels, row, spot, level, core = at.levels, at.row, at.spot, at.level, at.core
    first, second, both, above, below = at.first, at.second, at.both, at.above, at.below
    sender = Sender(sends)
    here = {"dp": first, "seq": spot}
    begin, width = columns
    columns = pl.ds(begin, width)
    ways = [(far, up) for far in range(levels - 1, 0, -1) for up in (True, False)] + [(0, True)]

    def there(way):
        far, up = way
        if far == 0:
            return None, level
        return (level + far < levels, level + far) if up else (level - far >= 0, level - far)

    def add(target, other):
        def body(step, _):
            part = pl.ds(pl.multiple_of(step * chunk, chunk), chunk)
            target[:, part] = target[:, part] + other[:, part]
            return 0

        lax.fori_loop(0, width // chunk, body, 0)

    def arrived(target, arrival):
        sender.arrived(None, target, here, arrival)

    def listing(one, two):
        out = []
        for turn in range(len(ways) + LAG):
            if turn < len(ways):
                out += [(True, ways[turn], half, side, owner) for half in (1, 0) for side, owner in ((0, one), (1, both))]
            if turn >= LAG:
                out += [(False, ways[turn - LAG], half, side, owner) for half in (1, 0) for side, owner in ((0, row), (1, two))]
        return out

    listed = listing(second, first)
    given = listing(first, second)

    def to_core(number):
        _, way, half, _, owner = given[number]
        condition, end = there(way)
        device = {"dp": row, "seq": at.sibling}
        source = grads.at[at.rows_of(owner, end * 2 + 1 - core, half), columns]
        sender.start(condition, source, total.at[half, owner, end], device, core_sem.at[half, owner, end])

    for number in range(WINDOW):
        to_core(number)

    def load(number):
        _, way, half, _, owner = listed[number]
        slot = number % SLOTS
        source = grads.at[at.rows_of(owner, there(way)[1] * 2 + core, half), columns]
        return pltpu.make_async_copy(source, staged.at[slot], load_sem.at[slot])

    def start_load(number):
        if staged is not None and number < len(listed):
            when(there(listed[number][1])[0], lambda: load(number).start())

    for slot in range(SLOTS):
        start_load(slot)
    yield "started"

    def take_listed(number):
        leaves, way, half, side, owner = listed[number]
        if number + WINDOW < len(listed):
            to_core(number + WINDOW)
        condition, end = there(way)
        sums = total.at[half, owner, end]

        def take():
            if staged is not None:
                load(number).wait()
            arrived(sums, core_sem.at[half, owner, end])
            if staged is None:
                add(sums, grads.at[at.rows_of(owner, end * 2 + core, half), columns])
            else:
                add(sums, staged.at[number % SLOTS])

        when(condition, take)
        start_load(number + SLOTS)
        if leaves:
            device = {"dp": second, "seq": spot}
            sender.start(condition, sums, by_second.at[half, side, end], device, second_sem.at[half, side, end])

    for number in range(len(listed)):
        take_listed(number)
        if number % 4 == 3:
            yield "step"
    yield "sent"

    def along(half, side, owner, way):
        far, up = way
        if far == 0:
            return
        condition, end = there(way)
        sums = total.at[half, owner, end]
        place = 0 if half == 0 else 1 + side
        if far < levels - 1:

            def take():
                arrived(by_level.at[place, end], level_sem.at[place, end])
                add(sums, by_level.at[place, end])

            pl.when(condition & (below if up else above))(take)
        slot = end if up or far > 1 else levels
        device = {"dp": row, "seq": spot + 2 if up else spot - 2}
        sender.start(condition, sums, by_level.at[place, slot], device, level_sem.at[place, slot])

    def from_second(half, side, owner, way):
        condition, end = there(way)

        def take():
            arrived(by_second.at[half, side, end], second_sem.at[half, side, end])
            add(total.at[half, owner, end], by_second.at[half, side, end])

        when(condition, take)

    def from_first(way):
        condition, end = there(way)

        def take():
            arrived(by_first.at[end], first_sem.at[end])
            add(total.at[0, row, end], by_first.at[end])

        when(condition, take)
        along(0, 0, row, way)

    previous = None
    for way in ways:
        condition, end = there(way)
        for side, owner in ((0, row), (1, first)):
            from_second(1, side, owner, way)
            along(1, side, owner, way)
        yield "step"
        from_second(0, 1, first, way)
        sender.start(condition, total.at[0, first, end], by_first.at[end], here, first_sem.at[end])
        from_second(0, 0, row, way)
        yield "step"
        if previous is not None:
            from_first(previous)
            yield "step"
        previous = way
    from_first(previous)
    yield "step"

    def collect(half, side, owner):
        sums = total.at[half, owner, level]
        place = 0 if half == 0 else 1 + side

        def take(slot):
            arrived(by_level.at[place, slot], level_sem.at[place, slot])
            add(sums, by_level.at[place, slot])

        pl.when(below)(lambda: take(level))
        pl.when(above)(lambda: take(levels))

    def final(half, *parts):
        rows, at_part = pl.ds(half * PIECE, PIECE), 0
        for target, start, length in targets:
            part = pl.ds(at_part, length)
            value = parts[0][:, part].astype(F32)
            for other in parts[1:]:
                value = value + other[:, part].astype(F32)
            target[rows, pl.ds(start, length)] = value
            at_part += length

    collect(1, 1, first)
    sender.start(None, total.at[1, first, level], by_first.at[levels], here, first_sem.at[levels])
    yield "step"
    collect(1, 0, row)
    yield "step"
    collect(0, 0, row)
    final(0, total.at[0, row, level])
    yield "step"
    arrived(by_first.at[levels], first_sem.at[levels])
    final(1, total.at[1, row, level], by_first.at[levels])
    sender.drain()


def segment(starts, row, places):
    total = jnp.zeros_like(places)
    for k in range(PACKED):
        begin = starts[row, k]
        total = total + jnp.where((begin > 0) & (places >= begin), 1, 0)
    return total


def row_scalars(starts, row, first):
    before = jnp.int32(0)
    last = jnp.int32(0)
    for k in range(PACKED):
        begin = starts[row, k]
        before = before + jnp.where((begin > 0) & (begin <= first - 1), 1, 0)
        last = last + jnp.where((begin > 0) & (begin <= first + TOKENS - 1), 1, 0)
    return before, last


def fill_masks(starts, first, carry_in, carry_out, taps, within, below):
    places = first + lax.broadcasted_iota(jnp.int32, (TOKENS, HEAD_SIZE), 0)
    side = lax.broadcasted_iota(jnp.int32, (TOKENS, TOKENS), 0)
    across = lax.broadcasted_iota(jnp.int32, (TOKENS, TOKENS), 1)
    within[...] = jnp.zeros_like(within)
    below[...] = jnp.zeros_like(below)
    for row in range(ROWS):
        span = pl.ds(row * TOKENS, TOKENS)
        mine = segment(starts, row, places)
        before, last = row_scalars(starts, row, first)
        carry_in[span, :] = (mine == before).astype(F32)
        carry_out[span, :] = (mine == last).astype(F32)
        for shift in range(1, KW):
            there = places - shift
            same = (segment(starts, row, there) == mine) & (there >= 0)
            taps[shift - 1, span, :] = same.astype(F32)
        same = segment(starts, row, first + side) == segment(starts, row, first + across)
        within[span, span] = (same & (side >= across)).astype(F32)
        below[span, span] = (same & (side > across)).astype(F32)


def padded(main, halo):
    return jnp.concatenate([halo, main], axis=0)


def unit_scale(values):
    return lax.rsqrt(jnp.sum(values * values, axis=-1, keepdims=True) + NEAR_ZERO)


def lane_of(values, lane):
    lanes = lax.broadcasted_iota(jnp.int32, values.shape, 1)
    return jnp.sum(jnp.where(lanes == lane, values, 0.0), axis=-1, keepdims=True)


def head_columns(part, head):
    return pl.ds(pl.multiple_of(part * MODEL_WIDTH + head * HEAD_SIZE, HEAD_SIZE), HEAD_SIZE)


def halves(value):
    high = low(value)
    return high, low(value - high.astype(F32))


def gram_of(keys):
    high, rest = halves(keys)
    return nt(high, high) + nt(high, rest) + nt(rest, high)


def per_row(function, *arrays):
    return jnp.concatenate(
        [
            function(row, *[array[row * TOKENS : (row + 1) * TOKENS] for array in arrays])
            for row in range(ROWS)
        ],
        axis=0,
    )


def invert(system, apart):
    eye = jnp.where(apart == 0, 1.0, 0.0)
    solved = eye - jnp.where(apart == 1, system, 0.0)
    size = 2
    while size < TOKENS:
        cross = low(jnp.where((apart >= size) & (apart < 2 * size), system, 0.0))
        rough = low(solved)
        solved = solved - nn(low(nn(rough, cross)), rough)
        size *= 2
    return solved


def kappa_eye(kept):
    side = lax.broadcasted_iota(jnp.int32, (HEAD_SIZE, HEAD_SIZE), 0)
    across = lax.broadcasted_iota(jnp.int32, (HEAD_SIZE, HEAD_SIZE), 1)
    return jnp.where(side == across, 1.0, 0.0) * kept


def tap_moves():
    group = 3 * HEAD_SIZE
    side = lax.broadcasted_iota(jnp.int32, (group, group), 0)
    across = lax.broadcasted_iota(jnp.int32, (group, group), 1)
    third, device, lane = side // HEAD_SIZE, (side % HEAD_SIZE) // 32, side % 32
    return jnp.where(across == device * 96 + third * 32 + lane, 1.0, 0.0).astype(BF16)


def tap_rows(small_rows):
    move = tap_moves()
    wanted = []
    for block in range(MODEL_WIDTH // HEAD_SIZE):
        lanes = slice(block * HEAD_SIZE, (block + 1) * HEAD_SIZE)
        parts = [small_rows[CONV_AT + 3 * j : CONV_AT + 3 * j + 3, lanes] for j in range(KW)]
        source = jnp.concatenate(
            [jnp.concatenate([part[c : c + 1] for c in range(3)], axis=1) for part in parts], axis=0
        )
        wanted.append(nn(low(source), move))
    return wanted


def pack_few(target, turned, mixer_gain, mlp_gain, beta, conv):
    turned[...] = jnp.zeros_like(turned)
    share = 2 * PIECE
    turned[0:1, 0:share] = mixer_gain[...].astype(F32)
    turned[1:2, 0:share] = mlp_gain[...].astype(F32)
    taps = conv[...].astype(F32)
    for tap in range(KW):
        for third in range(3):
            place = CONV_AT + 3 * tap + third
            turned[place : place + 1, 0:share] = taps[tap : tap + 1, third * share : (third + 1) * share]
    value = turned[...].T[:share]
    turned[...] = jnp.zeros_like(turned)
    turned[0:share, BETA_AT:CONV_AT] = beta[...].astype(F32)
    target[:, AT_SMALL:AT_OUT] = low(value + turned[0:share, :])


def mixer_forward_kernel(routed, *refs):
    (starts, tokens, head_gain), refs = refs[:3], refs[3:]
    if routed:
        (mix_share, out_share, up_share, down_share, *few), refs = refs[:8], refs[8:]
    (full, normed, pre_low, raw, beta, solved, solved_w, fresh, state, power, outputs, gated, conv, gains), refs = refs[:14], refs[14:]
    (every, carry_in, carry_out, taps, within, below, apart), refs = refs[:7], refs[7:]
    (offset, solved_u, attend, queries, arriving, leaving, send, receive), refs = refs[:8], refs[8:]
    (mix, small, halo, halo_send, halo_receive, load_sem, pre), refs = refs[:7], refs[7:]
    count = lax.axis_size("seq")
    index = lax.axis_index("seq")
    first = index * TOKENS
    rest = iter(())
    if routed:
        keep_sem, packed, turned = refs[:3]
        routes = refs[3:]
        at = Place(count // 2)

        def keep(number, share, begin):
            columns = pl.ds(begin, share.shape[-1])
            copy = pltpu.make_async_copy(share, packed.at[:, columns], keep_sem.at[number])
            copy.start()
            return copy

        kept = [keep(0, mix_share, 0), keep(1, out_share, AT_OUT), keep(2, up_share, AT_UP)]
        pack_few(packed, turned, *few)
        at.greet(1)
    else:
        barrier = pltpu.get_barrier_semaphore()

        @pl.when(index > 0)
        def _():
            pl.semaphore_signal(barrier, inc=1, device_id={"seq": index - 1}, device_id_type=MESH)

        @pl.when(index + 1 < count)
        def _():
            pl.semaphore_wait(barrier, 1)

    def tail(row):
        return pltpu.make_async_remote_copy(
            src_ref=tokens.at[pl.ds((row + 1) * TOKENS - EDGE, EDGE), :], dst_ref=halo.at[pl.ds(row * EDGE, EDGE), :],
            send_sem=halo_send.at[row], recv_sem=halo_receive.at[row], device_id={"seq": index + 1}, device_id_type=MESH,
        )

    @pl.when(index + 1 < count)
    def _():
        for row in range(ROWS):
            tail(row).start()

    if routed:
        kept[0].wait()
        wanted = gather_steps(at, packed, full, pl.ds(0, AT_OUT), *routes[:5])
        until(wanted, "started")
        rows = down_share[...].astype(F32)

        def store(row, column, value):
            packed[row : row + PIECE, AT_DOWN + column : AT_DOWN + column + 128] = low(value)

        pack_hand(rows, 0, store)

    @pl.when(index == 0)
    def _():
        arriving[...] = jnp.zeros_like(arriving)
        halo[...] = jnp.zeros_like(halo)

    fill_masks(starts, first, carry_in, carry_out, taps, within, below)
    side = lax.broadcasted_iota(jnp.int32, (ALL, ALL), 0)
    across = lax.broadcasted_iota(jnp.int32, (ALL, ALL), 1)
    apart[...] = jnp.bitwise_xor(side, across)
    if routed:
        kept[1].wait()
        kept[2].wait()
        mine = pl.ds(pl.multiple_of((at.row * count + index) * 2 * PIECE, 2 * PIECE), 2 * PIECE)
        own = pltpu.make_async_copy(packed, full.at[mine, :], keep_sem.at[3])
        own.start()
        until(wanted, "issued")
        rest = gather_steps(at, packed, full, pl.ds(AT_OUT, PACK - AT_OUT), *routes[5:])
        until(rest, "started")
        until(wanted, "arrived")
        own.wait()

    def load(number):
        if number < 0:
            return pltpu.make_async_copy(full.at[:, pl.ds(AT_SMALL, SMALL)], small, load_sem.at[MIX // WIDE])
        columns = pl.ds(number * WIDE, WIDE)
        return pltpu.make_async_copy(full.at[:, columns], mix.at[:, columns], load_sem.at[number])

    for number in range(-1, MIX // WIDE):
        load(number).start()
    load(-1).wait()
    small_rows = small[:, pl.ds(0, HEAD_SIZE)].astype(F32).T
    gains[...] = small_rows[:8]
    for block, part in enumerate(tap_rows(small_rows)):
        conv[:, pl.ds(block * 3 * HEAD_SIZE, 3 * HEAD_SIZE)] = part

    def norm(source, target, rows):
        values = source[...].astype(F32)
        scale = lax.rsqrt(jnp.mean(values * values, axis=-1, keepdims=True) + NEAR_ZERO)
        target[rows, :] = low(values * scale * gains[0:1, :])

    norm(tokens, every, pl.ds(0, ALL))

    @pl.when(index > 0)
    def _():
        for row in range(ROWS):
            tail(row).wait_recv()

    norm(halo, every, pl.ds(ALL, ROWS * EDGE))
    normed[...] = low(every[pl.ds(0, ALL), :].astype(F32).T)
    beta[...] = jax.nn.sigmoid(nn(every[pl.ds(0, ALL), :], small[...]))
    for number in range(MIX // WIDE):
        load(number).wait()
        columns = pl.ds(number * WIDE, WIDE)
        wide = nn(every[...], mix[:, columns])
        pre[:, columns] = wide
        pre_low[:, columns] = low(wide)

    def convolve(columns):
        weight = conv[:, columns]
        rows = []
        for row in range(ROWS):
            main = pre[pl.ds(row * TOKENS, TOKENS), columns]
            before = pre[pl.ds(ALL + (row + 1) * EDGE - HALO, HALO), columns]
            longer = padded(main, before)
            total = weight[0:1] * main
            for shift in range(1, KW):
                tap = taps[shift - 1, pl.ds(row * TOKENS, TOKENS), :]
                total = total + weight[shift : shift + 1] * longer[HALO - shift : HALO - shift + TOKENS] * tap
            rows.append(total)
        total = jnp.concatenate(rows, axis=0)
        raw[:, columns] = low(total)
        return total * jax.nn.sigmoid(total)

    def local(head):
        active_q = convolve(head_columns(0, head))
        active_k = convolve(head_columns(1, head))
        values = convolve(head_columns(2, head))
        query = active_q * (unit_scale(active_q) * HEAD_SIZE**-0.5)
        key = active_k * unit_scale(active_k)
        strength = lane_of(beta[...], BETA_AT + head)
        columns = head_columns(0, head)
        system = below[...] * (strength * gram_of(key))
        inverse = low(invert(system, apart[...]))
        solved[head] = inverse
        enter = carry_in[...]
        w = low(nn(inverse, low(strength * enter * key)))
        u = nn(inverse, low(strength * values))
        solved_w[:, columns] = w
        solved_u[:, columns] = u
        leave = low(carry_out[...] * key)
        u_low = low(u)
        for row in range(ROWS):
            span = slice(row * TOKENS, (row + 1) * TOKENS)
            before, last = row_scalars(starts, row, first)
            kept = jnp.where(before == last, 1.0, 0.0)
            power[head, row] = low(kappa_eye(kept) - tn(leave[span], w[span]))
            offset[head, row] = tn(leave[span], u_low[span])
        attend[head] = low(within[...] * nt(low(query), low(key)))
        queries[:, columns] = low(enter * query)


    for step in range(HEADS // GROUP):
        for part in range(GROUP):
            local(step * GROUP + part)
        advance(rest, 2)

    def copy(head):
        return pltpu.make_async_remote_copy(
            src_ref=leaving.at[head], dst_ref=arriving.at[head], send_sem=send.at[head], recv_sem=receive.at[head],
            device_id={"seq": index + 1}, device_id_type=MESH,
        )

    def chain(head):
        @pl.when(index > 0)
        def _():
            copy(head).wait_recv()

        @pl.when(index + 1 < count)
        def _():
            for row in range(ROWS):
                leaving[head, row] = low(nn(power[head, row], arriving[head, row]) + offset[head, row])
            copy(head).start()

        columns = head_columns(0, head)
        w, u, query = solved_w[:, columns], solved_u[:, columns], queries[:, columns]
        x = low(u - per_row(lambda row, part: nn(part, arriving[head, row]), w))
        fresh[:, columns] = x
        output = per_row(lambda row, part: nn(part, arriving[head, row]), query) + nn(attend[head], x)
        outputs[:, columns] = output
        scale = lax.rsqrt(jnp.mean(output * output, axis=-1, keepdims=True) + HEAD_ZERO)
        gate = pre[pl.ds(0, ALL), head_columns(3, head)]
        gated[:, columns] = low(output * scale * head_gain[...].astype(F32) * (gate * jax.nn.sigmoid(gate)))

    advance(rest, 8)
    for head in range(HEADS):
        chain(head)
        advance(rest)
    state[...] = arriving[...]

    @pl.when(index + 1 < count)
    def _():
        for row in range(ROWS):
            tail(row).wait_send()

        def drain(head, _):
            copy(head).wait_send()
            return 0

        lax.fori_loop(0, HEADS, drain, 0)

    until(rest, "end")
    if routed:
        until(wanted, "end")


def mixer_forward(starts, tokens, head_gain, weights):
    routed = len(weights) > 1
    vmem, anywhere = pl.BlockSpec(memory_space=pltpu.VMEM), pl.BlockSpec(memory_space=pl.ANY)
    dma = pltpu.SemaphoreType.DMA
    shape = jax.ShapeDtypeStruct
    states = (HEADS, ROWS, HEAD_SIZE, HEAD_SIZE)
    long = ALL + ROWS * EDGE
    whole = [shape((MODEL_WIDTH, PACK), BF16)] if routed else []
    levels = lax.axis_size("seq") // 2
    routes = []
    if routed:
        routes = [
            dma((4,)),
            pltpu.VMEM((2 * PIECE, PACK), BF16),
            pltpu.VMEM((SMALL, SMALL), F32),
        ]
        routes += gather_semaphores(levels) + gather_semaphores(levels)
    results = pl.pallas_call(
        functools.partial(mixer_forward_kernel, routed),
        out_shape=whole + [
            shape((MODEL_WIDTH, ALL), BF16),
            shape((long, MIX), BF16),
            shape((ALL, QKV), BF16),
            shape((ALL, SMALL), F32),
            shape((HEADS, ALL, ALL), BF16),
            shape((ALL, MODEL_WIDTH), BF16),
            shape((ALL, MODEL_WIDTH), BF16),
            shape(states, BF16),
            shape(states, BF16),
            shape((ALL, MODEL_WIDTH), F32),
            shape((ALL, MODEL_WIDTH), BF16),
            shape((KW, QKV), F32),
            shape((8, MODEL_WIDTH), F32),
        ],
        in_specs=[pl.BlockSpec(memory_space=pltpu.SMEM), vmem, vmem] + ([anywhere] * 3 + [vmem] * 5 if routed else [anywhere]),
        out_specs=[anywhere] * len(whole) + [vmem] * 13,
        scratch_shapes=[
            pltpu.VMEM((long, MODEL_WIDTH), BF16),
            pltpu.VMEM((ALL, HEAD_SIZE), F32),
            pltpu.VMEM((ALL, HEAD_SIZE), F32),
            pltpu.VMEM((KW - 1, ALL, HEAD_SIZE), F32),
            pltpu.VMEM((ALL, ALL), F32),
            pltpu.VMEM((ALL, ALL), F32),
            pltpu.VMEM((ALL, ALL), jnp.int32),
            pltpu.VMEM(states, F32),
            pltpu.VMEM((ALL, MODEL_WIDTH), F32),
            pltpu.VMEM((HEADS, ALL, ALL), BF16),
            pltpu.VMEM((ALL, MODEL_WIDTH), BF16),
            pltpu.VMEM(states, BF16),
            pltpu.VMEM(states, BF16),
            dma((HEADS,)),
            dma((HEADS,)),
            pltpu.VMEM((MODEL_WIDTH, MIX), BF16),
            pltpu.VMEM((MODEL_WIDTH, SMALL), BF16),
            pltpu.VMEM((ROWS * EDGE, MODEL_WIDTH), BF16),
            dma((ROWS,)),
            dma((ROWS,)),
            dma((MIX // WIDE + 1,)),
            pltpu.VMEM((long, MIX), F32),
        ] + routes,
        compiler_params=pltpu.CompilerParams(
            collective_id=1, has_side_effects=True, vmem_limit_bytes=56 * 2**20
        ),
        name="mixer_forward",
    )(starts, tokens, head_gain, *weights)
    return results if routed else [weights[0]] + list(results)


def mixer_backward_kernel(routed, *refs):
    (starts, grad_gated, grad_mid, tokens, gains, full, conv, head_gain), refs = refs[:8], refs[8:]
    (pre, raw, beta, solved, solved_w, fresh, state, power, outputs), refs = refs[:9], refs[9:]
    if routed:
        (normed_t, grad_mlp, grads), refs = refs[:3], refs[3:]
        (grad_hidden, *targets), refs = refs[:4], refs[4:]
        (mix_sum, small_sum, head_sum), refs = refs[:3], refs[3:]
        (grad_project, grad_logits, grad_conv, grad_head, grad_gain), refs = refs[:5], refs[5:]
    else:
        (grad_hidden, grad_project, grad_logits, grad_conv, grad_head, grad_gain), refs = refs[:6], refs[6:]
    (carry_in, carry_out, taps, within, below), refs = refs[:5], refs[5:]
    (grad_out, grad_raw, grad_beta, arriving, leaving, halo_out, halo_in), refs = refs[:7], refs[7:]
    (send, receive, halo_send, halo_receive, mix, load_sem), refs = refs[:6], refs[6:]
    fresh_part, offset = grad_hidden, grad_raw
    small = mix.at[:, pl.ds(AT_SMALL, SMALL)]
    count = lax.axis_size("seq")
    index = lax.axis_index("seq")
    first = index * TOKENS
    sums = after = iter(())
    if routed:
        at = Place(count // 2)
        at.greet(-1)
        parts, by_level, part_sem, level_sem, head_sends = refs[:5]
        refs = refs[5:]
        out_sum, up_sum, down_sum = targets
        cut = FIRST_REST - MODEL_WIDTH
        sums = scatter_steps(
            at, (0, FIRST_REST), FIRST_REST, grads, ((out_sum, 0, MODEL_WIDTH), (up_sum, 0, cut)), *refs[:11]
        )
        after = scatter_steps(
            at, (FIRST_REST, LAST_REST), LAST_REST, grads, ((up_sum, cut, 2 * FF - cut), (down_sum, 0, FF)), *refs[11:22]
        )
        until(sums, "started")
    else:
        barrier = pltpu.get_barrier_semaphore()

        @pl.when(index + 1 < count)
        def _():
            pl.semaphore_signal(barrier, inc=1, device_id={"seq": index + 1}, device_id_type=MESH)

        @pl.when(index > 0)
        def _():
            pl.semaphore_wait(barrier, 1)

    load_mix = pltpu.make_async_copy(full.at[:, pl.ds(0, AT_OUT)], mix, load_sem)
    load_mix.start()

    @pl.when(index + 1 == count)
    def _():
        arriving[...] = jnp.zeros_like(arriving)
        halo_in[...] = jnp.zeros_like(halo_in)

    fill_masks(starts, first, carry_in, carry_out, taps, within, below)
    grad_head[...] = jnp.zeros_like(grad_head)
    grad_beta[...] = jnp.zeros_like(grad_beta)

    def active_of(part, head):
        values = raw[:, head_columns(part, head)].astype(F32)
        return values * jax.nn.sigmoid(values)

    def prepare(head):
        columns = head_columns(0, head)
        gate_columns = head_columns(3, head)
        gate = pre[pl.ds(0, ALL), gate_columns].astype(F32)
        sigma = jax.nn.sigmoid(gate)
        output = outputs[:, columns]
        scale = lax.rsqrt(jnp.mean(output * output, axis=-1, keepdims=True) + HEAD_ZERO)
        sample = output * scale
        incoming = grad_gated[:, columns]
        gain = head_gain[...].astype(F32)
        grad_project[:, gate_columns] = low(incoming * sample * gain * (sigma * (1.0 + gate * (1.0 - sigma))))
        grad_sample = incoming * (gate * sigma)
        grad_head[0:1, :] += jnp.sum(grad_sample * sample, axis=0, keepdims=True)
        scaled = grad_sample * gain
        mean = jnp.mean(scaled * output, axis=-1, keepdims=True)
        here = low(scale * scaled - output * (scale * scale * scale * mean))
        grad_out[:, columns] = here
        active_q, active_k = active_of(0, head), active_of(1, head)
        query = active_q * (unit_scale(active_q) * HEAD_SIZE**-0.5)
        key = active_k * unit_scale(active_k)
        attend = low(within[...] * nt(low(query), low(key)))
        part = tn(attend, here)
        fresh_part[:, columns] = part
        entering = low(carry_in[...] * query)
        part_low = low(part)
        w = solved_w[:, columns]
        for row in range(ROWS):
            span = slice(row * TOKENS, (row + 1) * TOKENS)
            offset[span, columns] = tn(entering[span], here[span]) - tn(w[span], part_low[span])

    for head in range(HEADS):
        prepare(head)
        advance(sums, AT_PREPARE)

    def copy(head):
        return pltpu.make_async_remote_copy(
            src_ref=leaving.at[head], dst_ref=arriving.at[head], send_sem=send.at[head], recv_sem=receive.at[head],
            device_id={"seq": index - 1}, device_id_type=MESH,
        )

    def chain(head):
        @pl.when(index + 1 < count)
        def _():
            copy(head).wait_recv()

        @pl.when(index > 0)
        def _():
            for row in range(ROWS):
                start = offset[pl.ds(row * TOKENS, TOKENS), head_columns(0, head)]
                leaving[head, row] = low(tn(power[head, row], arriving[head, row]) + start)
            copy(head).start()

    until(after, "started")
    both_advance(AT_CHAIN, sums, after)
    more = iter(())
    if routed:
        sender = Sender(head_sends)

        def exchange(number, value, row, spot):
            parts[2 * number] = value
            device = {"dp": row, "seq": spot}
            sender.start(None, parts.at[2 * number], parts.at[2 * number + 1], device, part_sem.at[number])
            return lambda: sender.arrived(None, parts.at[2 * number + 1], device, part_sem.at[number])

        pending = exchange(0, grad_head[...], at.row, at.sibling)

    for head in range(HEADS):
        chain(head)

    def finish(head):
        columns = head_columns(0, head)
        raw_q, raw_k = raw[:, columns].astype(F32), raw[:, head_columns(1, head)].astype(F32)
        raw_v = raw[:, head_columns(2, head)].astype(F32)
        sigma_q, sigma_k, sigma_v = jax.nn.sigmoid(raw_q), jax.nn.sigmoid(raw_k), jax.nn.sigmoid(raw_v)
        active_q, active_k, values = raw_q * sigma_q, raw_k * sigma_k, raw_v * sigma_v
        scale_q, scale_k = unit_scale(active_q), unit_scale(active_k)
        query = low(active_q * (scale_q * HEAD_SIZE**-0.5))
        key_full = active_k * scale_k
        key = low(key_full)
        enter, leave = carry_in[...], carry_out[...]
        strength = lane_of(beta[...], BETA_AT + head)
        here = grad_out[:, columns]
        x = fresh[:, columns]
        leaving_keys = low(leave * key_full)
        grad_x = fresh_part[:, columns] + per_row(lambda row, part: nn(part, arriving[head, row]), leaving_keys)
        y = tn(solved[head], low(grad_x))
        y_low = low(y)
        grad_attend = low(within[...] * nt(here, x))
        gram = gram_of(key_full)
        grad_system = -below[...] * nt(y_low, x)
        grad_gram = low(strength * grad_system)
        grad_q = nn(grad_attend, key) + enter * per_row(lambda row, part: nt(part, state[head, row]), here)
        grad_k = (
            tn(grad_attend, query)
            + leave * per_row(lambda row, part: nt(part, arriving[head, row]), x)
            + nn(grad_gram, key)
            + tn(grad_gram, key)
            - strength * enter * per_row(lambda row, part: nt(part, state[head, row]), y_low)
        )
        z = values - enter * per_row(lambda row, part: nn(part, state[head, row]), key)
        grad_v = strength * y
        grad_strength = jnp.sum(y * z, axis=-1, keepdims=True) + jnp.sum(grad_system * gram, axis=-1, keepdims=True)
        lanes = lax.broadcasted_iota(jnp.int32, grad_beta.shape, 1)
        grad_beta[...] = jnp.where(lanes == BETA_AT + head, grad_strength, grad_beta[...])

        def through(grad, active, scale, part, sigma, extra):
            grad = grad * extra
            mean = jnp.sum(active * grad, axis=-1, keepdims=True)
            grad = scale * grad - active * (scale * scale * scale * mean)
            return grad * (sigma * (1.0 + part * (1.0 - sigma)))

        grad_raw[:, columns] = through(grad_q, active_q, scale_q, raw_q, sigma_q, HEAD_SIZE**-0.5)
        grad_raw[:, head_columns(1, head)] = through(grad_k, active_k, scale_k, raw_k, sigma_k, 1.0)
        grad_raw[:, head_columns(2, head)] = grad_v * (sigma_v * (1.0 + raw_v * (1.0 - sigma_v)))

    for head in range(HEADS):
        finish(head)
        both_advance(AT_FINISH, sums, after)

    def convolve_back(step, _):
        columns = pl.ds(pl.multiple_of(step * HEAD_SIZE, HEAD_SIZE), HEAD_SIZE)
        weight = conv[:, columns]
        nothing = jnp.zeros((HALO, HEAD_SIZE), F32)
        sums = [jnp.zeros((1, HEAD_SIZE), F32) for _ in range(KW)]
        early = []
        for row in range(ROWS):
            span = pl.ds(row * TOKENS, TOKENS)
            grad = grad_raw[span, columns]
            main = pre[span, columns].astype(F32)
            edge = pre[pl.ds(ALL + row * EDGE, EDGE), columns].astype(F32)
            longer = padded(main, edge[EDGE - HALO :])
            total = weight[0:1] * jnp.concatenate([nothing, grad], axis=0)
            sums[0] = sums[0] + jnp.sum(grad * main, axis=0, keepdims=True)
            for shift in range(1, KW):
                masked = grad * taps[shift - 1, span, :]
                wide = jnp.concatenate([nothing, masked, nothing], axis=0)
                total = total + weight[shift : shift + 1] * wide[shift : shift + HALO + TOKENS]
                before = longer[HALO - shift : HALO - shift + TOKENS]
                sums[shift] = sums[shift] + jnp.sum(masked * before, axis=0, keepdims=True)
            early.append(total[:HALO])
            grad_raw[span, columns] = total[HALO:]
        halo_out[:, columns] = low(jnp.concatenate(early, axis=0))
        grad_conv[:, columns] = jnp.concatenate(sums, axis=0)
        return 0

    for part in range(3):
        lax.fori_loop(part * HEADS, (part + 1) * HEADS, convolve_back, 0)
        both_advance(AT_CONV, sums, after)
    back = pltpu.make_async_remote_copy(
        src_ref=halo_out, dst_ref=halo_in, send_sem=halo_send, recv_sem=halo_receive,
        device_id={"seq": index - 1}, device_id_type=MESH,
    )

    @pl.when(index > 0)
    def _():
        back.start()

    strengths = beta[...]
    grad_logits[...] = low(grad_beta[...] * strengths * (1.0 - strengths))

    @pl.when(index + 1 < count)
    def _():
        back.wait_recv()

    for row in range(ROWS):
        end = pl.ds((row + 1) * TOKENS - HALO, HALO)
        grad_raw[end, :] += halo_in[...].astype(F32)[row * HALO : (row + 1) * HALO]

    def narrow(step, _):
        rows = pl.ds(pl.multiple_of(step * 32, 32), 32)
        grad_project[rows, pl.ds(0, QKV)] = low(grad_raw[rows, :])
        return 0

    lax.fori_loop(0, ALL // 32, narrow, 0)

    load_mix.wait()
    both_advance(AT_NORMED, sums, after)

    def normed_back(step, _):
        rows = pl.ds(pl.multiple_of(step * 256, 256), 256)
        grad_hidden[:, rows] = nt(grad_project[...], mix[rows, pl.ds(0, MIX)]) + nt(grad_logits[...], small[rows, :])
        return 0

    lax.fori_loop(0, MODEL_WIDTH // 256, normed_back, 0)
    grad_gain[...] = jnp.zeros_like(grad_gain)

    def hidden_back(step, _):
        rows = pl.ds(pl.multiple_of(step * 32, 32), 32)
        hidden = tokens[rows, :].astype(F32)
        scale = lax.rsqrt(jnp.mean(hidden * hidden, axis=-1, keepdims=True) + NEAR_ZERO)
        grad = grad_hidden[rows, :]
        grad_gain[...] += jnp.sum(grad * hidden * scale, axis=0, keepdims=True)
        scaled = grad * gains[0:1, :]
        mean = jnp.mean(scaled * hidden, axis=-1, keepdims=True)
        grad_hidden[rows, :] = grad_mid[rows, :] + scale * scaled - hidden * (scale * scale * scale * mean)
        return 0

    lax.fori_loop(0, ALL // 32, hidden_back, 0)
    if routed:
        turned = grad_raw.at[pl.ds(0, HEAD_SIZE), pl.ds(0, MODEL_WIDTH)]
        turned[...] = jnp.zeros_like(turned)
        turned[0:1, :] = grad_gain[...]
        turned[1:2, :] = grad_mlp[...]
        move = tap_moves()
        for block in range(MODEL_WIDTH // HEAD_SIZE):
            wide = nt(low(grad_conv[:, pl.ds(block * 3 * HEAD_SIZE, 3 * HEAD_SIZE)]), move)
            lanes = pl.ds(block * HEAD_SIZE, HEAD_SIZE)
            for tap in range(KW):
                for third in range(3):
                    place = CONV_AT + 3 * tap + third
                    turned[place : place + 1, lanes] = wide[tap : tap + 1, third * HEAD_SIZE : (third + 1) * HEAD_SIZE]

        def weigh(tile, _):
            columns = pl.ds(pl.multiple_of(tile * 256, 256), 256)
            mix[:, columns] = low(nn(normed_t[...], grad_project[:, columns]))
            return 0

        lax.fori_loop(0, MIX // 256, weigh, 0)
        mix[:, pl.ds(AT_SMALL, SMALL)] = low(nn(normed_t[...], grad_logits[...]) + turned[...].T)
        more = scatter_steps(
            at, (0, AT_OUT), CHUNK_MIX, mix, ((mix_sum, 0, MIX), (small_sum, 0, SMALL)), *refs[22:]
        )
        until(more, "started")
        for number, (row, spot) in enumerate(((at.near, at.spot), (at.far, at.spot))):
            both_advance(AT_END, sums, after, more)
            pending()
            value = parts[2 * number] + parts[2 * number + 1]
            pending = exchange(number + 1, value, row, spot)
        both_advance(AT_END, sums, after, more)
        pending()
        by_level[at.level] = parts[4] + parts[5]
        here = {"dp": at.near, "seq": at.spot}

        def pass_on(condition, up, source):
            device = {"dp": at.row, "seq": at.spot + 2 if up else at.spot - 2}
            sender.start(condition, by_level.at[source], by_level.at[source], device, level_sem.at[source])

        pass_on(at.above, True, at.level)
        pass_on(at.below, False, at.level)
        for step in range(1, at.levels):
            both_advance(AT_END, sums, after, more)
            for condition, source, up, onward in (
                (at.level - step >= 0, at.level - step, True, at.above),
                (at.level + step < at.levels, at.level + step, False, at.below),
            ):
                sender.arrived(condition, by_level.at[source], here, level_sem.at[source])
                if step < at.levels - 1:
                    pass_on(condition & onward, up, source)
        value = by_level[0]
        for level in range(1, at.levels):
            value = value + by_level[level]
        head_sum[...] = jnp.broadcast_to(jnp.sum(value, axis=0, keepdims=True), value.shape)
        for _ in range(12):
            both_advance(AT_END, sums, after, more)
        until(sums, "end")
        until(after, "end")
        until(more, "end")
        sender.drain()

    @pl.when(index > 0)
    def _():
        back.wait_send()

        def drain(head, _):
            copy(head).wait_send()
            return 0

        lax.fori_loop(0, HEADS, drain, 0)


def mixer_backward(operands, normed, grad_mlp, grads, routed):
    vmem, anywhere = pl.BlockSpec(memory_space=pltpu.VMEM), pl.BlockSpec(memory_space=pl.ANY)
    dma = pltpu.SemaphoreType.DMA
    shape = jax.ShapeDtypeStruct
    states = (HEADS, ROWS, HEAD_SIZE, HEAD_SIZE)
    levels = lax.axis_size("seq") // 2
    local = [
        ((ALL, MIX), BF16),
        ((ALL, SMALL), BF16),
        ((KW, QKV), F32),
        ((8, HEAD_SIZE), F32),
        ((1, MODEL_WIDTH), F32),
    ]
    scratch = [
        pltpu.VMEM((ALL, HEAD_SIZE), F32),
        pltpu.VMEM((ALL, HEAD_SIZE), F32),
        pltpu.VMEM((KW - 1, ALL, HEAD_SIZE), F32),
        pltpu.VMEM((ALL, ALL), F32),
        pltpu.VMEM((ALL, ALL), F32),
        pltpu.VMEM((ALL, MODEL_WIDTH), BF16),
        pltpu.VMEM((ALL, QKV), F32),
        pltpu.VMEM((ALL, SMALL), F32),
        pltpu.VMEM(states, BF16),
        pltpu.VMEM(states, BF16),
        pltpu.VMEM((ROWS * HALO, QKV), BF16),
        pltpu.VMEM((ROWS * HALO, QKV), BF16),
        dma((HEADS,)),
        dma((HEADS,)),
        dma,
        dma,
        pltpu.VMEM((MODEL_WIDTH, AT_OUT), BF16),
        dma,
    ]
    more = []
    out_shape = [shape((ALL, MODEL_WIDTH), F32)]
    if routed:
        more = [normed, grad_mlp, grads]
        out_shape += [shape((2 * PIECE, width), F32) for width in (MODEL_WIDTH, 2 * FF, FF, MIX, SMALL)]
        out_shape += [shape((8, HEAD_SIZE), F32)]
        scratch = [pltpu.VMEM(*entry) for entry in local] + scratch
        scratch += [
            pltpu.VMEM((6, 8, HEAD_SIZE), F32),
            pltpu.VMEM((levels, 8, HEAD_SIZE), F32),
            dma((3,)),
            dma((levels,)),
            dma((3 + 2 * levels,)),
        ]
        scratch += scatter_buffers(levels, FIRST_REST, True) + scatter_buffers(levels, LAST_REST, True)
        scratch += scatter_buffers(levels, AT_OUT, False)
    else:
        out_shape += [shape(*entry) for entry in local]
    in_specs = [pl.BlockSpec(memory_space=pltpu.SMEM)] + [vmem] * 4 + [anywhere] + [vmem] * 11
    in_specs += [vmem, vmem, anywhere] if routed else []
    return pl.pallas_call(
        functools.partial(mixer_backward_kernel, routed),
        out_shape=out_shape,
        in_specs=in_specs,
        out_specs=[vmem] * len(out_shape),
        scratch_shapes=scratch,
        compiler_params=pltpu.CompilerParams(
            collective_id=2, has_side_effects=True, vmem_limit_bytes=63 * 2**20
        ),
        name="mixer_backward",
    )(*operands, *more)


TILE = 256
HANDS = 32
OWN = FF // HANDS
GROUP_ROWS = 4 * OWN


def pack_hand(source, begin, store):
    for half in range(2):
        for lane in range(2):
            for step in range(11):
                rows = slice(begin + step * 8, begin + step * 8 + 8)
                first = (4 * half + lane) * 128
                second = (4 * half + 2 + lane) * 128
                pair = jnp.concatenate([source[rows, first : first + 128], source[rows, second : second + 128]], axis=0)
                store(half * PIECE, (lane * 11 + step) * 128, pair)


def mlp_kernel(
    full, tokens, cotangent, gated, gains,
    output, grad_mid, grad_gated, grad_gain, grads,
    out_w, up_w, packed, wide, down_w, hidden, normed, total, grad_normed,
    normed_t, gated_t, acted_t, up_stage, stage, load_sem, up_sem, store_sem, stage_sem,
):
    def load(number):
        columns, target = (
            (pl.ds(AT_OUT, MODEL_WIDTH), out_w),
            (pl.ds(AT_DOWN, FF), packed),
        )[number]
        return pltpu.make_async_copy(full.at[:, columns], target, load_sem.at[number])

    def load_up(tile, side):
        begin = pl.multiple_of(side * FF + tile * TILE, TILE)
        source = full.at[:, pl.ds(pl.multiple_of(AT_UP + begin, 128), TILE)]
        return pltpu.make_async_copy(source, up_w.at[:, pl.ds(begin, TILE)], up_sem.at[side, tile])

    load(1).start()
    load(0).start()

    def start_up(tile, _):
        load_up(tile, 0).start()
        load_up(tile, 1).start()
        return 0

    lax.fori_loop(0, FF // TILE, start_up, 0)
    load(1).wait()

    def unpack(hand, _):
        for half in range(2):
            rows = pl.ds(pl.multiple_of((hand * 2 + half) * PIECE, PIECE), PIECE)
            piece = packed[rows, :].astype(F32)
            for lane in range(2):
                for step in range(11):
                    source = (lane * 11 + step) * 128
                    target = pl.ds(pl.multiple_of(hand * OWN + step * 8, 8), 8)
                    for top in range(2):
                        column = (4 * half + 2 * top + lane) * 128
                        wide[target, column : column + 128] = piece[top * 8 : top * 8 + 8, source : source + 128]
        return 0

    lax.fori_loop(0, HANDS, unpack, 0)

    def narrow(tile, _):
        rows = pl.ds(pl.multiple_of(tile * TILE, TILE), TILE)
        down_w[rows, :] = low(wide[rows, :])
        return 0

    lax.fori_loop(0, FF // TILE, narrow, 0)
    load(0).wait()
    gated_t[...] = low(gated[...].astype(F32).T)
    middle = tokens[...].astype(F32) + nn(gated[...], out_w[...])
    hidden[...] = middle
    inverse = lax.rsqrt(jnp.mean(middle * middle, axis=-1, keepdims=True) + NEAR_ZERO)
    value = middle * inverse * gains[1:2, :]
    normed[...] = low(value)
    normed_t[...] = low(value.T)
    total[...] = jnp.zeros_like(total)
    grad_normed[...] = jnp.zeros_like(grad_normed)

    def store_up(tile, slot, side):
        begin = pl.multiple_of(MODEL_WIDTH + side * FF + tile * TILE, TILE)
        return pltpu.make_async_copy(up_stage.at[slot, side], grads.at[:, pl.ds(begin, TILE)], store_sem.at[slot, side])

    def tile_step(tile, _):
        slot = lax.rem(tile, 2)
        here = pl.ds(pl.multiple_of(tile * TILE, TILE), TILE)
        there = pl.ds(pl.multiple_of(FF + tile * TILE, TILE), TILE)
        load_up(tile, 0).wait()
        load_up(tile, 1).wait()

        @pl.when(tile >= 2)
        def _():
            store_up(tile - 2, slot, 0).wait()
            store_up(tile - 2, slot, 1).wait()

        gate = nn(normed[...], up_w[:, here])
        up = nn(normed[...], up_w[:, there])
        grad = nt(cotangent[...], down_w[here, :])
        sigma = jax.nn.sigmoid(gate)
        soft = gate * sigma
        acted = soft * up
        acted_low = low(acted)
        acted_t[here, :] = low(acted.T)
        total[...] += nn(acted_low, down_w[here, :])
        grad_gate = low(grad * up * (sigma * (1.0 + gate * (1.0 - sigma))))
        grad_up = low(grad * soft)
        grad_normed[...] += nt(grad_gate, up_w[:, here]) + nt(grad_up, up_w[:, there])
        up_stage[slot, 0] = low(nn(normed_t[...], grad_gate))
        up_stage[slot, 1] = low(nn(normed_t[...], grad_up))
        store_up(tile, slot, 0).start()
        store_up(tile, slot, 1).start()
        return 0

    tiles = FF // TILE
    lax.fori_loop(0, tiles, tile_step, 0)
    middle = hidden[...]
    output[...] = low(middle + total[...])
    inverse = lax.rsqrt(jnp.mean(middle * middle, axis=-1, keepdims=True) + NEAR_ZERO)
    grad = grad_normed[...]
    grad_gain[...] = jnp.sum(grad * middle * inverse, axis=0, keepdims=True)
    scaled = grad * gains[1:2, :]
    mean = jnp.mean(scaled * middle, axis=-1, keepdims=True)
    grad = cotangent[...].astype(F32) + inverse * scaled - middle * (inverse * inverse * inverse * mean)
    grad_mid[...] = grad
    grad_low = low(grad)
    grad_gated[...] = nt(grad_low, out_w[...])
    for last in range(2):
        tile = tiles - 2 + last
        for side in range(2):
            store_up(tile, tile % 2, side).wait()

    def store_out(tile):
        slot, side = divmod(tile, 2)
        columns = pl.ds(tile * TILE, TILE)
        return pltpu.make_async_copy(up_stage.at[slot, side], grads.at[:, columns], store_sem.at[slot, side])

    for tile in range(MODEL_WIDTH // TILE):
        slot, side = divmod(tile, 2)
        up_stage[slot, side] = low(nn(gated_t[...], grad_low[:, tile * TILE : (tile + 1) * TILE]))
        store_out(tile).start()

    def store_down(group, slot):
        rows = pl.ds(pl.multiple_of(group * 128, 128), 128)
        target = grads.at[rows, pl.ds(MODEL_WIDTH + 2 * FF, FF)]
        return pltpu.make_async_copy(stage.at[slot], target, stage_sem.at[slot])

    def down_step(group, _):
        slot = lax.rem(group, 2)

        @pl.when(group >= 2)
        def _():
            store_down(group - 2, slot).wait()

        rows = pl.ds(pl.multiple_of(group * GROUP_ROWS, GROUP_ROWS), GROUP_ROWS)
        wide[pl.ds(0, GROUP_ROWS), :] = nn(acted_t[rows, :], cotangent[...])
        for hand in range(4):

            def store(row, column, value, hand=hand):
                stage[slot, hand * 2 * PIECE + row : hand * 2 * PIECE + row + PIECE, column : column + 128] = low(value)

            pack_hand(wide, hand * OWN, store)
        store_down(group, slot).start()
        return 0

    groups = HANDS // 4
    lax.fori_loop(0, groups, down_step, 0)
    for group in (groups - 2, groups - 1):
        store_down(group, group % 2).wait()
    for tile in range(MODEL_WIDTH // TILE):
        store_out(tile).wait()


def mlp(full, tokens, cotangent, gated, gains):
    vmem, anywhere = pl.BlockSpec(memory_space=pltpu.VMEM), pl.BlockSpec(memory_space=pl.ANY)
    dma = pltpu.SemaphoreType.DMA
    shape = jax.ShapeDtypeStruct
    return pl.pallas_call(
        mlp_kernel,
        out_shape=[
            shape((ALL, MODEL_WIDTH), BF16),
            shape((ALL, MODEL_WIDTH), F32),
            shape((ALL, MODEL_WIDTH), F32),
            shape((1, MODEL_WIDTH), F32),
            shape((MODEL_WIDTH, PACK - AT_OUT), BF16),
        ],
        in_specs=[anywhere] + [vmem] * 4,
        out_specs=[vmem] * 4 + [anywhere],
        scratch_shapes=[
            pltpu.VMEM((MODEL_WIDTH, MODEL_WIDTH), BF16),
            pltpu.VMEM((MODEL_WIDTH, 2 * FF), BF16),
            pltpu.VMEM((MODEL_WIDTH, FF), BF16),
            pltpu.VMEM((FF, MODEL_WIDTH), F32),
            pltpu.VMEM((FF, MODEL_WIDTH), BF16),
            pltpu.VMEM((ALL, MODEL_WIDTH), F32),
            pltpu.VMEM((ALL, MODEL_WIDTH), BF16),
            pltpu.VMEM((ALL, MODEL_WIDTH), F32),
            pltpu.VMEM((ALL, MODEL_WIDTH), F32),
            pltpu.VMEM((MODEL_WIDTH, ALL), BF16),
            pltpu.VMEM((MODEL_WIDTH, ALL), BF16),
            pltpu.VMEM((FF, ALL), BF16),
            pltpu.VMEM((2, 2, MODEL_WIDTH, TILE), BF16),
            pltpu.VMEM((2, 128, FF), BF16),
            dma((2,)),
            dma((2, FF // TILE)),
            dma((2, 2)),
            dma((2,)),
        ],
        compiler_params=pltpu.CompilerParams(vmem_limit_bytes=60 * 2**20),
        name="mlp",
    )(full, tokens, cotangent, gated, gains)


def result_kernel(
    hidden, mix, out, up, down, small, head,
    hidden_to, mixer_to, mix_to, conv_to, beta_to, head_to, out_to, mlp_to, up_to, down_to,
):
    for source, target in ((mix, mix_to), (out, out_to), (up, up_to)):
        target[...] = source[...]

    def move(step, _):
        rows = pl.ds(pl.multiple_of(step * 32, 32), 32)
        hidden_to[rows, :] = hidden[rows, :]
        return 0

    lax.fori_loop(0, ALL // 32, move, 0)
    for group in range(4):
        for lane in range(2):
            for step in range(11):
                source = (lane * 11 + step) * 128
                target = (2 * group + lane) * 128
                down_to[step * 8 : step * 8 + 8, target : target + 128] = down[
                    group * 8 : group * 8 + 8, source : source + 128
                ]
    values = small[...]
    beta_to[...] = values[:, BETA_AT:CONV_AT]
    turned = jnp.concatenate([values, jnp.zeros((SMALL - 2 * PIECE, SMALL), F32)], axis=0).T
    mixer_to[...] = turned[0:1, : 2 * PIECE]
    mlp_to[...] = turned[1:2, : 2 * PIECE]
    for tap in range(KW):
        for third in range(3):
            place = CONV_AT + 3 * tap + third
            conv_to[tap : tap + 1, third * 2 * PIECE : (third + 1) * 2 * PIECE] = turned[place : place + 1, : 2 * PIECE]
    head_to[...] = head[0:1, :]


def result(hidden, mix, out, up, down, small, head):
    vmem = pl.BlockSpec(memory_space=pltpu.VMEM)
    shape = jax.ShapeDtypeStruct
    share = 2 * PIECE
    return pl.pallas_call(
        result_kernel,
        out_shape=[
            shape(hidden.shape, F32),
            shape((1, share), F32),
            shape(mix.shape, F32),
            shape((KW, 3 * share), F32),
            shape((share, HEADS), F32),
            shape((1, HEAD_SIZE), F32),
            shape(out.shape, F32),
            shape((1, share), F32),
            shape(up.shape, F32),
            shape((OWN, MODEL_WIDTH), F32),
        ],
        in_specs=[vmem] * 7,
        out_specs=[vmem] * 10,
        name="result",
    )(hidden, mix, out, up, down, small, head)


def pack_down(part):
    lead = part.shape[:-2]
    tiles = part.reshape(lead + (11, 8, 4, 2, 128))
    n = len(lead)
    moved = tiles.transpose(tuple(range(n)) + (n + 2, n + 1, n + 3, n, n + 4))
    return moved.reshape(lead + (2 * PIECE, FF))


def unpack_down(part):
    lead = part.shape[:-2]
    tiles = part.reshape(lead + (4, 8, 2, 11, 128))
    n = len(lead)
    moved = tiles.transpose(tuple(range(n)) + (n + 3, n + 1, n, n + 2, n + 4))
    return moved.reshape(lead + (OWN, MODEL_WIDTH))


def pack_taps(conv):
    taps = conv.reshape(KW, -1, 3, 2 * PIECE)
    return taps.transpose(1, 3, 0, 2).reshape(-1, 3 * KW)


def pack_small(mixer, mlp_part, beta, conv):
    parts = jnp.concatenate([mixer[:, None], mlp_part[:, None], beta, pack_taps(conv)], axis=1)
    return jnp.pad(parts, ((0, 0), (0, SMALL - parts.shape[1])))


def shards(
    tokens, cotangent, starts, mixer_gain, mix_weight, conv_weight, beta_weight, head_gain, out_weight, mlp_gain,
    upgate_weight, down_weight,
):
    rows, block, width = tokens.shape
    share = mix_weight.shape[1]
    both = ("dp", "seq")
    routed = lax.axis_size("dp") == 4 and lax.axis_size("seq") % 2 == 0 and share == 2 * PIECE
    if routed:
        weights = [
            mix_weight[0], out_weight[0], upgate_weight[0], down_weight[0], mixer_gain, mlp_gain, beta_weight[0],
            conv_weight[0],
        ]
    else:
        parts = [
            mixer_gain[0], mlp_gain[0], beta_weight[0], conv_weight[0].T, mix_weight[0], out_weight[0], upgate_weight[0],
            down_weight[0],
        ]
        parts = [lax.all_gather(part, both, axis=0, tiled=True) for part in parts]
        mixer_w, mlp_w, beta_w, conv_w, mix_w, out_w, up_w, down_w = parts
        small_w = pack_small(mixer_w, mlp_w, beta_w, conv_w.T)
        down_w = pack_down(down_w.reshape(-1, OWN, width)).reshape(-1, FF)
        weights = [jnp.concatenate([mix_w, small_w, out_w, up_w, down_w], axis=1)]

    flat = tokens.reshape(rows * block, width)
    flat_grad = cotangent.reshape(rows * block, width)
    full, normed, pre, raw, beta, solved, solved_w, fresh, state, power, outputs, gated, conv, gains = mixer_forward(
        starts, flat, head_gain, weights
    )
    output, grad_mid, grad_gated, grad_mlp, grads = mlp(full, flat, flat_grad, gated, gains)
    operands = [
        starts, grad_gated, grad_mid, flat, gains, full, conv, head_gain,
        pre, raw, beta, solved, solved_w, fresh, state, power, outputs,
    ]
    results = mixer_backward(operands, normed, grad_mlp, grads, routed)
    if routed:
        grad_hidden, out_sum, up_sum, down_sum, mix_sum, small_sum, head_sum = results
        parts = result(grad_hidden, mix_sum, out_sum, up_sum, down_sum, small_sum, head_sum)
        grad_hidden, mixer_mine, mix_mine, conv_mine, beta_mine, head_mine, out_mine, mlp_mine, up_mine, down_mine = parts
        mixer_mine, mlp_mine = mixer_mine[0], mlp_mine[0]
    else:
        grad_hidden, grad_project, grad_logits, grad_conv, grad_head, grad_mixer = results
        whole_mix = lax.dot_general(normed, grad_project, (((1,), (0,)), ((), ())), preferred_element_type=F32)
        whole_beta = lax.dot_general(normed, grad_logits, (((1,), (0,)), ((), ())), preferred_element_type=F32)
        whole_down = unpack_down(grads[:, MODEL_WIDTH + 2 * FF :].reshape(-1, 2 * PIECE, FF)).reshape(FF, width)
        listed = [
            whole_mix,
            grads[:, :MODEL_WIDTH],
            grads[:, MODEL_WIDTH : MODEL_WIDTH + 2 * FF],
            whole_down,
            grad_mixer[0],
            grad_mlp[0],
            whole_beta[:, BETA_AT:CONV_AT],
            grad_conv.T,
        ]
        listed = [
            lax.psum_scatter(part.astype(F32), both, scatter_dimension=0, tiled=True) for part in listed
        ]
        mix_mine, out_mine, up_mine, down_mine, mixer_mine, mlp_mine, beta_mine, conv_mine = listed
        conv_mine = conv_mine.T
        head_mine = lax.psum(jnp.sum(grad_head, axis=0, keepdims=True), both)
    return (
        output.reshape(rows, block, width),
        grad_hidden.reshape(rows, block, width),
        mixer_mine[None],
        mix_mine[None],
        conv_mine[None],
        beta_mine[None],
        head_mine,
        out_mine[None],
        mlp_mine[None],
        up_mine[None],
        down_mine[None],
    )


def solution(mesh):
    both = ("dp", "seq")
    in_specs = (
        P("dp", "seq", None),
        P("dp", "seq", None),
        P("dp", None),
        P(None, both),
        P(None, both, None),
        P(None, None, both),
        P(None, both, None),
        P(),
        P(None, both, None),
        P(None, both),
        P(None, both, None),
        P(None, both, None),
    )
    out_specs = (
        P("dp", "seq", None),
        P("dp", "seq", None),
        P(None, both),
        P(None, both, None),
        P(None, None, both),
        P(None, both, None),
        P(),
        P(None, both, None),
        P(None, both),
        P(None, both, None),
        P(None, both, None),
    )
    return jax.shard_map(shards, mesh=mesh, in_specs=in_specs, out_specs=out_specs, check_vma=False)
```

```python
import functools

import jax
import jax.numpy as jnp
from jax import lax
from jax.experimental import pallas as pl
from jax.experimental.pallas import tpu as pltpu
from jax.sharding import PartitionSpec as P

MODEL_WIDTH = 1024
HEADS = 8
HEAD_SIZE = 128
FF = 2816
KW = 4
PACKED = 4

MESH = pl.DeviceIdType.MESH
F32 = jnp.float32
BF16 = jnp.bfloat16
TOKENS = 128
ROWS = 2
ALL = ROWS * TOKENS
HALO = 8
NEAR_ZERO = 1e-06
HEAD_ZERO = 1e-05
MIX = 4 * MODEL_WIDTH
QKV = 3 * MODEL_WIDTH
SMALL = 128
BETA_AT = 2
CONV_AT = 10
AT_SMALL = MIX
AT_OUT = AT_SMALL + SMALL
AT_UP = AT_OUT + MODEL_WIDTH
AT_DOWN = AT_UP + 2 * FF
PACK = AT_DOWN + FF
FIRST_REST = 5504
LAST_REST = PACK - AT_OUT - FIRST_REST
CHUNK_MIX = AT_OUT // 3
PIECE = 16
SLOTS = 2
WINDOW = 24
LAG = 0
EDGE = 16
WIDE = 512
GROUP = 2
AT_PREPARE = 2
AT_CHAIN = (5, 2)
AT_FINISH = (1, 2)
AT_CONV = (0, 0)
AT_NORMED = (4, 4)
AT_END = (1, 2, 3)


def nn(a, b):
    return lax.dot_general(a, b, (((1,), (0,)), ((), ())), preferred_element_type=F32)


def nt(a, b):
    return lax.dot_general(a, b, (((1,), (1,)), ((), ())), preferred_element_type=F32)


def tn(a, b):
    return lax.dot_general(a, b, (((0,), (0,)), ((), ())), preferred_element_type=F32)


def low(value):
    return value.astype(BF16)


def when(condition, action):
    if condition is None:
        action()
    else:
        pl.when(condition)(action)


class Place:
    def __init__(self, levels):
        self.levels = levels
        self.row, self.spot = lax.axis_index("dp"), lax.axis_index("seq")
        self.level, self.core = self.spot // 2, lax.rem(self.spot, 2)
        self.near = self.row + 1 - 2 * lax.rem(self.row, 2)
        self.far = self.row + 2 - 4 * (self.row // 2)
        self.first = self.near * (1 - self.core) + self.far * self.core
        self.second = self.far * (1 - self.core) + self.near * self.core
        self.both = 3 - self.row
        self.above, self.below = self.level + 1 < levels, self.level >= 1
        self.sibling = self.spot + 1 - 2 * self.core

    def greet(self, chain):
        barrier = pltpu.get_barrier_semaphore()
        levels, level, core = self.levels, self.level, self.core

        def signal(row, spot):
            pl.semaphore_signal(barrier, inc=1, device_id={"dp": row, "seq": spot}, device_id_type=MESH)

        signal(self.first, self.spot)
        signal(self.second, self.spot)
        signal(self.row, self.sibling)
        pl.when(self.above)(lambda: signal(self.row, self.spot + 2))
        pl.when(self.below)(lambda: signal(self.row, self.spot - 2))
        has_above = (2 * levels - 2 - level) // levels
        has_below = (level + levels - 1) // levels
        peers = 3 + has_above + has_below
        if chain > 0:
            pl.when(self.below & (core == 0))(lambda: signal(self.row, self.spot - 1))
            peers = peers + has_above * core
        if chain < 0:
            pl.when(self.above & (core == 1))(lambda: signal(self.row, self.spot + 1))
            peers = peers + has_below * (1 - core)
        pl.semaphore_wait(barrier, peers)

    def rows_of(self, owner, spot, half):
        return pl.ds(pl.multiple_of(((owner * 2 * self.levels + spot) * 2 + half) * PIECE, PIECE), PIECE)


class Sender:
    def __init__(self, semaphores):
        self.semaphores, self.used, self.pending = semaphores, 0, []

    def start(self, condition, source, target, device, arrival):
        copy = pltpu.make_async_remote_copy(
            src_ref=source, dst_ref=target, send_sem=self.semaphores.at[self.used], recv_sem=arrival,
            device_id=device, device_id_type=MESH,
        )
        self.used += 1
        when(condition, copy.start)
        self.pending.append((condition, copy))

    def arrived(self, condition, target, device, arrival):
        copy = pltpu.make_async_remote_copy(
            src_ref=target, dst_ref=target, send_sem=self.semaphores.at[0], recv_sem=arrival,
            device_id=device, device_id_type=MESH,
        )
        when(condition, copy.wait_recv)

    def drain(self):
        for condition, copy in self.pending:
            when(condition, copy.wait_send)


def advance(steps, count=1):
    for _ in range(count):
        next(steps, None)


def both_advance(counts, *listed):
    for steps, count in zip(listed, counts):
        advance(steps, count)


def until(steps, mark):
    for found in steps:
        if found == mark:
            return


def gather_semaphores(levels):
    dma = pltpu.SemaphoreType.DMA
    return [dma((2, 2, levels)), dma((2, levels)), dma((2, 2, levels)), dma((2, 4, levels)), dma((8 + 34 * levels,))]


def gather_steps(at, share, full, columns, by_level, by_first, by_second, by_core, sends):
    levels, row, spot, level, core = at.levels, at.row, at.spot, at.level, at.core
    first, second, both, above, below = at.first, at.second, at.both, at.above, at.below
    sender = Sender(sends)
    here = {"dp": first, "seq": spot}

    def piece(half, owner, owner_level):
        return full.at[at.rows_of(owner, owner_level * 2 + core, half), columns]

    def send(condition, half, owner, owner_level, device, arrival):
        target = piece(half, owner, owner_level)
        own = owner is row and owner_level is level
        source = share.at[pl.ds(half * PIECE, PIECE), columns] if own else target
        sender.start(condition, source, target, device, arrival)

    def along(condition, up, half, side, owner, owner_level):
        device = {"dp": row, "seq": spot + 2 if up else spot - 2}
        send(condition, half, owner, owner_level, device, by_level.at[half, side, owner_level])

    def to_first(condition, half, owner_level):
        send(condition, half, row, owner_level, here, by_first.at[half, owner_level])

    def to_second(condition, half, side, owner, owner_level):
        device = {"dp": second, "seq": spot}
        send(condition, half, owner, owner_level, device, by_second.at[half, side, owner_level])

    def to_core(condition, half, owner, owner_level):
        device = {"dp": row, "seq": at.sibling}
        send(condition, half, owner, owner_level, device, by_core.at[half, owner, owner_level])

    def arrived(condition, half, owner, owner_level, arrival):
        sender.arrived(condition, piece(half, owner, owner_level), here, arrival)

    to_first(None, 1, level)
    along(above, True, 0, 0, row, level)
    along(below, False, 0, 0, row, level)
    to_second(None, 0, 0, row, level)
    to_first(None, 0, level)
    to_second(None, 1, 0, row, level)
    along(above, True, 1, 0, row, level)
    along(below, False, 1, 0, row, level)
    to_core(None, 0, row, level)
    to_core(None, 1, row, level)
    yield "started"
    arrived(None, 1, first, level, by_first.at[1, level])
    along(above, True, 1, 1, first, level)
    along(below, False, 1, 1, first, level)
    to_second(None, 1, 1, first, level)
    to_core(None, 1, first, level)
    yield "step"
    arrived(None, 0, first, level, by_first.at[0, level])
    to_second(None, 0, 1, first, level)
    to_core(None, 0, first, level)
    yield "step"

    def from_second(condition, owner_level, half):
        for side, owner in ((0, second), (1, both)):
            arrived(condition, half, owner, owner_level, by_second.at[half, side, owner_level])
            to_core(condition, half, owner, owner_level)

    waiting = [(None, level)]
    for step in range(1, levels):
        ways = ((level - step >= 0, level - step, True), (level + step < levels, level + step, False))

        def onward(up, step=step):
            if up:
                return (level - step >= 0) & above
            return (level + step < levels) & below

        for condition, source, up in ways:
            arrived(condition, 0, row, source, by_level.at[0, 0, source])
            if step < levels - 1:
                along(onward(up), up, 0, 0, row, source)
            to_first(condition, 0, source)
            to_second(condition, 0, 0, row, source)
            to_core(condition, 0, row, source)
        yield "step"
        for side, owner in ((0, row), (1, first)):
            for condition, source, up in ways:
                arrived(condition, 1, owner, source, by_level.at[1, side, source])
                if step < levels - 1:
                    along(onward(up), up, 1, side, owner, source)
                to_second(condition, 1, side, owner, source)
                to_core(condition, 1, owner, source)
            yield "step"
        for condition, source, up in ways:
            arrived(condition, 0, first, source, by_first.at[0, source])
            to_second(condition, 0, 1, first, source)
            to_core(condition, 0, first, source)
        yield "step"
        if step == levels - 1:
            yield "leveled"
        for half in range(2):
            for condition, source in waiting:
                from_second(condition, source, half)
            yield "step"
        waiting = [(condition, source) for condition, source, _ in ways]
    for half in range(2):
        for condition, source in waiting:
            from_second(condition, source, half)
        yield "step"
    yield "issued"
    for half in range(2):
        for owner in range(4):
            for source in range(levels):
                target = full.at[at.rows_of(owner, source * 2 + 1 - core, half), columns]
                sender.arrived(None, target, here, by_core.at[half, owner, source])
    yield "arrived"
    sender.drain()


def scatter_buffers(levels, width, staged):
    dma = pltpu.SemaphoreType.DMA
    buffers = [
        pltpu.VMEM((2, 4, levels, PIECE, width), BF16),
        pltpu.VMEM((2, 2, levels, PIECE, width), BF16),
        pltpu.VMEM((levels + 1, PIECE, width), BF16),
        pltpu.VMEM((3, levels + 1, PIECE, width), BF16),
        dma((2, 4, levels)),
        dma((2, 2, levels)),
        dma((levels + 1,)),
        dma((3, levels + 1)),
        dma((8 + 44 * levels,)),
    ]
    if staged:
        buffers += [pltpu.VMEM((SLOTS, PIECE, width), BF16), dma((SLOTS,))]
    return buffers


def scatter_steps(
    at, columns, chunk, grads, targets, total, by_second, by_first, by_level,
    core_sem, second_sem, first_sem, level_sem, sends, staged=None, load_sem=None,
):
    levels, row, spot, level, core = at.levels, at.row, at.spot, at.level, at.core
    first, second, both, above, below = at.first, at.second, at.both, at.above, at.below
    sender = Sender(sends)
    here = {"dp": first, "seq": spot}
    begin, width = columns
    columns = pl.ds(begin, width)
    ways = [(far, up) for far in range(levels - 1, 0, -1) for up in (True, False)] + [(0, True)]

    def there(way):
        far, up = way
        if far == 0:
            return None, level
        return (level + far < levels, level + far) if up else (level - far >= 0, level - far)

    def add(target, other):
        def body(step, _):
            part = pl.ds(pl.multiple_of(step * chunk, chunk), chunk)
            target[:, part] = target[:, part] + other[:, part]
            return 0

        lax.fori_loop(0, width // chunk, body, 0)

    def arrived(target, arrival):
        sender.arrived(None, target, here, arrival)

    def listing(one, two):
        out = []
        for turn in range(len(ways) + LAG):
            if turn < len(ways):
                out += [(True, ways[turn], half, side, owner) for half in (1, 0) for side, owner in ((0, one), (1, both))]
            if turn >= LAG:
                out += [(False, ways[turn - LAG], half, side, owner) for half in (1, 0) for side, owner in ((0, row), (1, two))]
        return out

    listed = listing(second, first)
    given = listing(first, second)

    def to_core(number):
        _, way, half, _, owner = given[number]
        condition, end = there(way)
        device = {"dp": row, "seq": at.sibling}
        source = grads.at[at.rows_of(owner, end * 2 + 1 - core, half), columns]
        sender.start(condition, source, total.at[half, owner, end], device, core_sem.at[half, owner, end])

    for number in range(WINDOW):
        to_core(number)

    def load(number):
        _, way, half, _, owner = listed[number]
        slot = number % SLOTS
        source = grads.at[at.rows_of(owner, there(way)[1] * 2 + core, half), columns]
        return pltpu.make_async_copy(source, staged.at[slot], load_sem.at[slot])

    def start_load(number):
        if staged is not None and number < len(listed):
            when(there(listed[number][1])[0], lambda: load(number).start())

    for slot in range(SLOTS):
        start_load(slot)
    yield "started"

    def take_listed(number):
        leaves, way, half, side, owner = listed[number]
        if number + WINDOW < len(listed):
            to_core(number + WINDOW)
        condition, end = there(way)
        sums = total.at[half, owner, end]

        def take():
            if staged is not None:
                load(number).wait()
            arrived(sums, core_sem.at[half, owner, end])
            if staged is None:
                add(sums, grads.at[at.rows_of(owner, end * 2 + core, half), columns])
            else:
                add(sums, staged.at[number % SLOTS])

        when(condition, take)
        start_load(number + SLOTS)
        if leaves:
            device = {"dp": second, "seq": spot}
            sender.start(condition, sums, by_second.at[half, side, end], device, second_sem.at[half, side, end])

    for number in range(len(listed)):
        take_listed(number)
        if number % 4 == 3:
            yield "step"
    yield "sent"

    def along(half, side, owner, way):
        far, up = way
        if far == 0:
            return
        condition, end = there(way)
        sums = total.at[half, owner, end]
        place = 0 if half == 0 else 1 + side
        if far < levels - 1:

            def take():
                arrived(by_level.at[place, end], level_sem.at[place, end])
                add(sums, by_level.at[place, end])

            pl.when(condition & (below if up else above))(take)
        slot = end if up or far > 1 else levels
        device = {"dp": row, "seq": spot + 2 if up else spot - 2}
        sender.start(condition, sums, by_level.at[place, slot], device, level_sem.at[place, slot])

    def from_second(half, side, owner, way):
        condition, end = there(way)

        def take():
            arrived(by_second.at[half, side, end], second_sem.at[half, side, end])
            add(total.at[half, owner, end], by_second.at[half, side, end])

        when(condition, take)

    def from_first(way):
        condition, end = there(way)

        def take():
            arrived(by_first.at[end], first_sem.at[end])
            add(total.at[0, row, end], by_first.at[end])

        when(condition, take)
        along(0, 0, row, way)

    previous = None
    for way in ways:
        condition, end = there(way)
        for side, owner in ((0, row), (1, first)):
            from_second(1, side, owner, way)
            along(1, side, owner, way)
        yield "step"
        from_second(0, 1, first, way)
        sender.start(condition, total.at[0, first, end], by_first.at[end], here, first_sem.at[end])
        from_second(0, 0, row, way)
        yield "step"
        if previous is not None:
            from_first(previous)
            yield "step"
        previous = way
    from_first(previous)
    yield "step"

    def collect(half, side, owner):
        sums = total.at[half, owner, level]
        place = 0 if half == 0 else 1 + side

        def take(slot):
            arrived(by_level.at[place, slot], level_sem.at[place, slot])
            add(sums, by_level.at[place, slot])

        pl.when(below)(lambda: take(level))
        pl.when(above)(lambda: take(levels))

    def final(half, *parts):
        rows, at_part = pl.ds(half * PIECE, PIECE), 0
        for target, start, length in targets:
            part = pl.ds(at_part, length)
            value = parts[0][:, part].astype(F32)
            for other in parts[1:]:
                value = value + other[:, part].astype(F32)
            target[rows, pl.ds(start, length)] = value
            at_part += length

    collect(1, 1, first)
    sender.start(None, total.at[1, first, level], by_first.at[levels], here, first_sem.at[levels])
    yield "step"
    collect(1, 0, row)
    yield "step"
    collect(0, 0, row)
    final(0, total.at[0, row, level])
    yield "step"
    arrived(by_first.at[levels], first_sem.at[levels])
    final(1, total.at[1, row, level], by_first.at[levels])
    sender.drain()


def segment(starts, row, places):
    total = jnp.zeros_like(places)
    for k in range(PACKED):
        begin = starts[row, k]
        total = total + jnp.where((begin > 0) & (places >= begin), 1, 0)
    return total


def row_scalars(starts, row, first):
    before = jnp.int32(0)
    last = jnp.int32(0)
    for k in range(PACKED):
        begin = starts[row, k]
        before = before + jnp.where((begin > 0) & (begin <= first - 1), 1, 0)
        last = last + jnp.where((begin > 0) & (begin <= first + TOKENS - 1), 1, 0)
    return before, last


def fill_masks(starts, first, carry_in, carry_out, taps, within, below):
    places = first + lax.broadcasted_iota(jnp.int32, (TOKENS, HEAD_SIZE), 0)
    side = lax.broadcasted_iota(jnp.int32, (TOKENS, TOKENS), 0)
    across = lax.broadcasted_iota(jnp.int32, (TOKENS, TOKENS), 1)
    within[...] = jnp.zeros_like(within)
    below[...] = jnp.zeros_like(below)
    for row in range(ROWS):
        span = pl.ds(row * TOKENS, TOKENS)
        mine = segment(starts, row, places)
        before, last = row_scalars(starts, row, first)
        carry_in[span, :] = (mine == before).astype(F32)
        carry_out[span, :] = (mine == last).astype(F32)
        for shift in range(1, KW):
            there = places - shift
            same = (segment(starts, row, there) == mine) & (there >= 0)
            taps[shift - 1, span, :] = same.astype(F32)
        same = segment(starts, row, first + side) == segment(starts, row, first + across)
        within[span, span] = (same & (side >= across)).astype(F32)
        below[span, span] = (same & (side > across)).astype(F32)


def padded(main, halo):
    return jnp.concatenate([halo, main], axis=0)


def unit_scale(values):
    return lax.rsqrt(jnp.sum(values * values, axis=-1, keepdims=True) + NEAR_ZERO)


def lane_of(values, lane):
    lanes = lax.broadcasted_iota(jnp.int32, values.shape, 1)
    return jnp.sum(jnp.where(lanes == lane, values, 0.0), axis=-1, keepdims=True)


def head_columns(part, head):
    return pl.ds(pl.multiple_of(part * MODEL_WIDTH + head * HEAD_SIZE, HEAD_SIZE), HEAD_SIZE)


def halves(value):
    high = low(value)
    return high, low(value - high.astype(F32))


def gram_of(keys):
    high, rest = halves(keys)
    return nt(high, high) + nt(high, rest) + nt(rest, high)


def per_row(function, *arrays):
    return jnp.concatenate(
        [
            function(row, *[array[row * TOKENS : (row + 1) * TOKENS] for array in arrays])
            for row in range(ROWS)
        ],
        axis=0,
    )


def invert(system, apart):
    eye = jnp.where(apart == 0, 1.0, 0.0)
    solved = eye - jnp.where(apart == 1, system, 0.0)
    size = 2
    while size < TOKENS:
        cross = low(jnp.where((apart >= size) & (apart < 2 * size), system, 0.0))
        rough = low(solved)
        solved = solved - nn(low(nn(rough, cross)), rough)
        size *= 2
    return solved


def kappa_eye(kept):
    side = lax.broadcasted_iota(jnp.int32, (HEAD_SIZE, HEAD_SIZE), 0)
    across = lax.broadcasted_iota(jnp.int32, (HEAD_SIZE, HEAD_SIZE), 1)
    return jnp.where(side == across, 1.0, 0.0) * kept


def tap_moves():
    group = 3 * HEAD_SIZE
    side = lax.broadcasted_iota(jnp.int32, (group, group), 0)
    across = lax.broadcasted_iota(jnp.int32, (group, group), 1)
    third, device, lane = side // HEAD_SIZE, (side % HEAD_SIZE) // 32, side % 32
    return jnp.where(across == device * 96 + third * 32 + lane, 1.0, 0.0).astype(BF16)


def tap_rows(small_rows):
    move = tap_moves()
    wanted = []
    for block in range(MODEL_WIDTH // HEAD_SIZE):
        lanes = slice(block * HEAD_SIZE, (block + 1) * HEAD_SIZE)
        parts = [small_rows[CONV_AT + 3 * j : CONV_AT + 3 * j + 3, lanes] for j in range(KW)]
        source = jnp.concatenate(
            [jnp.concatenate([part[c : c + 1] for c in range(3)], axis=1) for part in parts], axis=0
        )
        wanted.append(nn(low(source), move))
    return wanted


def pack_few(target, turned, mixer_gain, mlp_gain, beta, conv):
    turned[...] = jnp.zeros_like(turned)
    share = 2 * PIECE
    turned[0:1, 0:share] = mixer_gain[...].astype(F32)
    turned[1:2, 0:share] = mlp_gain[...].astype(F32)
    taps = conv[...].astype(F32)
    for tap in range(KW):
        for third in range(3):
            place = CONV_AT + 3 * tap + third
            turned[place : place + 1, 0:share] = taps[tap : tap + 1, third * share : (third + 1) * share]
    value = turned[...].T[:share]
    turned[...] = jnp.zeros_like(turned)
    turned[0:share, BETA_AT:CONV_AT] = beta[...].astype(F32)
    target[:, AT_SMALL:AT_OUT] = low(value + turned[0:share, :])


def mixer_forward_kernel(routed, *refs):
    (starts, tokens, head_gain), refs = refs[:3], refs[3:]
    if routed:
        (mix_share, out_share, up_share, down_share, *few), refs = refs[:8], refs[8:]
    (full, normed, pre_low, raw, beta, solved, solved_w, fresh, state, power, outputs, gated, conv, gains), refs = refs[:14], refs[14:]
    (every, carry_in, carry_out, taps, within, below, apart), refs = refs[:7], refs[7:]
    (offset, solved_u, attend, queries, arriving, leaving, send, receive), refs = refs[:8], refs[8:]
    (mix, small, halo, halo_send, halo_receive, load_sem, pre), refs = refs[:7], refs[7:]
    count = lax.axis_size("seq")
    index = lax.axis_index("seq")
    first = index * TOKENS
    rest = iter(())
    if routed:
        keep_sem, packed, turned = refs[:3]
        routes = refs[3:]
        at = Place(count // 2)

        def keep(number, share, begin):
            columns = pl.ds(begin, share.shape[-1])
            copy = pltpu.make_async_copy(share, packed.at[:, columns], keep_sem.at[number])
            copy.start()
            return copy

        kept = [keep(0, mix_share, 0), keep(1, out_share, AT_OUT), keep(2, up_share, AT_UP)]
        pack_few(packed, turned, *few)
        at.greet(1)
    else:
        barrier = pltpu.get_barrier_semaphore()

        @pl.when(index > 0)
        def _():
            pl.semaphore_signal(barrier, inc=1, device_id={"seq": index - 1}, device_id_type=MESH)

        @pl.when(index + 1 < count)
        def _():
            pl.semaphore_wait(barrier, 1)

    def tail(row):
        return pltpu.make_async_remote_copy(
            src_ref=tokens.at[pl.ds((row + 1) * TOKENS - EDGE, EDGE), :], dst_ref=halo.at[pl.ds(row * EDGE, EDGE), :],
            send_sem=halo_send.at[row], recv_sem=halo_receive.at[row], device_id={"seq": index + 1}, device_id_type=MESH,
        )

    @pl.when(index + 1 < count)
    def _():
        for row in range(ROWS):
            tail(row).start()

    if routed:
        kept[0].wait()
        wanted = gather_steps(at, packed, full, pl.ds(0, AT_OUT), *routes[:5])
        until(wanted, "started")
        rows = down_share[...].astype(F32)

        def store(row, column, value):
            packed[row : row + PIECE, AT_DOWN + column : AT_DOWN + column + 128] = low(value)

        pack_hand(rows, 0, store)

    @pl.when(index == 0)
    def _():
        arriving[...] = jnp.zeros_like(arriving)
        halo[...] = jnp.zeros_like(halo)

    fill_masks(starts, first, carry_in, carry_out, taps, within, below)
    side = lax.broadcasted_iota(jnp.int32, (ALL, ALL), 0)
    across = lax.broadcasted_iota(jnp.int32, (ALL, ALL), 1)
    apart[...] = jnp.bitwise_xor(side, across)
    if routed:
        kept[1].wait()
        kept[2].wait()
        mine = pl.ds(pl.multiple_of((at.row * count + index) * 2 * PIECE, 2 * PIECE), 2 * PIECE)
        own = pltpu.make_async_copy(packed, full.at[mine, :], keep_sem.at[3])
        own.start()
        until(wanted, "issued")
        rest = gather_steps(at, packed, full, pl.ds(AT_OUT, PACK - AT_OUT), *routes[5:])
        until(rest, "started")
        until(wanted, "arrived")
        own.wait()

    def load(number):
        if number < 0:
            return pltpu.make_async_copy(full.at[:, pl.ds(AT_SMALL, SMALL)], small, load_sem.at[MIX // WIDE])
        columns = pl.ds(number * WIDE, WIDE)
        return pltpu.make_async_copy(full.at[:, columns], mix.at[:, columns], load_sem.at[number])

    for number in range(-1, MIX // WIDE):
        load(number).start()
    load(-1).wait()
    small_rows = small[:, pl.ds(0, HEAD_SIZE)].astype(F32).T
    gains[...] = small_rows[:8]
    for block, part in enumerate(tap_rows(small_rows)):
        conv[:, pl.ds(block * 3 * HEAD_SIZE, 3 * HEAD_SIZE)] = part

    def norm(source, target, rows):
        values = source[...].astype(F32)
        scale = lax.rsqrt(jnp.mean(values * values, axis=-1, keepdims=True) + NEAR_ZERO)
        target[rows, :] = low(values * scale * gains[0:1, :])

    norm(tokens, every, pl.ds(0, ALL))

    @pl.when(index > 0)
    def _():
        for row in range(ROWS):
            tail(row).wait_recv()

    norm(halo, every, pl.ds(ALL, ROWS * EDGE))
    normed[...] = low(every[pl.ds(0, ALL), :].astype(F32).T)
    beta[...] = jax.nn.sigmoid(nn(every[pl.ds(0, ALL), :], small[...]))
    for number in range(MIX // WIDE):
        load(number).wait()
        columns = pl.ds(number * WIDE, WIDE)
        wide = nn(every[...], mix[:, columns])
        pre[:, columns] = wide
        pre_low[:, columns] = low(wide)

    def convolve(columns):
        weight = conv[:, columns]
        rows = []
        for row in range(ROWS):
            main = pre[pl.ds(row * TOKENS, TOKENS), columns]
            before = pre[pl.ds(ALL + (row + 1) * EDGE - HALO, HALO), columns]
            longer = padded(main, before)
            total = weight[0:1] * main
            for shift in range(1, KW):
                tap = taps[shift - 1, pl.ds(row * TOKENS, TOKENS), :]
                total = total + weight[shift : shift + 1] * longer[HALO - shift : HALO - shift + TOKENS] * tap
            rows.append(total)
        total = jnp.concatenate(rows, axis=0)
        raw[:, columns] = low(total)
        return total * jax.nn.sigmoid(total)

    def local(head):
        active_q = convolve(head_columns(0, head))
        active_k = convolve(head_columns(1, head))
        values = convolve(head_columns(2, head))
        query = active_q * (unit_scale(active_q) * HEAD_SIZE**-0.5)
        key = active_k * unit_scale(active_k)
        strength = lane_of(beta[...], BETA_AT + head)
        columns = head_columns(0, head)
        system = below[...] * (strength * gram_of(key))
        inverse = low(invert(system, apart[...]))
        solved[head] = inverse
        enter = carry_in[...]
        w = low(nn(inverse, low(strength * enter * key)))
        u = nn(inverse, low(strength * values))
        solved_w[:, columns] = w
        solved_u[:, columns] = u
        leave = low(carry_out[...] * key)
        u_low = low(u)
        for row in range(ROWS):
            span = slice(row * TOKENS, (row + 1) * TOKENS)
            before, last = row_scalars(starts, row, first)
            kept = jnp.where(before == last, 1.0, 0.0)
            power[head, row] = low(kappa_eye(kept) - tn(leave[span], w[span]))
            offset[head, row] = tn(leave[span], u_low[span])
        attend[head] = low(within[...] * nt(low(query), low(key)))
        queries[:, columns] = low(enter * query)


    for step in range(HEADS // GROUP):
        for part in range(GROUP):
            local(step * GROUP + part)
        advance(rest, 2)

    def copy(head):
        return pltpu.make_async_remote_copy(
            src_ref=leaving.at[head], dst_ref=arriving.at[head], send_sem=send.at[head], recv_sem=receive.at[head],
            device_id={"seq": index + 1}, device_id_type=MESH,
        )

    def chain(head):
        @pl.when(index > 0)
        def _():
            copy(head).wait_recv()

        @pl.when(index + 1 < count)
        def _():
            for row in range(ROWS):
                leaving[head, row] = low(nn(power[head, row], arriving[head, row]) + offset[head, row])
            copy(head).start()

        columns = head_columns(0, head)
        w, u, query = solved_w[:, columns], solved_u[:, columns], queries[:, columns]
        x = low(u - per_row(lambda row, part: nn(part, arriving[head, row]), w))
        fresh[:, columns] = x
        output = per_row(lambda row, part: nn(part, arriving[head, row]), query) + nn(attend[head], x)
        outputs[:, columns] = output
        scale = lax.rsqrt(jnp.mean(output * output, axis=-1, keepdims=True) + HEAD_ZERO)
        gate = pre[pl.ds(0, ALL), head_columns(3, head)]
        gated[:, columns] = low(output * scale * head_gain[...].astype(F32) * (gate * jax.nn.sigmoid(gate)))

    advance(rest, 8)
    for head in range(HEADS):
        chain(head)
        advance(rest)
    state[...] = arriving[...]

    @pl.when(index + 1 < count)
    def _():
        for row in range(ROWS):
            tail(row).wait_send()

        def drain(head, _):
            copy(head).wait_send()
            return 0

        lax.fori_loop(0, HEADS, drain, 0)

    until(rest, "end")
    if routed:
        until(wanted, "end")


def mixer_forward(starts, tokens, head_gain, weights):
    routed = len(weights) > 1
    vmem, anywhere = pl.BlockSpec(memory_space=pltpu.VMEM), pl.BlockSpec(memory_space=pl.ANY)
    dma = pltpu.SemaphoreType.DMA
    shape = jax.ShapeDtypeStruct
    states = (HEADS, ROWS, HEAD_SIZE, HEAD_SIZE)
    long = ALL + ROWS * EDGE
    whole = [shape((MODEL_WIDTH, PACK), BF16)] if routed else []
    levels = lax.axis_size("seq") // 2
    routes = []
    if routed:
        routes = [
            dma((4,)),
            pltpu.VMEM((2 * PIECE, PACK), BF16),
            pltpu.VMEM((SMALL, SMALL), F32),
        ]
        routes += gather_semaphores(levels) + gather_semaphores(levels)
    results = pl.pallas_call(
        functools.partial(mixer_forward_kernel, routed),
        out_shape=whole + [
            shape((MODEL_WIDTH, ALL), BF16),
            shape((long, MIX), BF16),
            shape((ALL, QKV), BF16),
            shape((ALL, SMALL), F32),
            shape((HEADS, ALL, ALL), BF16),
            shape((ALL, MODEL_WIDTH), BF16),
            shape((ALL, MODEL_WIDTH), BF16),
            shape(states, BF16),
            shape(states, BF16),
            shape((ALL, MODEL_WIDTH), F32),
            shape((ALL, MODEL_WIDTH), BF16),
            shape((KW, QKV), F32),
            shape((8, MODEL_WIDTH), F32),
        ],
        in_specs=[pl.BlockSpec(memory_space=pltpu.SMEM), vmem, vmem] + ([anywhere] * 3 + [vmem] * 5 if routed else [anywhere]),
        out_specs=[anywhere] * len(whole) + [vmem] * 13,
        scratch_shapes=[
            pltpu.VMEM((long, MODEL_WIDTH), BF16),
            pltpu.VMEM((ALL, HEAD_SIZE), F32),
            pltpu.VMEM((ALL, HEAD_SIZE), F32),
            pltpu.VMEM((KW - 1, ALL, HEAD_SIZE), F32),
            pltpu.VMEM((ALL, ALL), F32),
            pltpu.VMEM((ALL, ALL), F32),
            pltpu.VMEM((ALL, ALL), jnp.int32),
            pltpu.VMEM(states, F32),
            pltpu.VMEM((ALL, MODEL_WIDTH), F32),
            pltpu.VMEM((HEADS, ALL, ALL), BF16),
            pltpu.VMEM((ALL, MODEL_WIDTH), BF16),
            pltpu.VMEM(states, BF16),
            pltpu.VMEM(states, BF16),
            dma((HEADS,)),
            dma((HEADS,)),
            pltpu.VMEM((MODEL_WIDTH, MIX), BF16),
            pltpu.VMEM((MODEL_WIDTH, SMALL), BF16),
            pltpu.VMEM((ROWS * EDGE, MODEL_WIDTH), BF16),
            dma((ROWS,)),
            dma((ROWS,)),
            dma((MIX // WIDE + 1,)),
            pltpu.VMEM((long, MIX), F32),
        ] + routes,
        compiler_params=pltpu.CompilerParams(
            collective_id=1, has_side_effects=True, vmem_limit_bytes=56 * 2**20
        ),
        name="mixer_forward",
    )(starts, tokens, head_gain, *weights)
    return results if routed else [weights[0]] + list(results)


def mixer_backward_kernel(routed, *refs):
    (starts, grad_gated, grad_mid, tokens, gains, full, conv, head_gain), refs = refs[:8], refs[8:]
    (pre, raw, beta, solved, solved_w, fresh, state, power, outputs), refs = refs[:9], refs[9:]
    if routed:
        (normed_t, grad_mlp, grads), refs = refs[:3], refs[3:]
        (grad_hidden, *targets), refs = refs[:4], refs[4:]
        (mix_sum, small_sum, head_sum), refs = refs[:3], refs[3:]
        (grad_project, grad_logits, grad_conv, grad_head, grad_gain), refs = refs[:5], refs[5:]
    else:
        (grad_hidden, grad_project, grad_logits, grad_conv, grad_head, grad_gain), refs = refs[:6], refs[6:]
    (carry_in, carry_out, taps, within, below), refs = refs[:5], refs[5:]
    (grad_out, grad_raw, grad_beta, arriving, leaving, halo_out, halo_in), refs = refs[:7], refs[7:]
    (send, receive, halo_send, halo_receive, mix, load_sem), refs = refs[:6], refs[6:]
    fresh_part, offset = grad_hidden, grad_raw
    small = mix.at[:, pl.ds(AT_SMALL, SMALL)]
    count = lax.axis_size("seq")
    index = lax.axis_index("seq")
    first = index * TOKENS
    sums = after = iter(())
    if routed:
        at = Place(count // 2)
        at.greet(-1)
        parts, by_level, part_sem, level_sem, head_sends = refs[:5]
        refs = refs[5:]
        out_sum, up_sum, down_sum = targets
        cut = FIRST_REST - MODEL_WIDTH
        sums = scatter_steps(
            at, (0, FIRST_REST), FIRST_REST, grads, ((out_sum, 0, MODEL_WIDTH), (up_sum, 0, cut)), *refs[:11]
        )
        after = scatter_steps(
            at, (FIRST_REST, LAST_REST), LAST_REST, grads, ((up_sum, cut, 2 * FF - cut), (down_sum, 0, FF)), *refs[11:22]
        )
        until(sums, "started")
    else:
        barrier = pltpu.get_barrier_semaphore()

        @pl.when(index + 1 < count)
        def _():
            pl.semaphore_signal(barrier, inc=1, device_id={"seq": index + 1}, device_id_type=MESH)

        @pl.when(index > 0)
        def _():
            pl.semaphore_wait(barrier, 1)

    load_mix = pltpu.make_async_copy(full.at[:, pl.ds(0, AT_OUT)], mix, load_sem)
    load_mix.start()

    @pl.when(index + 1 == count)
    def _():
        arriving[...] = jnp.zeros_like(arriving)
        halo_in[...] = jnp.zeros_like(halo_in)

    fill_masks(starts, first, carry_in, carry_out, taps, within, below)
    grad_head[...] = jnp.zeros_like(grad_head)
    grad_beta[...] = jnp.zeros_like(grad_beta)

    def active_of(part, head):
        values = raw[:, head_columns(part, head)].astype(F32)
        return values * jax.nn.sigmoid(values)

    def prepare(head):
        columns = head_columns(0, head)
        gate_columns = head_columns(3, head)
        gate = pre[pl.ds(0, ALL), gate_columns].astype(F32)
        sigma = jax.nn.sigmoid(gate)
        output = outputs[:, columns]
        scale = lax.rsqrt(jnp.mean(output * output, axis=-1, keepdims=True) + HEAD_ZERO)
        sample = output * scale
        incoming = grad_gated[:, columns]
        gain = head_gain[...].astype(F32)
        grad_project[:, gate_columns] = low(incoming * sample * gain * (sigma * (1.0 + gate * (1.0 - sigma))))
        grad_sample = incoming * (gate * sigma)
        grad_head[0:1, :] += jnp.sum(grad_sample * sample, axis=0, keepdims=True)
        scaled = grad_sample * gain
        mean = jnp.mean(scaled * output, axis=-1, keepdims=True)
        here = low(scale * scaled - output * (scale * scale * scale * mean))
        grad_out[:, columns] = here
        active_q, active_k = active_of(0, head), active_of(1, head)
        query = active_q * (unit_scale(active_q) * HEAD_SIZE**-0.5)
        key = active_k * unit_scale(active_k)
        attend = low(within[...] * nt(low(query), low(key)))
        part = tn(attend, here)
        fresh_part[:, columns] = part
        entering = low(carry_in[...] * query)
        part_low = low(part)
        w = solved_w[:, columns]
        for row in range(ROWS):
            span = slice(row * TOKENS, (row + 1) * TOKENS)
            offset[span, columns] = tn(entering[span], here[span]) - tn(w[span], part_low[span])

    for head in range(HEADS):
        prepare(head)
        advance(sums, AT_PREPARE)

    def copy(head):
        return pltpu.make_async_remote_copy(
            src_ref=leaving.at[head], dst_ref=arriving.at[head], send_sem=send.at[head], recv_sem=receive.at[head],
            device_id={"seq": index - 1}, device_id_type=MESH,
        )

    def chain(head):
        @pl.when(index + 1 < count)
        def _():
            copy(head).wait_recv()

        @pl.when(index > 0)
        def _():
            for row in range(ROWS):
                start = offset[pl.ds(row * TOKENS, TOKENS), head_columns(0, head)]
                leaving[head, row] = low(tn(power[head, row], arriving[head, row]) + start)
            copy(head).start()

    until(after, "started")
    both_advance(AT_CHAIN, sums, after)
    more = iter(())
    if routed:
        sender = Sender(head_sends)

        def exchange(number, value, row, spot):
            parts[2 * number] = value
            device = {"dp": row, "seq": spot}
            sender.start(None, parts.at[2 * number], parts.at[2 * number + 1], device, part_sem.at[number])
            return lambda: sender.arrived(None, parts.at[2 * number + 1], device, part_sem.at[number])

        pending = exchange(0, grad_head[...], at.row, at.sibling)

    for head in range(HEADS):
        chain(head)

    def finish(head):
        columns = head_columns(0, head)
        raw_q, raw_k = raw[:, columns].astype(F32), raw[:, head_columns(1, head)].astype(F32)
        raw_v = raw[:, head_columns(2, head)].astype(F32)
        sigma_q, sigma_k, sigma_v = jax.nn.sigmoid(raw_q), jax.nn.sigmoid(raw_k), jax.nn.sigmoid(raw_v)
        active_q, active_k, values = raw_q * sigma_q, raw_k * sigma_k, raw_v * sigma_v
        scale_q, scale_k = unit_scale(active_q), unit_scale(active_k)
        query = low(active_q * (scale_q * HEAD_SIZE**-0.5))
        key_full = active_k * scale_k
        key = low(key_full)
        enter, leave = carry_in[...], carry_out[...]
        strength = lane_of(beta[...], BETA_AT + head)
        here = grad_out[:, columns]
        x = fresh[:, columns]
        leaving_keys = low(leave * key_full)
        grad_x = fresh_part[:, columns] + per_row(lambda row, part: nn(part, arriving[head, row]), leaving_keys)
        y = tn(solved[head], low(grad_x))
        y_low = low(y)
        grad_attend = low(within[...] * nt(here, x))
        gram = gram_of(key_full)
        grad_system = -below[...] * nt(y_low, x)
        grad_gram = low(strength * grad_system)
        grad_q = nn(grad_attend, key) + enter * per_row(lambda row, part: nt(part, state[head, row]), here)
        grad_k = (
            tn(grad_attend, query)
            + leave * per_row(lambda row, part: nt(part, arriving[head, row]), x)
            + nn(grad_gram, key)
            + tn(grad_gram, key)
            - strength * enter * per_row(lambda row, part: nt(part, state[head, row]), y_low)
        )
        z = values - enter * per_row(lambda row, part: nn(part, state[head, row]), key)
        grad_v = strength * y
        grad_strength = jnp.sum(y * z, axis=-1, keepdims=True) + jnp.sum(grad_system * gram, axis=-1, keepdims=True)
        lanes = lax.broadcasted_iota(jnp.int32, grad_beta.shape, 1)
        grad_beta[...] = jnp.where(lanes == BETA_AT + head, grad_strength, grad_beta[...])

        def through(grad, active, scale, part, sigma, extra):
            grad = grad * extra
            mean = jnp.sum(active * grad, axis=-1, keepdims=True)
            grad = scale * grad - active * (scale * scale * scale * mean)
            return grad * (sigma * (1.0 + part * (1.0 - sigma)))

        grad_raw[:, columns] = through(grad_q, active_q, scale_q, raw_q, sigma_q, HEAD_SIZE**-0.5)
        grad_raw[:, head_columns(1, head)] = through(grad_k, active_k, scale_k, raw_k, sigma_k, 1.0)
        grad_raw[:, head_columns(2, head)] = grad_v * (sigma_v * (1.0 + raw_v * (1.0 - sigma_v)))

    for head in range(HEADS):
        finish(head)
        both_advance(AT_FINISH, sums, after)

    def convolve_back(step, _):
        columns = pl.ds(pl.multiple_of(step * HEAD_SIZE, HEAD_SIZE), HEAD_SIZE)
        weight = conv[:, columns]
        nothing = jnp.zeros((HALO, HEAD_SIZE), F32)
        sums = [jnp.zeros((1, HEAD_SIZE), F32) for _ in range(KW)]
        early = []
        for row in range(ROWS):
            span = pl.ds(row * TOKENS, TOKENS)
            grad = grad_raw[span, columns]
            main = pre[span, columns].astype(F32)
            edge = pre[pl.ds(ALL + row * EDGE, EDGE), columns].astype(F32)
            longer = padded(main, edge[EDGE - HALO :])
            total = weight[0:1] * jnp.concatenate([nothing, grad], axis=0)
            sums[0] = sums[0] + jnp.sum(grad * main, axis=0, keepdims=True)
            for shift in range(1, KW):
                masked = grad * taps[shift - 1, span, :]
                wide = jnp.concatenate([nothing, masked, nothing], axis=0)
                total = total + weight[shift : shift + 1] * wide[shift : shift + HALO + TOKENS]
                before = longer[HALO - shift : HALO - shift + TOKENS]
                sums[shift] = sums[shift] + jnp.sum(masked * before, axis=0, keepdims=True)
            early.append(total[:HALO])
            grad_raw[span, columns] = total[HALO:]
        halo_out[:, columns] = low(jnp.concatenate(early, axis=0))
        grad_conv[:, columns] = jnp.concatenate(sums, axis=0)
        return 0

    for part in range(3):
        lax.fori_loop(part * HEADS, (part + 1) * HEADS, convolve_back, 0)
        both_advance(AT_CONV, sums, after)
    back = pltpu.make_async_remote_copy(
        src_ref=halo_out, dst_ref=halo_in, send_sem=halo_send, recv_sem=halo_receive,
        device_id={"seq": index - 1}, device_id_type=MESH,
    )

    @pl.when(index > 0)
    def _():
        back.start()

    strengths = beta[...]
    grad_logits[...] = low(grad_beta[...] * strengths * (1.0 - strengths))

    @pl.when(index + 1 < count)
    def _():
        back.wait_recv()

    for row in range(ROWS):
        end = pl.ds((row + 1) * TOKENS - HALO, HALO)
        grad_raw[end, :] += halo_in[...].astype(F32)[row * HALO : (row + 1) * HALO]

    def narrow(step, _):
        rows = pl.ds(pl.multiple_of(step * 32, 32), 32)
        grad_project[rows, pl.ds(0, QKV)] = low(grad_raw[rows, :])
        return 0

    lax.fori_loop(0, ALL // 32, narrow, 0)

    load_mix.wait()
    both_advance(AT_NORMED, sums, after)

    def normed_back(step, _):
        rows = pl.ds(pl.multiple_of(step * 256, 256), 256)
        grad_hidden[:, rows] = nt(grad_project[...], mix[rows, pl.ds(0, MIX)]) + nt(grad_logits[...], small[rows, :])
        return 0

    lax.fori_loop(0, MODEL_WIDTH // 256, normed_back, 0)
    grad_gain[...] = jnp.zeros_like(grad_gain)

    def hidden_back(step, _):
        rows = pl.ds(pl.multiple_of(step * 32, 32), 32)
        hidden = tokens[rows, :].astype(F32)
        scale = lax.rsqrt(jnp.mean(hidden * hidden, axis=-1, keepdims=True) + NEAR_ZERO)
        grad = grad_hidden[rows, :]
        grad_gain[...] += jnp.sum(grad * hidden * scale, axis=0, keepdims=True)
        scaled = grad * gains[0:1, :]
        mean = jnp.mean(scaled * hidden, axis=-1, keepdims=True)
        grad_hidden[rows, :] = grad_mid[rows, :] + scale * scaled - hidden * (scale * scale * scale * mean)
        return 0

    lax.fori_loop(0, ALL // 32, hidden_back, 0)
    if routed:
        turned = grad_raw.at[pl.ds(0, HEAD_SIZE), pl.ds(0, MODEL_WIDTH)]
        turned[...] = jnp.zeros_like(turned)
        turned[0:1, :] = grad_gain[...]
        turned[1:2, :] = grad_mlp[...]
        move = tap_moves()
        for block in range(MODEL_WIDTH // HEAD_SIZE):
            wide = nt(low(grad_conv[:, pl.ds(block * 3 * HEAD_SIZE, 3 * HEAD_SIZE)]), move)
            lanes = pl.ds(block * HEAD_SIZE, HEAD_SIZE)
            for tap in range(KW):
                for third in range(3):
                    place = CONV_AT + 3 * tap + third
                    turned[place : place + 1, lanes] = wide[tap : tap + 1, third * HEAD_SIZE : (third + 1) * HEAD_SIZE]

        def weigh(tile, _):
            columns = pl.ds(pl.multiple_of(tile * 256, 256), 256)
            mix[:, columns] = low(nn(normed_t[...], grad_project[:, columns]))
            return 0

        lax.fori_loop(0, MIX // 256, weigh, 0)
        mix[:, pl.ds(AT_SMALL, SMALL)] = low(nn(normed_t[...], grad_logits[...]) + turned[...].T)
        more = scatter_steps(
            at, (0, AT_OUT), CHUNK_MIX, mix, ((mix_sum, 0, MIX), (small_sum, 0, SMALL)), *refs[22:]
        )
        until(more, "started")
        for number, (row, spot) in enumerate(((at.near, at.spot), (at.far, at.spot))):
            both_advance(AT_END, sums, after, more)
            pending()
            value = parts[2 * number] + parts[2 * number + 1]
            pending = exchange(number + 1, value, row, spot)
        both_advance(AT_END, sums, after, more)
        pending()
        by_level[at.level] = parts[4] + parts[5]
        here = {"dp": at.near, "seq": at.spot}

        def pass_on(condition, up, source):
            device = {"dp": at.row, "seq": at.spot + 2 if up else at.spot - 2}
            sender.start(condition, by_level.at[source], by_level.at[source], device, level_sem.at[source])

        pass_on(at.above, True, at.level)
        pass_on(at.below, False, at.level)
        for step in range(1, at.levels):
            both_advance(AT_END, sums, after, more)
            for condition, source, up, onward in (
                (at.level - step >= 0, at.level - step, True, at.above),
                (at.level + step < at.levels, at.level + step, False, at.below),
            ):
                sender.arrived(condition, by_level.at[source], here, level_sem.at[source])
                if step < at.levels - 1:
                    pass_on(condition & onward, up, source)
        value = by_level[0]
        for level in range(1, at.levels):
            value = value + by_level[level]
        head_sum[...] = jnp.broadcast_to(jnp.sum(value, axis=0, keepdims=True), value.shape)
        for _ in range(12):
            both_advance(AT_END, sums, after, more)
        until(sums, "end")
        until(after, "end")
        until(more, "end")
        sender.drain()

    @pl.when(index > 0)
    def _():
        back.wait_send()

        def drain(head, _):
            copy(head).wait_send()
            return 0

        lax.fori_loop(0, HEADS, drain, 0)


def mixer_backward(operands, normed, grad_mlp, grads, routed):
    vmem, anywhere = pl.BlockSpec(memory_space=pltpu.VMEM), pl.BlockSpec(memory_space=pl.ANY)
    dma = pltpu.SemaphoreType.DMA
    shape = jax.ShapeDtypeStruct
    states = (HEADS, ROWS, HEAD_SIZE, HEAD_SIZE)
    levels = lax.axis_size("seq") // 2
    local = [
        ((ALL, MIX), BF16),
        ((ALL, SMALL), BF16),
        ((KW, QKV), F32),
        ((8, HEAD_SIZE), F32),
        ((1, MODEL_WIDTH), F32),
    ]
    scratch = [
        pltpu.VMEM((ALL, HEAD_SIZE), F32),
        pltpu.VMEM((ALL, HEAD_SIZE), F32),
        pltpu.VMEM((KW - 1, ALL, HEAD_SIZE), F32),
        pltpu.VMEM((ALL, ALL), F32),
        pltpu.VMEM((ALL, ALL), F32),
        pltpu.VMEM((ALL, MODEL_WIDTH), BF16),
        pltpu.VMEM((ALL, QKV), F32),
        pltpu.VMEM((ALL, SMALL), F32),
        pltpu.VMEM(states, BF16),
        pltpu.VMEM(states, BF16),
        pltpu.VMEM((ROWS * HALO, QKV), BF16),
        pltpu.VMEM((ROWS * HALO, QKV), BF16),
        dma((HEADS,)),
        dma((HEADS,)),
        dma,
        dma,
        pltpu.VMEM((MODEL_WIDTH, AT_OUT), BF16),
        dma,
    ]
    more = []
    out_shape = [shape((ALL, MODEL_WIDTH), F32)]
    if routed:
        more = [normed, grad_mlp, grads]
        out_shape += [shape((2 * PIECE, width), F32) for width in (MODEL_WIDTH, 2 * FF, FF, MIX, SMALL)]
        out_shape += [shape((8, HEAD_SIZE), F32)]
        scratch = [pltpu.VMEM(*entry) for entry in local] + scratch
        scratch += [
            pltpu.VMEM((6, 8, HEAD_SIZE), F32),
            pltpu.VMEM((levels, 8, HEAD_SIZE), F32),
            dma((3,)),
            dma((levels,)),
            dma((3 + 2 * levels,)),
        ]
        scratch += scatter_buffers(levels, FIRST_REST, True) + scatter_buffers(levels, LAST_REST, True)
        scratch += scatter_buffers(levels, AT_OUT, False)
    else:
        out_shape += [shape(*entry) for entry in local]
    in_specs = [pl.BlockSpec(memory_space=pltpu.SMEM)] + [vmem] * 4 + [anywhere] + [vmem] * 11
    in_specs += [vmem, vmem, anywhere] if routed else []
    return pl.pallas_call(
        functools.partial(mixer_backward_kernel, routed),
        out_shape=out_shape,
        in_specs=in_specs,
        out_specs=[vmem] * len(out_shape),
        scratch_shapes=scratch,
        compiler_params=pltpu.CompilerParams(
            collective_id=2, has_side_effects=True, vmem_limit_bytes=63 * 2**20
        ),
        name="mixer_backward",
    )(*operands, *more)


TILE = 256
HANDS = 32
OWN = FF // HANDS
GROUP_ROWS = 4 * OWN


def pack_hand(source, begin, store):
    for half in range(2):
        for lane in range(2):
            for step in range(11):
                rows = slice(begin + step * 8, begin + step * 8 + 8)
                first = (4 * half + lane) * 128
                second = (4 * half + 2 + lane) * 128
                pair = jnp.concatenate([source[rows, first : first + 128], source[rows, second : second + 128]], axis=0)
                store(half * PIECE, (lane * 11 + step) * 128, pair)


def mlp_kernel(
    full, tokens, cotangent, gated, gains,
    output, grad_mid, grad_gated, grad_gain, grads,
    out_w, up_w, packed, wide, down_w, hidden, normed, total, grad_normed,
    normed_t, gated_t, acted_t, up_stage, stage, load_sem, up_sem, store_sem, stage_sem,
):
    def load(number):
        columns, target = (
            (pl.ds(AT_OUT, MODEL_WIDTH), out_w),
            (pl.ds(AT_DOWN, FF), packed),
        )[number]
        return pltpu.make_async_copy(full.at[:, columns], target, load_sem.at[number])

    def load_up(tile, side):
        begin = pl.multiple_of(side * FF + tile * TILE, TILE)
        source = full.at[:, pl.ds(pl.multiple_of(AT_UP + begin, 128), TILE)]
        return pltpu.make_async_copy(source, up_w.at[:, pl.ds(begin, TILE)], up_sem.at[side, tile])

    load(1).start()
    load(0).start()

    def start_up(tile, _):
        load_up(tile, 0).start()
        load_up(tile, 1).start()
        return 0

    lax.fori_loop(0, FF // TILE, start_up, 0)
    load(1).wait()

    def unpack(hand, _):
        for half in range(2):
            rows = pl.ds(pl.multiple_of((hand * 2 + half) * PIECE, PIECE), PIECE)
            piece = packed[rows, :].astype(F32)
            for lane in range(2):
                for step in range(11):
                    source = (lane * 11 + step) * 128
                    target = pl.ds(pl.multiple_of(hand * OWN + step * 8, 8), 8)
                    for top in range(2):
                        column = (4 * half + 2 * top + lane) * 128
                        wide[target, column : column + 128] = piece[top * 8 : top * 8 + 8, source : source + 128]
        return 0

    lax.fori_loop(0, HANDS, unpack, 0)

    def narrow(tile, _):
        rows = pl.ds(pl.multiple_of(tile * TILE, TILE), TILE)
        down_w[rows, :] = low(wide[rows, :])
        return 0

    lax.fori_loop(0, FF // TILE, narrow, 0)
    load(0).wait()
    gated_t[...] = low(gated[...].astype(F32).T)
    middle = tokens[...].astype(F32) + nn(gated[...], out_w[...])
    hidden[...] = middle
    inverse = lax.rsqrt(jnp.mean(middle * middle, axis=-1, keepdims=True) + NEAR_ZERO)
    value = middle * inverse * gains[1:2, :]
    normed[...] = low(value)
    normed_t[...] = low(value.T)
    total[...] = jnp.zeros_like(total)
    grad_normed[...] = jnp.zeros_like(grad_normed)

    def store_up(tile, slot, side):
        begin = pl.multiple_of(MODEL_WIDTH + side * FF + tile * TILE, TILE)
        return pltpu.make_async_copy(up_stage.at[slot, side], grads.at[:, pl.ds(begin, TILE)], store_sem.at[slot, side])

    def tile_step(tile, _):
        slot = lax.rem(tile, 2)
        here = pl.ds(pl.multiple_of(tile * TILE, TILE), TILE)
        there = pl.ds(pl.multiple_of(FF + tile * TILE, TILE), TILE)
        load_up(tile, 0).wait()
        load_up(tile, 1).wait()

        @pl.when(tile >= 2)
        def _():
            store_up(tile - 2, slot, 0).wait()
            store_up(tile - 2, slot, 1).wait()

        gate = nn(normed[...], up_w[:, here])
        up = nn(normed[...], up_w[:, there])
        grad = nt(cotangent[...], down_w[here, :])
        sigma = jax.nn.sigmoid(gate)
        soft = gate * sigma
        acted = soft * up
        acted_low = low(acted)
        acted_t[here, :] = low(acted.T)
        total[...] += nn(acted_low, down_w[here, :])
        grad_gate = low(grad * up * (sigma * (1.0 + gate * (1.0 - sigma))))
        grad_up = low(grad * soft)
        grad_normed[...] += nt(grad_gate, up_w[:, here]) + nt(grad_up, up_w[:, there])
        up_stage[slot, 0] = low(nn(normed_t[...], grad_gate))
        up_stage[slot, 1] = low(nn(normed_t[...], grad_up))
        store_up(tile, slot, 0).start()
        store_up(tile, slot, 1).start()
        return 0

    tiles = FF // TILE
    lax.fori_loop(0, tiles, tile_step, 0)
    middle = hidden[...]
    output[...] = low(middle + total[...])
    inverse = lax.rsqrt(jnp.mean(middle * middle, axis=-1, keepdims=True) + NEAR_ZERO)
    grad = grad_normed[...]
    grad_gain[...] = jnp.sum(grad * middle * inverse, axis=0, keepdims=True)
    scaled = grad * gains[1:2, :]
    mean = jnp.mean(scaled * middle, axis=-1, keepdims=True)
    grad = cotangent[...].astype(F32) + inverse * scaled - middle * (inverse * inverse * inverse * mean)
    grad_mid[...] = grad
    grad_low = low(grad)
    grad_gated[...] = nt(grad_low, out_w[...])
    for last in range(2):
        tile = tiles - 2 + last
        for side in range(2):
            store_up(tile, tile % 2, side).wait()

    def store_out(tile):
        slot, side = divmod(tile, 2)
        columns = pl.ds(tile * TILE, TILE)
        return pltpu.make_async_copy(up_stage.at[slot, side], grads.at[:, columns], store_sem.at[slot, side])

    for tile in range(MODEL_WIDTH // TILE):
        slot, side = divmod(tile, 2)
        up_stage[slot, side] = low(nn(gated_t[...], grad_low[:, tile * TILE : (tile + 1) * TILE]))
        store_out(tile).start()

    def store_down(group, slot):
        rows = pl.ds(pl.multiple_of(group * 128, 128), 128)
        target = grads.at[rows, pl.ds(MODEL_WIDTH + 2 * FF, FF)]
        return pltpu.make_async_copy(stage.at[slot], target, stage_sem.at[slot])

    def down_step(group, _):
        slot = lax.rem(group, 2)

        @pl.when(group >= 2)
        def _():
            store_down(group - 2, slot).wait()

        rows = pl.ds(pl.multiple_of(group * GROUP_ROWS, GROUP_ROWS), GROUP_ROWS)
        wide[pl.ds(0, GROUP_ROWS), :] = nn(acted_t[rows, :], cotangent[...])
        for hand in range(4):

            def store(row, column, value, hand=hand):
                stage[slot, hand * 2 * PIECE + row : hand * 2 * PIECE + row + PIECE, column : column + 128] = low(value)

            pack_hand(wide, hand * OWN, store)
        store_down(group, slot).start()
        return 0

    groups = HANDS // 4
    lax.fori_loop(0, groups, down_step, 0)
    for group in (groups - 2, groups - 1):
        store_down(group, group % 2).wait()
    for tile in range(MODEL_WIDTH // TILE):
        store_out(tile).wait()


def mlp(full, tokens, cotangent, gated, gains):
    vmem, anywhere = pl.BlockSpec(memory_space=pltpu.VMEM), pl.BlockSpec(memory_space=pl.ANY)
    dma = pltpu.SemaphoreType.DMA
    shape = jax.ShapeDtypeStruct
    return pl.pallas_call(
        mlp_kernel,
        out_shape=[
            shape((ALL, MODEL_WIDTH), BF16),
            shape((ALL, MODEL_WIDTH), F32),
            shape((ALL, MODEL_WIDTH), F32),
            shape((1, MODEL_WIDTH), F32),
            shape((MODEL_WIDTH, PACK - AT_OUT), BF16),
        ],
        in_specs=[anywhere] + [vmem] * 4,
        out_specs=[vmem] * 4 + [anywhere],
        scratch_shapes=[
            pltpu.VMEM((MODEL_WIDTH, MODEL_WIDTH), BF16),
            pltpu.VMEM((MODEL_WIDTH, 2 * FF), BF16),
            pltpu.VMEM((MODEL_WIDTH, FF), BF16),
            pltpu.VMEM((FF, MODEL_WIDTH), F32),
            pltpu.VMEM((FF, MODEL_WIDTH), BF16),
            pltpu.VMEM((ALL, MODEL_WIDTH), F32),
            pltpu.VMEM((ALL, MODEL_WIDTH), BF16),
            pltpu.VMEM((ALL, MODEL_WIDTH), F32),
            pltpu.VMEM((ALL, MODEL_WIDTH), F32),
            pltpu.VMEM((MODEL_WIDTH, ALL), BF16),
            pltpu.VMEM((MODEL_WIDTH, ALL), BF16),
            pltpu.VMEM((FF, ALL), BF16),
            pltpu.VMEM((2, 2, MODEL_WIDTH, TILE), BF16),
            pltpu.VMEM((2, 128, FF), BF16),
            dma((2,)),
            dma((2, FF // TILE)),
            dma((2, 2)),
            dma((2,)),
        ],
        compiler_params=pltpu.CompilerParams(vmem_limit_bytes=60 * 2**20),
        name="mlp",
    )(full, tokens, cotangent, gated, gains)


def result_kernel(
    hidden, mix, out, up, down, small, head,
    hidden_to, mixer_to, mix_to, conv_to, beta_to, head_to, out_to, mlp_to, up_to, down_to,
):
    for source, target in ((mix, mix_to), (out, out_to), (up, up_to)):
        target[...] = source[...]

    def move(step, _):
        rows = pl.ds(pl.multiple_of(step * 32, 32), 32)
        hidden_to[rows, :] = hidden[rows, :]
        return 0

    lax.fori_loop(0, ALL // 32, move, 0)
    for group in range(4):
        for lane in range(2):
            for step in range(11):
                source = (lane * 11 + step) * 128
                target = (2 * group + lane) * 128
                down_to[step * 8 : step * 8 + 8, target : target + 128] = down[
                    group * 8 : group * 8 + 8, source : source + 128
                ]
    values = small[...]
    beta_to[...] = values[:, BETA_AT:CONV_AT]
    turned = jnp.concatenate([values, jnp.zeros((SMALL - 2 * PIECE, SMALL), F32)], axis=0).T
    mixer_to[...] = turned[0:1, : 2 * PIECE]
    mlp_to[...] = turned[1:2, : 2 * PIECE]
    for tap in range(KW):
        for third in range(3):
            place = CONV_AT + 3 * tap + third
            conv_to[tap : tap + 1, third * 2 * PIECE : (third + 1) * 2 * PIECE] = turned[place : place + 1, : 2 * PIECE]
    head_to[...] = head[0:1, :]


def result(hidden, mix, out, up, down, small, head):
    vmem = pl.BlockSpec(memory_space=pltpu.VMEM)
    shape = jax.ShapeDtypeStruct
    share = 2 * PIECE
    return pl.pallas_call(
        result_kernel,
        out_shape=[
            shape(hidden.shape, F32),
            shape((1, share), F32),
            shape(mix.shape, F32),
            shape((KW, 3 * share), F32),
            shape((share, HEADS), F32),
            shape((1, HEAD_SIZE), F32),
            shape(out.shape, F32),
            shape((1, share), F32),
            shape(up.shape, F32),
            shape((OWN, MODEL_WIDTH), F32),
        ],
        in_specs=[vmem] * 7,
        out_specs=[vmem] * 10,
        name="result",
    )(hidden, mix, out, up, down, small, head)


def pack_down(part):
    lead = part.shape[:-2]
    tiles = part.reshape(lead + (11, 8, 4, 2, 128))
    n = len(lead)
    moved = tiles.transpose(tuple(range(n)) + (n + 2, n + 1, n + 3, n, n + 4))
    return moved.reshape(lead + (2 * PIECE, FF))


def unpack_down(part):
    lead = part.shape[:-2]
    tiles = part.reshape(lead + (4, 8, 2, 11, 128))
    n = len(lead)
    moved = tiles.transpose(tuple(range(n)) + (n + 3, n + 1, n, n + 2, n + 4))
    return moved.reshape(lead + (OWN, MODEL_WIDTH))


def pack_taps(conv):
    taps = conv.reshape(KW, -1, 3, 2 * PIECE)
    return taps.transpose(1, 3, 0, 2).reshape(-1, 3 * KW)


def pack_small(mixer, mlp_part, beta, conv):
    parts = jnp.concatenate([mixer[:, None], mlp_part[:, None], beta, pack_taps(conv)], axis=1)
    return jnp.pad(parts, ((0, 0), (0, SMALL - parts.shape[1])))


def shards(
    tokens, cotangent, starts, mixer_gain, mix_weight, conv_weight, beta_weight, head_gain, out_weight, mlp_gain,
    upgate_weight, down_weight,
):
    rows, block, width = tokens.shape
    share = mix_weight.shape[1]
    both = ("dp", "seq")
    routed = lax.axis_size("dp") == 4 and lax.axis_size("seq") % 2 == 0 and share == 2 * PIECE
    if routed:
        weights = [
            mix_weight[0], out_weight[0], upgate_weight[0], down_weight[0], mixer_gain, mlp_gain, beta_weight[0],
            conv_weight[0],
        ]
    else:
        parts = [
            mixer_gain[0], mlp_gain[0], beta_weight[0], conv_weight[0].T, mix_weight[0], out_weight[0], upgate_weight[0],
            down_weight[0],
        ]
        parts = [lax.all_gather(part, both, axis=0, tiled=True) for part in parts]
        mixer_w, mlp_w, beta_w, conv_w, mix_w, out_w, up_w, down_w = parts
        small_w = pack_small(mixer_w, mlp_w, beta_w, conv_w.T)
        down_w = pack_down(down_w.reshape(-1, OWN, width)).reshape(-1, FF)
        weights = [jnp.concatenate([mix_w, small_w, out_w, up_w, down_w], axis=1)]

    flat = tokens.reshape(rows * block, width)
    flat_grad = cotangent.reshape(rows * block, width)
    full, normed, pre, raw, beta, solved, solved_w, fresh, state, power, outputs, gated, conv, gains = mixer_forward(
        starts, flat, head_gain, weights
    )
    output, grad_mid, grad_gated, grad_mlp, grads = mlp(full, flat, flat_grad, gated, gains)
    operands = [
        starts, grad_gated, grad_mid, flat, gains, full, conv, head_gain,
        pre, raw, beta, solved, solved_w, fresh, state, power, outputs,
    ]
    results = mixer_backward(operands, normed, grad_mlp, grads, routed)
    if routed:
        grad_hidden, out_sum, up_sum, down_sum, mix_sum, small_sum, head_sum = results
        parts = result(grad_hidden, mix_sum, out_sum, up_sum, down_sum, small_sum, head_sum)
        grad_hidden, mixer_mine, mix_mine, conv_mine, beta_mine, head_mine, out_mine, mlp_mine, up_mine, down_mine = parts
        mixer_mine, mlp_mine = mixer_mine[0], mlp_mine[0]
    else:
        grad_hidden, grad_project, grad_logits, grad_conv, grad_head, grad_mixer = results
        whole_mix = lax.dot_general(normed, grad_project, (((1,), (0,)), ((), ())), preferred_element_type=F32)
        whole_beta = lax.dot_general(normed, grad_logits, (((1,), (0,)), ((), ())), preferred_element_type=F32)
        whole_down = unpack_down(grads[:, MODEL_WIDTH + 2 * FF :].reshape(-1, 2 * PIECE, FF)).reshape(FF, width)
        listed = [
            whole_mix,
            grads[:, :MODEL_WIDTH],
            grads[:, MODEL_WIDTH : MODEL_WIDTH + 2 * FF],
            whole_down,
            grad_mixer[0],
            grad_mlp[0],
            whole_beta[:, BETA_AT:CONV_AT],
            grad_conv.T,
        ]
        listed = [
            lax.psum_scatter(part.astype(F32), both, scatter_dimension=0, tiled=True) for part in listed
        ]
        mix_mine, out_mine, up_mine, down_mine, mixer_mine, mlp_mine, beta_mine, conv_mine = listed
        conv_mine = conv_mine.T
        head_mine = lax.psum(jnp.sum(grad_head, axis=0, keepdims=True), both)
    return (
        output.reshape(rows, block, width),
        grad_hidden.reshape(rows, block, width),
        mixer_mine[None],
        mix_mine[None],
        conv_mine[None],
        beta_mine[None],
        head_mine,
        out_mine[None],
        mlp_mine[None],
        up_mine[None],
        down_mine[None],
    )


def solution(mesh):
    both = ("dp", "seq")
    in_specs = (
        P("dp", "seq", None),
        P("dp", "seq", None),
        P("dp", None),
        P(None, both),
        P(None, both, None),
        P(None, None, both),
        P(None, both, None),
        P(),
        P(None, both, None),
        P(None, both),
        P(None, both, None),
        P(None, both, None),
    )
    out_specs = (
        P("dp", "seq", None),
        P("dp", "seq", None),
        P(None, both),
        P(None, both, None),
        P(None, None, both),
        P(None, both, None),
        P(),
        P(None, both, None),
        P(None, both),
        P(None, both, None),
        P(None, both, None),
    )
    return jax.shard_map(shards, mesh=mesh, in_specs=in_specs, out_specs=out_specs, check_vma=False)
```
